32 devices in a mesh: batch: 16 (over z, y, x), head: 2 (over core).
Axes of the slice: x: 2, y: 2, z: 4, core: 2. Of those that a mesh axis runs over, the one named last changes fastest.
Arguments:
- tokens: bfloat16 [16, 1024, 768], P('batch'), may hold values from -6 to 6
- attn_gain: bfloat16 [768], P('batch'), may hold values from 0.099609375 to 1.8984375
- qkv_weight: bfloat16 [768, 3, 768], P('batch', None, 'head'), may hold values from -0.21875 to 0.21875
- out_weight: bfloat16 [768, 768], P('head', 'batch'), may hold values from -1.75 to 1.75
- ffn_gain: bfloat16 [768], P('batch'), may hold values from 0.099609375 to 1.8984375
- up_weight: bfloat16 [768, 3072], P('batch', 'head'), may hold values from -0.21875 to 0.21875
- down_weight: bfloat16 [3072, 768], P('head', 'batch'), may hold values from -0.109375 to 0.109375
- cotangent: bfloat16 [16, 1024, 768], P('batch'), may hold values from -6 to 6
- segment: int32 [16, 1024], P('batch'), may hold values from 0 to 9, as said below
- cluster: int32 [16, 12, 1024], P('batch', 'head'), may hold values from 0 to 99, as said below
- top_keys: int32 [16, 12, 100, 32], P('batch', 'head'), may hold values from 0 to 1023, as said below
Outputs:
- output: bfloat16 [16, 1024, 768], P('batch', 'head')
- tokens_grad: float32 [16, 1024, 768], P('batch', 'head')
- attn_gain_grad: float32 [768], P('batch')
- qkv_grad: float32 [768, 3, 768], P('batch', None, 'head')
- out_grad: float32 [768, 768], P('head', 'batch')
- ffn_gain_grad: float32 [768], P('batch')
- up_grad: float32 [768, 3072], P('batch', 'head')
- down_grad: float32 [3072, 768], P('head', 'batch')
The draws below stay inside these ranges and needn't reach their ends.
Inputs may be any that keep to these rules, and one draw needn't show every extreme that they name: Each row holds 10 documents of consecutive positions; segment ids never fall along a row, document d has id d, and each has at least 51 positions. Cluster c of a head in a row holds only positions of document c mod 10 of that row; a cluster may have no positions. `top_keys`: for each row, head and cluster c: 32 distinct positions of document c mod 10 of that row, in increasing order.
All inputs are finite; a program needn't handle non-finite values.
Results may differ from the reference program's by a relative error of at most 0.017.
Values may be sent and summed in bfloat16 or wider, within the bound.
A program may use at most 192 MiB of HBM per device.

```python
import jax
import jax.numpy as jnp
from jax import lax

D = 768
HEADS = 12
HD = 64
FF = 3072
CLUST = 100
TOPK = 32
DOCS = 10
LEN = 1024
SEQS = 16


def document_bounds(key):
    inner_key = jax.random.fold_in(key, 97)
    wiggle = LEN // (4 * DOCS)
    jitter = jax.random.randint(inner_key, (SEQS, DOCS - 1), -wiggle, wiggle + 1)
    even_bounds = jnp.arange(1, DOCS, dtype=jnp.int32) * LEN // DOCS
    inner_bounds = even_bounds[None, :] + jitter
    starts = jnp.concatenate([jnp.zeros((SEQS, 1), jnp.int32), inner_bounds], axis=1)
    finish = jnp.concatenate([inner_bounds, jnp.full((SEQS, 1), LEN, jnp.int32)], axis=1)
    return (starts, finish)


def segment_of(starts):
    places = jnp.arange(LEN, dtype=jnp.int32)
    return jnp.sum((places[None, None, :] >= starts[:, 1:, None]).astype(jnp.int32), axis=1)


def draw_segment(key, part):
    starts, finish = document_bounds(key)
    return segment_of(starts)


def draw_cluster(key, part):
    starts, finish = document_bounds(key)
    key = jax.random.fold_in(key, 2)
    documents = segment_of(starts)
    draws_pick = jax.random.randint(key, (SEQS, HEADS, LEN), 0, CLUST // DOCS)
    return documents[:, None, :] + DOCS * draws_pick


def draw_top_keys(key, part):
    starts, finish = document_bounds(key)
    key = jax.random.fold_in(key, 3)
    owner_doc = jnp.arange(CLUST, dtype=jnp.int32) % DOCS
    first_pos = starts[:, owner_doc][:, None, :, None]
    spacing = ((finish - starts)[:, owner_doc] // TOPK)[:, None, :, None]
    offsets = jax.random.randint(key, (SEQS, HEADS, CLUST, TOPK), 0, 1 << 20)
    slot_index = jnp.arange(TOPK, dtype=jnp.int32)
    return first_pos + slot_index * spacing + offsets % spacing


def strengthened(drawn, stream_key, source, target, shards_of, factor):
    owner, partner = [(jnp.arange(drawn.shape[axis_at]) // (drawn.shape[axis_at] // shards_of)).reshape([-1 if axis == axis_at else 1 for axis in range(drawn.ndim)]) for axis_at in (source, target)]
    chosen = jax.random.permutation(stream_key, shards_of)[partner]
    strong = (owner == chosen) | (owner == (partner + shards_of // 2) % shards_of)
    return jnp.where(strong, factor * drawn, drawn)


def level_of(rng, extent, cuts, low, top_value):
    gain, own = 1.0, jax.random.fold_in(rng, 6)
    for axis_at, blocks in cuts:
        heights = jnp.exp(jax.random.uniform(jax.random.fold_in(own, axis_at), (blocks,), jnp.float32, low / len(cuts), top_value / len(cuts)))
        gain = gain * jnp.repeat(heights, extent[axis_at] // blocks).reshape([-1 if axis == axis_at else 1 for axis in range(len(extent))])
    return gain


def normal_values(rng, extent, spread, limit, shards=(), held_as=jnp.bfloat16):
    drawn = jax.random.normal(rng, extent, jnp.float32) * spread
    if len(shards) > 0:
        drawn = level_of(rng, extent, shards, -0.22, 0.18) * drawn
    return jnp.clip(drawn, min=-limit, max=limit).astype(held_as)


def noise_with(rng, dims, width, most, shards, heavy, held_as=jnp.bfloat16):
    entries = width * jax.random.normal(rng, dims, jnp.float32)
    if shards:
        entries = entries * level_of(rng, dims, shards, -0.22, 0.18)
    return jnp.clip(strengthened(entries, jax.random.fold_in(rng, 3), *heavy), -most, most).astype(held_as)


def setup_inputs(seed: int = 0) -> dict:
    arg_keys = jax.random.split(jax.random.key(seed), 12)
    return {
        "tokens": noise_with(arg_keys[0], (SEQS, LEN, D), 1.0, 6.0, ((0, 16),), (0, 2, 16, 2.0)),
        "attn_gain": jnp.clip(1.0 + 0.18 * jax.random.normal(arg_keys[1], (D,), jnp.float32), 0.099609375, 1.8984375).astype(jnp.bfloat16),
        "qkv_weight": normal_values(arg_keys[2], (D, 3, D), D ** -0.5, 0.21875, ((0, 16), (2, 2))),
        "out_weight": normal_values(arg_keys[3], (D, D), (D // 64) ** -0.5, 1.75, ((0, 2), (1, 16))),
        "ffn_gain": jnp.clip(1.0 + 0.18 * jax.random.normal(arg_keys[4], (D,), jnp.float32), 0.099609375, 1.8984375).astype(jnp.bfloat16),
        "up_weight": normal_values(arg_keys[5], (D, FF), D ** -0.5, 0.21875, ((0, 16), (1, 2))),
        "down_weight": normal_values(arg_keys[6], (FF, D), FF ** -0.5, 0.109375, ((0, 2), (1, 16))),
        "cotangent": noise_with(arg_keys[7], (SEQS, LEN, D), 1.0, 6.0, ((0, 16),), (0, 2, 16, 2.0)),
        "segment": draw_segment(jax.random.fold_in(arg_keys[11], 71), 0),
        "cluster": draw_cluster(jax.random.fold_in(arg_keys[11], 71), 0),
        "top_keys": draw_top_keys(jax.random.fold_in(arg_keys[11], 71), 0),
    }


EPS = 1e-05
HIGH = lax.Precision.HIGHEST
NEGATIVE = -1e+30

@jax.custom_vjp
def low(v):
    return lax.optimization_barrier(v.astype(jnp.bfloat16)).astype(jnp.float32)

@jax.custom_vjp
def low_back(v):
    return v

def low_keep(v):
    return (low(v), None)

def low_pass(kept, grad):
    return (grad,)

def back_keep(v):
    return (v, None)

def back_low(kept, grad):
    return (low(grad),)
low.defvjp(low_keep, low_pass)
low_back.defvjp(back_keep, back_low)

def layer_norm(values, gain_row):
    row_mean = lax.optimization_barrier(jnp.mean(values, axis=-1, keepdims=True))
    centred = values - row_mean
    variance = lax.optimization_barrier(jnp.mean(centred * centred, axis=-1, keepdims=True))
    return centred * lax.rsqrt(variance + EPS) * gain_row

def one_head(queries, key_rows, value_rows, segments, owners, top_table):
    scaling = HD ** (-0.5)
    labels = jnp.arange(CLUST, dtype=jnp.int32)
    members = (owners[:, None] == labels[None, :]).astype(jnp.float32)
    counts = jnp.maximum(lax.optimization_barrier(jnp.sum(members, axis=0)), 1.0)
    centre = low(jnp.dot(members.T, queries, precision=HIGH) / counts[:, None])
    scores = low_back(scaling * jnp.dot(centre, key_rows.T, precision=HIGH))
    allowed = segments[None, :] == (labels % DOCS)[:, None]
    scores = jnp.where(allowed, scores, NEGATIVE)
    scores = scores - lax.optimization_barrier(jnp.max(scores, axis=1, keepdims=True))
    exp_scores = jnp.exp(scores)
    probability = exp_scores / lax.optimization_barrier(jnp.sum(exp_scores, axis=1, keepdims=True))
    top_mask = jnp.zeros((CLUST, LEN), jnp.float32).at[labels[:, None], top_table].set(1.0)
    top_mass = lax.optimization_barrier(jnp.sum(probability * top_mask, axis=1))
    rest_sum = low_back(jnp.dot(low(probability) * (1.0 - top_mask), value_rows, precision=HIGH))
    chosen = top_table[owners]
    keys_top = key_rows[chosen]
    values_top = value_rows[chosen]
    near_score = low_back(scaling * jnp.einsum('ld,ltd->lt', queries, keys_top, precision=HIGH))
    near_score = near_score - lax.optimization_barrier(jnp.max(near_score, axis=1, keepdims=True))
    exp_near = jnp.exp(near_score)
    weights = exp_near / lax.optimization_barrier(jnp.sum(exp_near, axis=1, keepdims=True))
    exact_sum = jnp.einsum('lt,ltd->ld', low(weights), values_top, precision=HIGH)
    return top_mass[owners][:, None] * exact_sum + rest_sum[owners]

def row_layer(token_rows, attn_gain, qkv_weight, out_weight, ffn_gain, up_weight, down_weight, segments, owners, top_table):
    normed_one = low(layer_norm(token_rows, attn_gain))
    qkv_all = low(low_back(jnp.einsum('td,dsf->stf', normed_one, qkv_weight, precision=HIGH)))
    per_head = qkv_all.reshape(3, LEN, HEADS, HD).transpose(0, 2, 1, 3)
    attended = jax.vmap(one_head, in_axes=(0, 0, 0, None, 0, 0))(per_head[0], per_head[1], per_head[2], segments, owners, top_table)
    attended = low(low_back(attended.transpose(1, 0, 2).reshape(LEN, D)))
    attn_sum = low_back(jnp.dot(attended, out_weight, precision=HIGH))
    hidden = token_rows + attn_sum
    normed_two = low(layer_norm(hidden, ffn_gain))
    up_proj = low_back(jnp.dot(normed_two, up_weight, precision=HIGH))
    activ = low(jax.nn.gelu(up_proj))
    return hidden + jnp.dot(activ, down_weight, precision=HIGH)

def reference(tokens, attn_gain, qkv_weight, out_weight, ffn_gain, up_weight, down_weight, cotangent, segment, cluster, top_keys):
    weights_f32 = tuple((matrix.astype(jnp.float32) for matrix in (attn_gain, qkv_weight, out_weight, ffn_gain, up_weight, down_weight)))

    def forward(inputs, *weights_in):

        def scan_step(carried, pieces):
            result = jax.checkpoint(row_layer)(pieces[0], *weights_in, pieces[1], pieces[2], pieces[3])
            return (carried, result)
        unused, outputs = lax.scan(scan_step, None, (inputs, segment, cluster, top_keys))
        return outputs
    inputs = tokens.astype(jnp.float32)
    outputs, pullback = jax.vjp(forward, inputs, *weights_f32)
    gradients = pullback(cotangent.astype(jnp.float32))
    return (outputs.astype(jnp.bfloat16), gradients[0], gradients[1], gradients[2], gradients[3], gradients[4], gradients[5], gradients[6])
```

```python
import functools

import jax
import jax.numpy as jnp
from jax import lax
from jax.experimental import pallas as pl
from jax.experimental.pallas import tpu as pltpu
from jax.sharding import PartitionSpec as P

F32=jnp.float32; BF=jnp.bfloat16
BIG=1e30
NT=(((1,),(1,)),((),()))
TN=(((0,),(0,)),((),()))
NN=(((1,),(0,)),((),()))
def dot(a,b,dims=NN): return lax.dot_general(a,b,dims,preferred_element_type=F32)
def split3(x):
    a=x.astype(BF); r=x-a.astype(F32); b=r.astype(BF); c=(r-b.astype(F32)).astype(BF)
    return a,b,c
def split2(x):
    a=x.astype(BF); return a,(x-a.astype(F32)).astype(BF)
L=1024
def lane(shape): return lax.broadcasted_iota(jnp.int32,shape,len(shape)-1)
def sub(shape): return lax.broadcasted_iota(jnp.int32,shape,len(shape)-2)

def build_masks(own_row, topT):
    mt=jnp.where(own_row==sub((128,L)),1.0,0.0).astype(BF)
    m=jnp.transpose(mt)
    hi=lax.shift_right_arithmetic(topT,5); bit=lax.shift_left(jnp.int32(1),topT&31)
    words=L//32
    a_iota=sub((words,128))
    w=jnp.zeros((words,128),jnp.int32)
    for t in range(topT.shape[0]):
        w=w|jnp.where(hi[t:t+1]==a_iota,bit[t:t+1],0)
    b_iota=sub((32,128)); ln=lane((32,128))
    extra=(ln>=100)&(ln<103)
    ns=[];ts=[]
    for a in range(words):
        b=(lax.shift_right_logical(jnp.broadcast_to(w[a:a+1],(32,128)),b_iota)&1)
        tmf=b.astype(F32)
        ts.append(tmf)
        ns.append(jnp.where(extra,-1.0,jnp.where(b==1,0.0,-BIG)))
    n=jnp.concatenate(ns,0).astype(BF)
    tm=jnp.transpose(jnp.concatenate(ts,0)).astype(BF)
    return m,mt,n,tm

def mask_kernel(cl,tt,m,mt,n,tm):
    a,b,c,d=build_masks(cl[0],tt[0])
    m[0]=a;mt[0]=b;n[0]=c;tm[0]=d
def masks(cluster,topk):
    H=cluster.shape[0]
    tt=jnp.pad(topk.transpose(0,2,1),((0,0),(0,0),(0,128-topk.shape[1])),constant_values=-1)
    return pl.pallas_call(mask_kernel,grid=(H,),
      in_specs=[pl.BlockSpec((1,1,L),lambda h:(h,0,0)),pl.BlockSpec((1,tt.shape[1],128),lambda h:(h,0,0))],
      out_specs=[pl.BlockSpec((1,L,128),lambda h:(h,0,0)),pl.BlockSpec((1,128,L),lambda h:(h,0,0)),pl.BlockSpec((1,L,128),lambda h:(h,0,0)),pl.BlockSpec((1,128,L),lambda h:(h,0,0))],
      out_shape=[jax.ShapeDtypeStruct((H,L,128),BF),jax.ShapeDtypeStruct((H,128,L),BF),jax.ShapeDtypeStruct((H,L,128),BF),jax.ShapeDtypeStruct((H,128,L),BF)],
      compiler_params=pltpu.CompilerParams(vmem_limit_bytes=50<<20))(cluster[:,None,:],tt)

TQ=256
def fwd_head(odd, q, k, v, m_ref, mt, n_ref, tm, seg_row, qaug, kaug):
    ln=lane((L,128)); mine=(ln>=64) if odd else (ln<64)
    lc=lane((128,128)); minec=(lc>=64) if odd else (lc<64)
    zero=jnp.zeros((),BF)
    qm=jnp.where(mine,q,zero)
    vaug=jnp.where(mine,v,jnp.ones((),BF))
    cnt=jnp.maximum(jnp.sum(mt.astype(F32),axis=1,keepdims=True),1.0)
    cen=(dot(mt,qm)/cnt).astype(BF)
    cs=(cen.astype(F32)*0.125).astype(BF)
    s=dot(cs,k,NT)
    cio=sub((128,L))
    cm=lax.rem(sub((128,1)),jnp.int32(10))
    s=jnp.where(seg_row==cm,s,-BIG)
    mx=jnp.max(s,axis=1,keepdims=True)
    e=jnp.exp(s-mx)
    tot=jnp.sum(e,axis=1,keepdims=True)
    prob=e/tot
    tmf=tm.astype(F32)
    mass=jnp.sum(prob*tmf,axis=1,keepdims=True)
    rw=(prob*(1.0-tmf)).astype(BF)
    rest=dot(rw,v)
    massb=jnp.broadcast_to(mass,(128,128))
    r=jnp.where(minec,rest,massb)
    rh,rl=split2(r)
    rr=jnp.concatenate([rh,rl],1)
    qaug[:,:128]=(qm.astype(F32)*0.125).astype(BF)
    qaug[:,128:]=m_ref
    kaug[:,:128]=k
    kaug[:,128:]=n_ref
    ex=[];att=[];mb=[]
    lt=lane((TQ,128)); minet=(lt>=64) if odd else (lt<64)
    for t in range(L//TQ):
        sl=pl.ds(t*TQ,TQ)
        sc=dot(qaug[sl,:],kaug[...],NT)
        mm=jnp.max(sc,axis=1,keepdims=True)
        p=jnp.exp(sc-mm).astype(BF)
        o=dot(p,vaug)
        mt_=qaug[sl,128:]
        ee=dot(mt_,rr); ee=ee[:,:128]+ee[:,128:]
        osw=pltpu.roll(o,64,1); esw=pltpu.roll(ee,64,1)
        exact=o/osw
        a=exact*esw+ee
        tot_=jnp.where(minet,osw,o); ms_=jnp.where(minet,esw,ee)
        lse=mm+jnp.log(tot_)-jnp.log(jnp.maximum(ms_,1e-37))
        h3,m3,l3=split3(lse)
        mbt=jnp.where(lt==100,h3.astype(F32),jnp.where(lt==101,m3.astype(F32),jnp.where(lt==102,l3.astype(F32),mt_.astype(F32)))).astype(BF)
        ex.append(exact);att.append(a);mb.append(mbt)
    return ex,att,mb,prob

def fwd_kernel(q,k,v,m,mt,n,tm,seg,att_o,ex_o,mb_o,prob_o,qaug,kaug):
    res=[]
    for h in range(2):
        ex,att,mb,prob=fwd_head(h==1,q[...],k[...],v[...],m[h],mt[h],n[h],tm[h],seg[...],qaug,kaug)
        lt=lane((TQ,128));
        for t in range(L//TQ):
            sl=pl.ds(t*TQ,TQ)
            mb_o[h,sl,:]=mb[t]
            if h==0:
                att_o[sl,:]=att[t].astype(BF); ex_o[sl,:]=ex[t]
            else:
                att_o[sl,:]=jnp.where(lt<64,att_o[sl,:],att[t].astype(BF))
                ex_o[sl,:]=jnp.where(lt<64,ex_o[sl,:],ex[t])
        prob_o[h]=prob
def attn_fwd(qkv,M,MT,N,TM,seg):
    H=M.shape[0]; P2=H//2
    ps=lambda off: pl.BlockSpec((L,128),lambda p,off=off:(0,off+p))
    hs=lambda a,b: pl.BlockSpec((2,a,b),lambda p:(p,0,0))
    return pl.pallas_call(fwd_kernel,grid=(P2,),
      in_specs=[ps(0),ps(P2),ps(2*P2),hs(L,128),hs(128,L),hs(L,128),hs(128,L),pl.BlockSpec((1,L),lambda p:(0,0))],
      out_specs=[ps(0),ps(0),hs(L,128),hs(128,L)],
      out_shape=[jax.ShapeDtypeStruct((L,P2*128),BF),jax.ShapeDtypeStruct((L,P2*128),F32),jax.ShapeDtypeStruct((H,L,128),BF),jax.ShapeDtypeStruct((H,128,L),F32)],
      scratch_shapes=[pltpu.VMEM((L,256),BF),pltpu.VMEM((L,256),BF)],
      compiler_params=pltpu.CompilerParams(vmem_limit_bytes=50<<20))(qkv,qkv,qkv,M,MT,N,TM,seg)

TJ=256
def bwd_kernel(q,k,v,g,ex,mb,mt_r,n,tm_r,prob_r,dq_o,dk_o,dv_o,qaug,kaug,gaug,vaug,dqt):
    ln=lane((L,128)); zero=jnp.zeros((),BF)
    lc=lane((128,128))
    qv=q[...];kv=k[...];vv=v[...];gv=g[...]
    kT=jnp.transpose(kv)
    prod=gv.astype(F32)*ex[...]
    for h in range(2):
        mine=(ln>=64) if h else (ln<64); minec=(lc>=64) if h else (lc<64)
        o=0 if h else 64
        r=jnp.sum(jnp.where(mine,prod,0.0),axis=1,keepdims=True)
        h3,m3,l3=split3(r)
        gm=jnp.where(mine,gv,zero)
        ga=jnp.where(ln==o,h3.astype(F32),jnp.where(ln==o+1,m3.astype(F32),jnp.where(ln==o+2,l3.astype(F32),gm.astype(F32)))).astype(BF)
        gaug[...]=ga
        vaug[...]=jnp.where(mine,vv,jnp.where((ln>=o)&(ln<o+3),jnp.full((),-1.0,BF),zero))
        qm=jnp.where(mine,qv,zero); qs=(qm.astype(F32)*0.125).astype(BF)
        qaug[:,:128]=qs; qaug[:,128:]=mb[h]
        kaug[:,:128]=kv; kaug[:,128:]=n[h]
        mt=mt_r[h]; tm=tm_r[h]; prob=prob_r[h]
        cnt=jnp.maximum(jnp.sum(mt.astype(F32),axis=1,keepdims=True),1.0)
        cen=(dot(mt,qm)/cnt).astype(BF)
        cs=(cen.astype(F32)*0.125).astype(BF)
        gr=dot(mt,ga)
        gmass=jnp.sum(jnp.where((lc>=o)&(lc<o+3),gr,0.0),axis=1,keepdims=True)
        grest=jnp.where(minec,gr,0.0).astype(BF)
        gp=dot(grest,vv,NT)
        tmb=tm.astype(F32)
        top=tmb>0.5
        gp=jnp.where(top,gmass,gp)
        t=jnp.sum(prob*gp,axis=1,keepdims=True)
        gs=(prob*(gp-t)).astype(BF)
        rw=jnp.where(top,0.0,prob).astype(BF)
        km=jnp.where(mine,kv,zero)
        gcen=dot(gs,km)/cnt
        gh,gl=split2(gcen)
        gg=jnp.concatenate([gh,gl],1)
        gsT=jnp.transpose(gs); rwT=jnp.transpose(rw)
        kTh=kT[64*h:64*h+64]
        gam=jnp.where(mine,gv,zero)
        for t_ in range(L//TJ):
            sl=pl.ds(t_*TJ,TJ)
            st=dot(kaug[sl,:],qaug[...],NT)
            p=jnp.exp(st)
            dp=dot(vaug[sl,:],gaug[...],NT)
            ds=(p*dp).astype(BF)
            pb=p.astype(BF)
            dv=dot(pb,gam)+dot(rwT[t_*TJ:(t_+1)*TJ],grest)
            dk=dot(ds,qs)+dot(gsT[t_*TJ:(t_+1)*TJ],cs)
            if h==0:
                dv_o[sl,:]=dv; dk_o[sl,:]=dk
            else:
                dv_o[sl,:]+=dv; dk_o[sl,:]+=dk
            dqp=dot(kTh[:,t_*TJ:(t_+1)*TJ],ds)
            if t_==0: dqt[64*h:64*h+64,:]=dqp
            else: dqt[64*h:64*h+64,:]+=dqp
        mbv=jnp.where(lane((L,128))<100,mb[h],zero)
        dd=dot(mbv,gg); dd=dd[:,:128]+dd[:,128:]
        if h==0: dq_o[...]=dd
        else: dq_o[...]+=dd
    dq_o[...]=(dq_o[...]+jnp.transpose(dqt[...]))*0.125
def bwd_wrap(q,k,v,g,ex,mb,mt_r,n,tm_r,prob_r,dq,dk,dv,qaug,kaug,gaug,vaug,dqt,dqs,dks,dvs):
    bwd_kernel(q,k,v,g,ex,mb,mt_r,n,tm_r,prob_r,dqs,dks,dvs,qaug,kaug,gaug,vaug,dqt)
    dq[...]=dqs[...].astype(BF);dk[...]=dks[...].astype(BF);dv[...]=dvs[...].astype(BF)
def attn_bwd(qkv,g,ex,MB,MT,N,TM,prob):
    H=N.shape[0]; P2=H//2
    ps=lambda off: pl.BlockSpec((L,128),lambda p,off=off:(0,off+p))
    hs=lambda a,b: pl.BlockSpec((2,a,b),lambda p:(p,0,0))
    o=jax.ShapeDtypeStruct((L,P2*128),BF)
    return pl.pallas_call(bwd_wrap,grid=(P2,),
      in_specs=[ps(0),ps(P2),ps(2*P2),ps(0),ps(0),hs(L,128),hs(128,L),hs(L,128),hs(128,L),hs(128,L)],
      out_specs=[ps(0),ps(0),ps(0)],
      out_shape=[o,o,o],
      scratch_shapes=[pltpu.VMEM((L,256),BF),pltpu.VMEM((L,256),BF),pltpu.VMEM((L,128),BF),pltpu.VMEM((L,128),BF),pltpu.VMEM((128,L),F32)]+[pltpu.VMEM((L,128),F32)]*3,
      compiler_params=pltpu.CompilerParams(vmem_limit_bytes=50<<20))(qkv,qkv,qkv,g,ex,MB,MT,N,TM,prob)
MESH=pl.DeviceIdType.MESH


GN=1;GM=1;SA=1;SN=1
def NOP(p): pass
class Place:
    def __init__(self, nb):
        self.nz=nb//4
        self.b=lax.axis_index("batch"); self.h=lax.axis_index("head")
        self.z=self.b//4; self.r=lax.rem(self.b,4)
        even=lax.rem(self.r,2)==0
        self.rx=jnp.where(even,self.r+1,self.r-1)
        self.ry=jnp.where(self.r<2,self.r+2,self.r-2)
        self.rd=3-self.r
        self.X=(self.z*4+self.rx,self.h); self.Y=(self.z*4+self.ry,self.h)
        self.up=(self.b+4,self.h); self.dn=(self.b-4,self.h); self.twin=(self.b,1-self.h)
    def barrier(self):
        bar=pltpu.get_barrier_semaphore()
        for d in (self.X,self.Y,self.twin):
            pl.semaphore_signal(bar,inc=1,device_id=d,device_id_type=MESH)
        @pl.when(self.z<self.nz-1)
        def _(): pl.semaphore_signal(bar,inc=1,device_id=self.up,device_id_type=MESH)
        @pl.when(self.z>0)
        def _(): pl.semaphore_signal(bar,inc=1,device_id=self.dn,device_id_type=MESH)
        lines=jnp.where(self.z<self.nz-1,1,0)+jnp.where(self.z>0,1,0)
        pl.semaphore_wait(bar,3+lines)

def rc(src,dst,ss,rs,dev):
    return pltpu.make_async_remote_copy(src_ref=src,dst_ref=dst,send_sem=ss,recv_sem=rs,device_id=dev,device_id_type=MESH)

class Gather:
    def __init__(self, pc, g, ss, rs):
        self.pc=pc; self.g=g; self.ss=ss; self.rs=rs; self.n=2*(pc.nz-1)
    def cz(self,p,zz,k,dev):
        s=self.g.at[p,zz,self.pc.r]
        return rc(s,s,self.ss.at[p,k],self.rs.at[p,k],dev)
    def z0(self,p):
        c=self.pc
        @pl.when(c.z<c.nz-1)
        def _(): self.cz(p,c.z,0,c.up).start()
        @pl.when(c.z>0)
        def _(): self.cz(p,c.z,1,c.dn).start()
    def zk(self,p,d):
        c=self.pc
        @pl.when(c.z-d>=0)
        def _():
            self.cz(p,c.z-d,2*(d-1),c.up).wait_recv()
        if d<c.nz-1:
            @pl.when((c.z-d>=0)&(c.z<c.nz-1))
            def _(): self.cz(p,c.z-d,2*d,c.up).start()
        @pl.when(c.z+d<c.nz)
        def _():
            self.cz(p,c.z+d,2*(d-1)+1,c.dn).wait_recv()
        if d<c.nz-1:
            @pl.when((c.z+d<c.nz)&(c.z>0))
            def _(): self.cz(p,c.z+d,2*d+1,c.dn).start()
    def cb(self,p,r,k,dev):
        s=self.g.at[p,:,r]
        return rc(s,s,self.ss.at[p,self.n+k],self.rs.at[p,self.n+k],dev)
    def ch(self,p,r,lo,k,dev):
        h=self.pc.nz//2
        s=self.g.at[p,pl.ds(0,h),r] if lo else self.g.at[p,pl.ds(h,self.pc.nz-h),r]
        return rc(s,s,self.ss.at[p,self.n+k],self.rs.at[p,self.n+k],dev)
    def x0(self,p):
        c=self.pc
        self.cb(p,c.r,0,c.X).start(); self.cb(p,c.r,1,c.Y).start()
    def x1(self,p):
        c=self.pc
        self.cb(p,c.rx,0,c.X).wait_recv()
        self.ch(p,c.rx,True,2,c.Y).start()
        self.cb(p,c.ry,1,c.Y).wait_recv()
        self.ch(p,c.ry,False,3,c.X).start()
    def x2(self,p):
        c=self.pc
        self.ch(p,c.rd,True,2,c.Y).wait_recv()
        self.ch(p,c.rd,False,3,c.X).wait_recv()
    def drain(self,p):
        c=self.pc
        for d in range(c.nz-1):
            @pl.when((c.z-d>=0)&(c.z<c.nz-1))
            def _(): self.cz(p,c.z-d,2*d,c.up).wait_send()
            @pl.when((c.z+d<c.nz)&(c.z>0))
            def _(): self.cz(p,c.z+d,2*d+1,c.dn).wait_send()
        self.cb(p,c.r,0,c.X).wait_send(); self.cb(p,c.r,1,c.Y).wait_send()
        self.ch(p,c.rx,True,2,c.Y).wait_send(); self.ch(p,c.ry,False,3,c.X).wait_send()
    def steps(self):
        nz=self.pc.nz
        def last(p):
            self.zk(p,nz-1); self.x0(p)
        return [self.z0]+[functools.partial(lambda d,p:self.zk(p,d),d) for d in range(1,nz-1)]+[last]+[NOP]*GN+[self.x1]+[NOP]*GM+[self.x2]

class Scatter:
    def __init__(self, pc, g, d, rx, ry, ru, rd, ss, rs):
        self.pc=pc;self.g=g;self.d=d;self.bx=rx;self.by=ry;self.bu=ru;self.bd=rd;self.ss=ss;self.rs=rs
        self.h=pc.nz//2
    def half(self,p,r,lo):
        h=self.h; n=self.pc.nz
        return (self.g.at[p,pl.ds(0,h),r],self.d.at[p,pl.ds(0,h)]) if lo else (self.g.at[p,pl.ds(h,n-h),r],self.d.at[p,pl.ds(h,n-h)])
    def c0(self,p,lo):
        s,t=self.half(p,self.pc.rd,lo); k=0 if lo else 1
        return rc(s,t,self.ss.at[p,k],self.rs.at[p,k],self.pc.X if lo else self.pc.Y)
    def c1(self,p,x):
        c=self.pc
        return rc(self.g.at[p,:,c.rx if x else c.ry],(self.bx if x else self.by).at[p],self.ss.at[p,2 if x else 3],self.rs.at[p,2 if x else 3],c.X if x else c.Y)
    def cu(self,p,zz,up):
        c=self.pc; k=4+zz if up else 4+c.nz+zz
        return rc(self.g.at[p,zz,c.r],(self.bu if up else self.bd).at[p,zz],self.ss.at[p,k],self.rs.at[p,k],c.up if up else c.dn)
    def add(self,dst,*srcs):
        v=dst[...].astype(F32)
        for s in srcs: v=v+s[...].astype(F32)
        dst[...]=v.astype(BF)
    def s0(self,p):
        self.c0(p,True).start(); self.c0(p,False).start()
    def s1(self,p):
        c=self.pc;h=self.h;n=c.nz
        self.c0(p,True).wait_recv()
        self.add(self.g.at[p,pl.ds(0,h),c.ry],self.d.at[p,pl.ds(0,h)])
        self.c1(p,False).start()
        self.c0(p,False).wait_recv()
        self.add(self.g.at[p,pl.ds(h,n-h),c.rx],self.d.at[p,pl.ds(h,n-h)])
        self.c1(p,True).start()
    def s2(self,p):
        c=self.pc
        self.c1(p,True).wait_recv(); self.c1(p,False).wait_recv()
        self.add(self.g.at[p,:,c.r],self.bx.at[p],self.by.at[p])
        self.zk(p,0)
    def zk(self,p,k):
        c=self.pc; nz=c.nz
        @pl.when(c.z==k)
        def _():
            for zz in range(nz-1,k,-1):
                if k>0:
                    self.cu(p,zz,True).wait_recv()
                    self.add(self.g.at[p,zz,c.r],self.bu.at[p,zz])
                self.cu(p,zz,True).start()
        @pl.when(c.z==nz-1-k)
        def _():
            for zz in range(0,nz-1-k):
                if k>0:
                    self.cu(p,zz,False).wait_recv()
                    self.add(self.g.at[p,zz,c.r],self.bd.at[p,zz])
                self.cu(p,zz,False).start()
    def fin(self,p,out):
        c=self.pc
        out[p]=self.g[p,c.z,c.r].astype(F32)
        @pl.when(c.z>0)
        def _():
            self.cu(p,c.z,True).wait_recv()
            out[p]+=self.bu[p,c.z].astype(F32)
        @pl.when(c.z<c.nz-1)
        def _():
            self.cu(p,c.z,False).wait_recv()
            out[p]+=self.bd[p,c.z].astype(F32)
    def drain(self,p):
        c=self.pc; nz=c.nz
        self.c0(p,True).wait_send(); self.c0(p,False).wait_send()
        self.c1(p,True).wait_send(); self.c1(p,False).wait_send()
        for zz in range(nz):
            @pl.when(zz>c.z)
            def _(): self.cu(p,zz,True).wait_send()
            @pl.when(zz<c.z)
            def _(): self.cu(p,zz,False).wait_send()
    def steps(self,out):
        nz=self.pc.nz
        return [self.s0]+[NOP]*SA+[self.s1]+[NOP]*SN+[self.s2]+[functools.partial(lambda k,p:self.zk(p,k),k) for k in range(1,nz-1)]+[lambda p:self.fin(p,out)]

def run_all(steps,parts):
    n=len(parts); S=len(steps)
    for t in range(n+S-1):
        for s in range(S-1,-1,-1):
            if 0<=t-s<n: steps[s](parts[t-s])

def ag_kernel(nb,w,go,g,ss,rs,ls):
    pc=Place(nb); pc.barrier()
    NP=w.shape[0]
    G=Gather(pc,g,ss,rs)
    for p in range(NP): g[p,pc.z,pc.r]=w[p]
    run_all(G.steps(),list(range(NP)))
    for p in range(NP): G.drain(p)
    c=pltpu.make_async_copy(g,go,ls); c.start(); c.wait()
def all_gather(w,nb,cid=0):
    NP,R,N=w.shape; nz=nb//4
    return pl.pallas_call(functools.partial(ag_kernel,nb),
      out_shape=jax.ShapeDtypeStruct((NP,nz,4,R,N),BF),
      in_specs=[pl.BlockSpec(memory_space=pltpu.VMEM)],out_specs=pl.BlockSpec(memory_space=pl.ANY),
      scratch_shapes=[pltpu.VMEM((NP,nz,4,R,N),BF),pltpu.SemaphoreType.DMA((NP,2*(nz-1)+4)),pltpu.SemaphoreType.DMA((NP,2*(nz-1)+4)),pltpu.SemaphoreType.DMA],
      compiler_params=pltpu.CompilerParams(collective_id=cid,has_side_effects=True,vmem_limit_bytes=60<<20))(w)
def rs_kernel(nb,gi,out,g,d,bx,by,bu,bd,ss,rs,ls):
    pc=Place(nb); pc.barrier()
    NP=g.shape[0]
    c=pltpu.make_async_copy(gi,g,ls); c.start(); c.wait()
    S=Scatter(pc,g,d,bx,by,bu,bd,ss,rs)
    run_all(S.steps(out),list(range(NP)))
    for p in range(NP): S.drain(p)
def reduce_scatter(g,cid=1):
    NP,nz,_,R,N=g.shape
    land=pltpu.VMEM((NP,nz,R,N),BF)
    return pl.pallas_call(functools.partial(rs_kernel,nz*4),
      out_shape=jax.ShapeDtypeStruct((NP,R,N),F32),
      in_specs=[pl.BlockSpec(memory_space=pl.ANY)],out_specs=pl.BlockSpec(memory_space=pltpu.VMEM),
      scratch_shapes=[pltpu.VMEM((NP,nz,4,R,N),BF)]+[land]*5+[pltpu.SemaphoreType.DMA((NP,4+2*nz)),pltpu.SemaphoreType.DMA((NP,4+2*nz)),pltpu.SemaphoreType.DMA],
      compiler_params=pltpu.CompilerParams(collective_id=cid,has_side_effects=True,vmem_limit_bytes=60<<20))(g)

EPS=1e-5
def norm_forward(values, gain_row):
    row_mean = jnp.mean(values, axis=-1, keepdims=True)
    centred = values - row_mean
    inverse = lax.rsqrt(jnp.mean(centred * centred, axis=-1, keepdims=True) + EPS)
    normed = centred * inverse
    return (normed * gain_row, normed, inverse)

def norm_backward(grad_out, normed, inverse, gain_row):
    grad_normed = grad_out * gain_row
    gain_grad = jnp.sum(grad_out * normed, axis=0)
    inner_term = grad_normed - jnp.mean(grad_normed, axis=-1, keepdims=True)
    inner_term = inner_term - normed * jnp.mean(grad_normed * normed, axis=-1, keepdims=True)
    return (inner_term * inverse, gain_grad)

def pack(q,o,u,d,ga,gf):
    R=q.shape[0]
    qp=q.reshape(R,3,3,128).transpose(2,0,1,3).reshape(3,R,384)
    up=u.reshape(R,4,384).transpose(1,0,2)
    dn=d.T.reshape(R,4,384).transpose(1,0,2)
    gains=jnp.pad(jnp.stack([ga,gf],1),((0,0),(0,382)))
    return jnp.concatenate([qp,o.T[None],up,dn,gains[None]],0)

def on_device(tokens,attn_gain,qkv_weight,out_weight,ffn_gain,up_weight,down_weight,cotangent,segment,cluster,top_keys):
    nb=lax.axis_size("batch")
    x=tokens[0].astype(F32)
    seg=segment; cl=cluster[0]; tk=top_keys[0]
    half=L//2
    off=lax.axis_index("head")*half
    share=lambda v: lax.dynamic_slice_in_dim(v,off,half,0)
    w=pack(qkv_weight,out_weight,up_weight,down_weight,attn_gain,ffn_gain)
    R=w.shape[1]
    custom=R%16==0 and nb%4==0
    if custom:
        W=all_gather(w,nb).reshape(13,768,384)
    else:
        W=lax.all_gather(w,"batch",axis=1,tiled=True)
    g1=W[12,:,0].astype(F32); g2=W[12,:,1].astype(F32)
    M,MT,N,TM=masks(cl,tk)
    n1,p1,i1=norm_forward(x,g1)
    n1=n1.astype(BF)
    mm=lambda s,a,b: jnp.einsum(s,a,b,preferred_element_type=F32)
    wq=W[0:3]; wo=W[3]; wu=W[4:8]; wd=W[8:12]
    qkv=mm("td,pdf->ptf",n1,wq).astype(BF)
    qkv=qkv.reshape(3,L,3,128).transpose(1,2,0,3).reshape(L,1152)
    att,ex,mb,prob=attn_fwd(qkv,M,MT,N,TM,seg)
    part=mm("te,fe->tf",att,wo)
    hid=x+lax.psum(part.astype(BF),"head").astype(F32)
    n2,p2,i2=norm_forward(hid,g2)
    n2=n2.astype(BF)
    up=mm("td,pdf->ptf",n2,wu)
    act=jax.nn.gelu(up).astype(BF)
    fp=mm("ptf,pdf->td",act,wd)
    output=(share(hid)+share(lax.psum(fp.astype(BF),"head").astype(F32))).astype(BF)[None]
    ct=cotangent[0]
    dwn_g=mm("td,ptf->pdf",ct,act)
    ga=mm("td,pdf->ptf",ct,wd)
    _,pull=jax.vjp(jax.nn.gelu,up)
    gu=pull(ga)[0].astype(BF)
    up_g=mm("td,ptf->pdf",n2,gu)
    gn=lax.psum(mm("ptf,pdf->td",gu,wu).astype(BF),"head").astype(F32)
    back,g2g=norm_backward(gn,p2,i2,g2)
    gh=ct.astype(F32)+back
    gat=gh.astype(BF)
    out_g=mm("tf,te->fe",gat,att)
    g=mm("tf,fe->te",gat,wo).astype(BF)
    dq,dk,dv=attn_bwd(qkv,g,ex,mb,MT,N,TM,prob)
    dqkv=jnp.stack([dq,dk,dv],1).reshape(L,3,3,128).transpose(2,0,1,3).reshape(3,L,384)
    qkv_g=mm("td,ptf->pdf",n1,dqkv)
    gn1=lax.psum(mm("ptf,pdf->td",dqkv,wq).astype(BF),"head").astype(F32)
    back1,g1g=norm_backward(gn1,p1,i1,g1)
    tg=(share(gh)+share(back1))[None]
    gg=jnp.pad(jnp.stack([g1g,g2g],1),((0,0),(0,382)))
    G=jnp.concatenate([dwn_g,up_g,out_g[None],qkv_g,gg[None]],0)
    if custom:
        S=reduce_scatter(G.astype(BF).reshape(13,nb//4,4,R,384))
    else:
        S=lax.psum_scatter(G,"batch",scatter_dimension=1,tiled=True)
    cat=lambda a: a.transpose(1,0,2).reshape(R,-1)
    qg=S[9:12].reshape(3,R,3,128).transpose(1,2,0,3).reshape(R,3,384)
    return output,tg,S[12,:,0],qg,S[8].T,S[12,:,1],cat(S[4:8]),cat(S[0:4]).T

def solution(mesh):
    in_specs=(P("batch",None,None),P("batch"),P("batch",None,"head"),P("head","batch"),P("batch"),P("batch","head"),P("head","batch"),P("batch",None,None),P("batch",None),P("batch","head",None),P("batch","head",None,None))
    out_specs=(P("batch","head",None),P("batch","head",None),P("batch"),P("batch",None,"head"),P("head","batch"),P("batch"),P("batch","head"),P("head","batch"))
    return jax.shard_map(on_device,mesh=mesh,in_specs=in_specs,out_specs=out_specs,check_vma=False)
```

```python
import functools

import jax
import jax.numpy as jnp
from jax import lax
from jax.experimental import pallas as pl
from jax.experimental.pallas import tpu as pltpu
from jax.sharding import PartitionSpec as P

F32=jnp.float32; BF=jnp.bfloat16
BIG=1e30
NT=(((1,),(1,)),((),()))
TN=(((0,),(0,)),((),()))
NN=(((1,),(0,)),((),()))
def dot(a,b,dims=NN): return lax.dot_general(a,b,dims,preferred_element_type=F32)
def split3(x):
    a=x.astype(BF); r=x-a.astype(F32); b=r.astype(BF); c=(r-b.astype(F32)).astype(BF)
    return a,b,c
def split2(x):
    a=x.astype(BF); return a,(x-a.astype(F32)).astype(BF)
L=1024
def lane(shape): return lax.broadcasted_iota(jnp.int32,shape,len(shape)-1)
def sub(shape): return lax.broadcasted_iota(jnp.int32,shape,len(shape)-2)

def build_masks(own_row, topT):
    mt=jnp.where(own_row==sub((128,L)),1.0,0.0).astype(BF)
    m=jnp.transpose(mt)
    hi=lax.shift_right_arithmetic(topT,5); bit=lax.shift_left(jnp.int32(1),topT&31)
    words=L//32
    a_iota=sub((words,128))
    w=jnp.zeros((words,128),jnp.int32)
    for t in range(topT.shape[0]):
        w=w|jnp.where(hi[t:t+1]==a_iota,bit[t:t+1],0)
    b_iota=sub((32,128)); ln=lane((32,128))
    extra=(ln>=100)&(ln<103)
    ns=[];ts=[]
    for a in range(words):
        b=(lax.shift_right_logical(jnp.broadcast_to(w[a:a+1],(32,128)),b_iota)&1)
        tmf=b.astype(F32)
        ts.append(tmf)
        ns.append(jnp.where(extra,-1.0,jnp.where(b==1,0.0,-BIG)))
    n=jnp.concatenate(ns,0).astype(BF)
    tm=jnp.transpose(jnp.concatenate(ts,0)).astype(BF)
    return m,mt,n,tm


TQ = 256
TJ = 256
MESH=pl.DeviceIdType.MESH


GN=1;GM=1;SA=1;SN=1
def NOP(p): pass
class Place:
    def __init__(self, nb):
        self.nz=nb//4
        self.b=lax.axis_index("batch"); self.h=lax.axis_index("head")
        self.z=self.b//4; self.r=lax.rem(self.b,4)
        even=lax.rem(self.r,2)==0
        self.rx=jnp.where(even,self.r+1,self.r-1)
        self.ry=jnp.where(self.r<2,self.r+2,self.r-2)
        self.rd=3-self.r
        self.X=(self.z*4+self.rx,self.h); self.Y=(self.z*4+self.ry,self.h)
        self.up=(self.b+4,self.h); self.dn=(self.b-4,self.h); self.twin=(self.b,1-self.h)
    def barrier(self):
        bar=pltpu.get_barrier_semaphore()
        for d in (self.X,self.Y,self.twin):
            pl.semaphore_signal(bar,inc=1,device_id=d,device_id_type=MESH)
        @pl.when(self.z<self.nz-1)
        def _(): pl.semaphore_signal(bar,inc=1,device_id=self.up,device_id_type=MESH)
        @pl.when(self.z>0)
        def _(): pl.semaphore_signal(bar,inc=1,device_id=self.dn,device_id_type=MESH)
        lines=jnp.where(self.z<self.nz-1,1,0)+jnp.where(self.z>0,1,0)
        pl.semaphore_wait(bar,3+lines)

def rc(src,dst,ss,rs,dev):
    return pltpu.make_async_remote_copy(src_ref=src,dst_ref=dst,send_sem=ss,recv_sem=rs,device_id=dev,device_id_type=MESH)

class Gather:
    def __init__(self, pc, g, ss, rs):
        self.pc=pc; self.g=g; self.ss=ss; self.rs=rs; self.n=2*(pc.nz-1)
    def cz(self,p,zz,k,dev):
        s=self.g.at[p,zz,self.pc.r]
        return rc(s,s,self.ss.at[p,k],self.rs.at[p,k],dev)
    def z0(self,p):
        c=self.pc
        @pl.when(c.z<c.nz-1)
        def _(): self.cz(p,c.z,0,c.up).start()
        @pl.when(c.z>0)
        def _(): self.cz(p,c.z,1,c.dn).start()
    def zk(self,p,d):
        c=self.pc
        @pl.when(c.z-d>=0)
        def _():
            self.cz(p,c.z-d,2*(d-1),c.up).wait_recv()
        if d<c.nz-1:
            @pl.when((c.z-d>=0)&(c.z<c.nz-1))
            def _(): self.cz(p,c.z-d,2*d,c.up).start()
        @pl.when(c.z+d<c.nz)
        def _():
            self.cz(p,c.z+d,2*(d-1)+1,c.dn).wait_recv()
        if d<c.nz-1:
            @pl.when((c.z+d<c.nz)&(c.z>0))
            def _(): self.cz(p,c.z+d,2*d+1,c.dn).start()
    def cb(self,p,r,k,dev):
        s=self.g.at[p,:,r]
        return rc(s,s,self.ss.at[p,self.n+k],self.rs.at[p,self.n+k],dev)
    def ch(self,p,r,lo,k,dev):
        h=self.pc.nz//2
        s=self.g.at[p,pl.ds(0,h),r] if lo else self.g.at[p,pl.ds(h,self.pc.nz-h),r]
        return rc(s,s,self.ss.at[p,self.n+k],self.rs.at[p,self.n+k],dev)
    def x0(self,p):
        c=self.pc
        self.cb(p,c.r,0,c.X).start(); self.cb(p,c.r,1,c.Y).start()
    def x1(self,p):
        c=self.pc
        self.cb(p,c.rx,0,c.X).wait_recv()
        self.ch(p,c.rx,True,2,c.Y).start()
        self.cb(p,c.ry,1,c.Y).wait_recv()
        self.ch(p,c.ry,False,3,c.X).start()
    def x2(self,p):
        c=self.pc
        self.ch(p,c.rd,True,2,c.Y).wait_recv()
        self.ch(p,c.rd,False,3,c.X).wait_recv()
    def drain(self,p):
        c=self.pc
        for d in range(c.nz-1):
            @pl.when((c.z-d>=0)&(c.z<c.nz-1))
            def _(): self.cz(p,c.z-d,2*d,c.up).wait_send()
            @pl.when((c.z+d<c.nz)&(c.z>0))
            def _(): self.cz(p,c.z+d,2*d+1,c.dn).wait_send()
        self.cb(p,c.r,0,c.X).wait_send(); self.cb(p,c.r,1,c.Y).wait_send()
        self.ch(p,c.rx,True,2,c.Y).wait_send(); self.ch(p,c.ry,False,3,c.X).wait_send()
    def steps(self):
        nz=self.pc.nz
        def last(p):
            self.zk(p,nz-1); self.x0(p)
        return [self.z0]+[functools.partial(lambda d,p:self.zk(p,d),d) for d in range(1,nz-1)]+[last]+[NOP]*GN+[self.x1]+[NOP]*GM+[self.x2]

class Scatter:
    def __init__(self, pc, g, d, rx, ry, ru, rd, ss, rs):
        self.pc=pc;self.g=g;self.d=d;self.bx=rx;self.by=ry;self.bu=ru;self.bd=rd;self.ss=ss;self.rs=rs
        self.h=pc.nz//2
    def half(self,p,r,lo):
        h=self.h; n=self.pc.nz
        return (self.g.at[p,pl.ds(0,h),r],self.d.at[p,pl.ds(0,h)]) if lo else (self.g.at[p,pl.ds(h,n-h),r],self.d.at[p,pl.ds(h,n-h)])
    def c0(self,p,lo):
        s,t=self.half(p,self.pc.rd,lo); k=0 if lo else 1
        return rc(s,t,self.ss.at[p,k],self.rs.at[p,k],self.pc.X if lo else self.pc.Y)
    def c1(self,p,x):
        c=self.pc
        return rc(self.g.at[p,:,c.rx if x else c.ry],(self.bx if x else self.by).at[p],self.ss.at[p,2 if x else 3],self.rs.at[p,2 if x else 3],c.X if x else c.Y)
    def cu(self,p,zz,up):
        c=self.pc; k=4+zz if up else 4+c.nz+zz
        return rc(self.g.at[p,zz,c.r],(self.bu if up else self.bd).at[p,zz],self.ss.at[p,k],self.rs.at[p,k],c.up if up else c.dn)
    def add(self,dst,*srcs):
        v=dst[...].astype(F32)
        for s in srcs: v=v+s[...].astype(F32)
        dst[...]=v.astype(BF)
    def s0(self,p):
        self.c0(p,True).start(); self.c0(p,False).start()
    def s1(self,p):
        c=self.pc;h=self.h;n=c.nz
        self.c0(p,True).wait_recv()
        self.add(self.g.at[p,pl.ds(0,h),c.ry],self.d.at[p,pl.ds(0,h)])
        self.c1(p,False).start()
        self.c0(p,False).wait_recv()
        self.add(self.g.at[p,pl.ds(h,n-h),c.rx],self.d.at[p,pl.ds(h,n-h)])
        self.c1(p,True).start()
    def s2(self,p):
        c=self.pc
        self.c1(p,True).wait_recv(); self.c1(p,False).wait_recv()
        self.add(self.g.at[p,:,c.r],self.bx.at[p],self.by.at[p])
        self.zk(p,0)
    def zk(self,p,k):
        c=self.pc; nz=c.nz
        @pl.when(c.z==k)
        def _():
            for zz in range(nz-1,k,-1):
                if k>0:
                    self.cu(p,zz,True).wait_recv()
                    self.add(self.g.at[p,zz,c.r],self.bu.at[p,zz])
                self.cu(p,zz,True).start()
        @pl.when(c.z==nz-1-k)
        def _():
            for zz in range(0,nz-1-k):
                if k>0:
                    self.cu(p,zz,False).wait_recv()
                    self.add(self.g.at[p,zz,c.r],self.bd.at[p,zz])
                self.cu(p,zz,False).start()
    def fin(self,p,out):
        c=self.pc
        out[p]=self.g[p,c.z,c.r].astype(F32)
        @pl.when(c.z>0)
        def _():
            self.cu(p,c.z,True).wait_recv()
            out[p]+=self.bu[p,c.z].astype(F32)
        @pl.when(c.z<c.nz-1)
        def _():
            self.cu(p,c.z,False).wait_recv()
            out[p]+=self.bd[p,c.z].astype(F32)
    def drain(self,p):
        c=self.pc; nz=c.nz
        self.c0(p,True).wait_send(); self.c0(p,False).wait_send()
        self.c1(p,True).wait_send(); self.c1(p,False).wait_send()
        for zz in range(nz):
            @pl.when(zz>c.z)
            def _(): self.cu(p,zz,True).wait_send()
            @pl.when(zz<c.z)
            def _(): self.cu(p,zz,False).wait_send()
    def steps(self,out):
        nz=self.pc.nz
        return [self.s0]+[NOP]*SA+[self.s1]+[NOP]*SN+[self.s2]+[functools.partial(lambda k,p:self.zk(p,k),k) for k in range(1,nz-1)]+[lambda p:self.fin(p,out)]


EPS = 1e-5
RT = 256


def pick(static, cond, body):
    if isinstance(cond, (bool, int)):
        if cond:
            body()
    else:
        pl.when(cond)(body)


def norm_rows(values):
    mean = jnp.mean(values, axis=1, keepdims=True)
    centred = values - mean
    inverse = lax.rsqrt(jnp.mean(centred * centred, axis=1, keepdims=True) + EPS)
    return centred * inverse, inverse


def gelu_both(u):
    c = 0.7978845608028654
    u2 = u * u
    t = jnp.tanh(c * u * (1.0 + 0.044715 * u2))
    half = 0.5 + 0.5 * t
    act = u * half
    grad = half + (0.5 * c) * u * (1.0 - t * t) * (1.0 + (3 * 0.044715) * u2)
    return act, grad


def flat(ref, p):
    v = ref[p]
    return v.reshape(-1, v.shape[-1])


def tiles(n):
    return lambda f: pl.loop(0, n)(f)


def rows_of(i, n=RT):
    return pl.ds(pl.multiple_of(i * n, n), n)


def twin_copy(pc, src, dst, ss, rs):
    return rc(src, dst, ss, rs, pc.twin)


def fwd_head(p, h, qkv, mb, mt_s, n_s, tm_s, seg, qaug, kaug, att, ex, prob_o):
    odd = h == 1
    hh = 2 * p + h
    q = qkv[p, :, 0:128]
    k = qkv[p, :, 128:256]
    v = qkv[p, :, 256:384]
    ln = lane((L, 128))
    mine = (ln >= 64) if odd else (ln < 64)
    lc = lane((128, 128))
    minec = (lc >= 64) if odd else (lc < 64)
    zero = jnp.zeros((), BF)
    qm = jnp.where(mine, q, zero)
    vaug = jnp.where(mine, v, jnp.ones((), BF))
    mt = mt_s[hh]
    cnt = jnp.maximum(jnp.sum(mt.astype(F32), axis=1, keepdims=True), 1.0)
    cen = (dot(mt, qm) / cnt).astype(BF)
    cs = (cen.astype(F32) * 0.125).astype(BF)
    s = dot(cs, k, NT)
    cm = lax.rem(sub((128, 1)), jnp.int32(10))
    s = jnp.where(seg[...] == cm, s, -BIG)
    mx = jnp.max(s, axis=1, keepdims=True)
    e = jnp.exp(s - mx)
    prob = e / jnp.sum(e, axis=1, keepdims=True)
    tmf = tm_s[hh].astype(F32)
    mass = jnp.sum(prob * tmf, axis=1, keepdims=True)
    prob_o[hh] = prob.astype(BF)
    rest = dot((prob * (1.0 - tmf)).astype(BF), v)
    rh, rl = split2(jnp.where(minec, rest, jnp.broadcast_to(mass, (128, 128))))
    rr = jnp.concatenate([rh, rl], 1)
    qaug[:, :128] = (qm.astype(F32) * 0.125).astype(BF)
    qaug[:, 128:] = mb[hh]
    kaug[:, :128] = k
    kaug[:, 128:] = n_s[hh]
    lt = lane((TQ, 128))
    minet = (lt >= 64) if odd else (lt < 64)
    cols = pl.ds(pl.multiple_of(p * 128, 128), 128)
    for t in range(L // TQ):
        sl = pl.ds(t * TQ, TQ)
        sc = dot(qaug[sl, :], kaug[...], NT)
        mm = jnp.max(sc, axis=1, keepdims=True)
        pr = jnp.exp(sc - mm).astype(BF)
        o = dot(pr, vaug)
        mt_ = qaug[sl, 128:]
        ee = dot(mt_, rr)
        ee = ee[:, :128] + ee[:, 128:]
        osw = pltpu.roll(o, 64, 1)
        esw = pltpu.roll(ee, 64, 1)
        exact = o / osw
        a = exact * esw + ee
        tot = jnp.where(minet, osw, o)
        ms = jnp.where(minet, esw, ee)
        lse = mm + jnp.log(tot) - jnp.log(jnp.maximum(ms, 1e-37))
        h3, m3, l3 = split3(lse)
        mb[hh, sl, :] = jnp.where(lt == 100, h3.astype(F32), jnp.where(lt == 101, m3.astype(F32), jnp.where(lt == 102, l3.astype(F32), mt_.astype(F32)))).astype(BF)
        if odd:
            att[sl, cols] = jnp.where(lt < 64, att[sl, cols], a.astype(BF))
            ex[sl, cols] = jnp.where(lt < 64, ex[sl, cols], exact.astype(BF))
        else:
            att[sl, cols] = a.astype(BF)
            ex[sl, cols] = exact.astype(BF)


N1OUT = ("gr", "n1", "qkv", "att", "ex", "mb", "mt", "ns", "tm", "prob", "hid", "n2", "act", "dg")


def k1_shapes(w_shape):
    H = 6
    f = lambda *s: (s, F32)
    b = lambda *s: (s, BF)
    return {
        "gr": f(8, 768), "n1": b(L, 768), "qkv": b(3, L, 384), "att": b(L, 384), "ex": b(L, 384),
        "mb": b(H, L, 128), "mt": b(H, 128, L), "ns": b(H, L, 128), "tm": b(H, 128, L), "prob": b(H, 128, L),
        "hid": f(L, 768), "n2": b(L, 768), "act": b(4, L, 384), "dg": b(4, L, 384),
    }


def k1_body(nb, custom, *refs):
    refs = list(refs)
    take = lambda n: [refs.pop(0) for _ in range(n)]
    x, w, gw, seg, cl, tt = take(6)
    outs = dict(zip(N1OUT, take(len(N1OUT))))
    (y,) = take(1)
    if custom:
        (wo,) = take(1)
    s = dict(zip(N1OUT, take(len(N1OUT))))
    qaug, kaug, eb, er, fb, fr, osem, es, ers, fs, frs = take(11)
    pc = Place(nb)
    pc.barrier()
    if custom:
        g, gg, ss, rs, gss, grs, wsem = take(7)
        G = Gather(pc, g, ss, rs)
        Gg = Gather(pc, gg, gss, grs)
        g[:, pc.z, pc.r] = w[...]
        gg[0, pc.z, pc.r] = gw[...]
        steps, gsteps = G.steps(), Gg.steps()
        NP = 12

        def tick(t):
            for i in range(len(steps) - 1, -1, -1):
                p = t - i
                ok = (p >= 0 and p < NP) if isinstance(t, int) else ((p >= 0) & (p < NP))
                pick(None, ok, lambda i=i, p=p: steps[i](p))
                if isinstance(t, int) and t == i:
                    gsteps[i](0)
        last = NP - 1 + len(steps) - 1
        first = len(steps) - 1
    else:
        g, gg = w, gw
        tick = lambda t: None
        last, first = 18, 7
    copies = []

    def out(name):
        c = pltpu.make_async_copy(s[name], outs[name], osem.at[N1OUT.index(name)])
        c.start()
        copies.append(c)

    hid, n1, n2, qkv, att, ex = s["hid"], s["n1"], s["n2"], s["qkv"], s["att"], s["ex"]
    tick(0)

    @tiles(L // RT)
    def _(i):
        hid[rows_of(i), :] = norm_rows(x[rows_of(i), :].astype(F32))[0]

    tick(1)

    def mask(h):
        a, b, c, d = build_masks(cl[h], tt[h])
        s["mb"][h], s["mt"][h], s["ns"][h], s["tm"][h] = a, b, c, d

    pl.loop(0, 2)(mask)
    tick(2)
    pl.loop(2, 4)(mask)
    tick(3)
    pl.loop(4, 6)(mask)
    for n in ("mt", "ns", "tm"):
        out(n)
    for t in range(4, first + 1):
        tick(t)
    gains = gg[0].reshape(768, 128) if custom else gg[...]
    s["gr"][...] = jnp.transpose(gains.astype(F32))[0:8]
    out("gr")

    @tiles(L // RT)
    def _(i):
        n1[rows_of(i), :] = (hid[rows_of(i), :] * s["gr"][0:1, :]).astype(BF)

    out("n1")

    @pl.loop(0, 3)
    def _(p):
        @tiles(L // RT)
        def _(i):
            qkv[p, rows_of(i), :] = dot(n1[rows_of(i), :], flat(g, p)).astype(BF)
        for h in range(2):
            tick(first + 1 + 3 * p + h)
            fwd_head(p, h, qkv, s["mb"], s["mt"], s["ns"], s["tm"], seg, qaug, kaug, att, ex, s["prob"])
        tick(first + 3 + 3 * p)

    for n in ("qkv", "att", "ex", "mb", "prob"):
        out(n)

    def send1(i):
        return twin_copy(pc, eb.at[rows_of(i)], er.at[rows_of(i)], es.at[i], ers.at[i])

    @tiles(L // RT)
    def _(i):
        eb[rows_of(i), :] = dot(att[rows_of(i), :], flat(g, 3), NT).astype(BF)
        send1(i).start()

    t = first + 10
    if t <= last:
        tick(t)

    @tiles(L // RT)
    def _(i):
        r = rows_of(i)
        send1(i).wait_recv()
        hv = x[r, :].astype(F32) + (eb[r, :].astype(F32) + er[r, :].astype(F32))
        hid[r, :] = hv
        n2[r, :] = (norm_rows(hv)[0] * s["gr"][1:2, :]).astype(BF)

    out("hid")
    out("n2")

    def up(q):
        @tiles(L // RT)
        def _(i):
            a, d = gelu_both(dot(n2[rows_of(i), :], flat(g, 4 + q)))
            s["act"][q, rows_of(i), :] = a.astype(BF)
            s["dg"][q, rows_of(i), :] = d.astype(BF)

    pl.loop(0, 2)(up)
    for t in range(first + 11, last + 1):
        tick(t)
    if custom:
        cw = pltpu.make_async_copy(g, wo, wsem)
        cw.start()
        copies.append(cw)
    pl.loop(2, 4)(up)
    out("act")
    out("dg")
    half = L // 2 // RT

    def part(i):
        acc = dot(s["act"][0, rows_of(i), :], flat(g, 8), NT)
        for q in range(1, 4):
            acc += dot(s["act"][q, rows_of(i), :], flat(g, 8 + q), NT)
        return acc

    def send2(i):
        return twin_copy(pc, fb.at[rows_of(i)], fr.at[rows_of(i)], fs.at[i], frs.at[i])

    @tiles(half)
    def _(i):
        fb[rows_of(i), :] = part((1 - pc.h) * half + i).astype(BF)
        send2(i).start()

    @tiles(half)
    def _(i):
        acc = part(pc.h * half + i).astype(BF).astype(F32)
        send2(i).wait_recv()
        y[rows_of(i), :] = (hid[rows_of(pc.h * half + i), :] + (acc + fr[rows_of(i), :].astype(F32))).astype(BF)

    @tiles(L // RT)
    def _(i):
        send1(i).wait_send()

    @tiles(half)
    def _(i):
        send2(i).wait_send()

    if custom:
        @pl.loop(0, 12)
        def _(p):
            G.drain(p)
        Gg.drain(0)
    for c in copies:
        c.wait()


def vm(shape_dtype):
    return pltpu.VMEM(*shape_dtype)


def forward(nb, custom, x, w, gw, seg, cl, tt):
    shapes = k1_shapes(w.shape)
    sds = lambda sd: jax.ShapeDtypeStruct(*sd)
    V = pl.BlockSpec(memory_space=pltpu.VMEM)
    A = pl.BlockSpec(memory_space=pl.ANY)
    nz = nb // 4
    dma = pltpu.SemaphoreType.DMA
    out_shape = [sds(shapes[n]) for n in N1OUT] + [jax.ShapeDtypeStruct((L // 2, 768), BF)]
    out_specs = [A] * len(N1OUT) + [V]
    scratch = [vm(shapes[n]) for n in N1OUT] + [
        pltpu.VMEM((L, 256), BF), pltpu.VMEM((L, 256), BF), pltpu.VMEM((L, 768), BF), pltpu.VMEM((L, 768), BF),
        pltpu.VMEM((L // 2, 768), BF), pltpu.VMEM((L // 2, 768), BF), dma((len(N1OUT),)), dma((4,)), dma((4,)), dma((2,)), dma((2,))]
    if custom:
        R = w.shape[1]
        ns = 2 * (nz - 1) + 4
        out_shape.append(jax.ShapeDtypeStruct((12, nz, 4, R, 384), BF))
        out_specs.append(A)
        scratch += [pltpu.VMEM((12, nz, 4, R, 384), BF), pltpu.VMEM((1, nz, 4, R, 128), BF), dma((12, ns)), dma((12, ns)), dma((1, ns)), dma((1, ns)), dma]
    r = pl.pallas_call(
        functools.partial(k1_body, nb, custom),
        out_shape=out_shape, in_specs=[V] * 6, out_specs=out_specs, scratch_shapes=scratch,
        compiler_params=pltpu.CompilerParams(collective_id=0, has_side_effects=True, vmem_limit_bytes=62 << 20),
    )(x, w, gw, seg, cl, tt)
    d = dict(zip(N1OUT, r))
    return d, r[len(N1OUT)], (r[-1] if custom else w)


def bwd_head(p, h, s, qaug, kaug, gaug, vaug, dq_o, dk_o, dv_o, dqt):
    qkv, g, ex = s["qkv"], s["gatt"], s["ex"]
    hh = 2 * p + h
    cols = pl.ds(pl.multiple_of(p * 128, 128), 128)
    qv = qkv[p, :, 0:128]
    kv = qkv[p, :, 128:256]
    vv = qkv[p, :, 256:384]
    gv = g[:, cols]
    ln = lane((L, 128))
    zero = jnp.zeros((), BF)
    lc = lane((128, 128))
    kT = jnp.transpose(kv)
    prod = gv.astype(F32) * ex[:, cols].astype(F32)
    mine = (ln >= 64) if h else (ln < 64)
    minec = (lc >= 64) if h else (lc < 64)
    o = 0 if h else 64
    r = jnp.sum(jnp.where(mine, prod, 0.0), axis=1, keepdims=True)
    h3, m3, l3 = split3(r)
    gm = jnp.where(mine, gv, zero)
    ga = jnp.where(ln == o, h3.astype(F32), jnp.where(ln == o + 1, m3.astype(F32), jnp.where(ln == o + 2, l3.astype(F32), gm.astype(F32)))).astype(BF)
    gaug[...] = ga
    vaug[...] = jnp.where(mine, vv, jnp.where((ln >= o) & (ln < o + 3), jnp.full((), -1.0, BF), zero))
    qm = jnp.where(mine, qv, zero)
    qs = (qm.astype(F32) * 0.125).astype(BF)
    qaug[:, :128] = qs
    qaug[:, 128:] = s["mb"][hh]
    kaug[:, :128] = kv
    kaug[:, 128:] = s["ns"][hh]
    mt = s["mt"][hh]
    prob = s["prob"][hh].astype(F32)
    cnt = jnp.maximum(jnp.sum(mt.astype(F32), axis=1, keepdims=True), 1.0)
    cen = (dot(mt, qm) / cnt).astype(BF)
    cs = (cen.astype(F32) * 0.125).astype(BF)
    gr = dot(mt, ga)
    gmass = jnp.sum(jnp.where((lc >= o) & (lc < o + 3), gr, 0.0), axis=1, keepdims=True)
    grest = jnp.where(minec, gr, 0.0).astype(BF)
    top = s["tm"][hh].astype(F32) > 0.5
    gp = jnp.where(top, gmass, dot(grest, vv, NT))
    gs = (prob * (gp - jnp.sum(prob * gp, axis=1, keepdims=True))).astype(BF)
    rw = jnp.where(top, 0.0, prob).astype(BF)
    gcen = dot(gs, jnp.where(mine, kv, zero)) / cnt
    gh, gl = split2(gcen)
    gg = jnp.concatenate([gh, gl], 1)
    gsT = jnp.transpose(gs)
    rwT = jnp.transpose(rw)
    kTh = kT[64 * h:64 * h + 64]
    for t in range(L // TJ):
        sl = pl.ds(t * TJ, TJ)
        st = dot(kaug[sl, :], qaug[...], NT)
        pr = jnp.exp(st)
        dp = dot(vaug[sl, :], gaug[...], NT)
        ds = (pr * dp).astype(BF)
        dv = dot(pr.astype(BF), gm) + dot(rwT[t * TJ:(t + 1) * TJ], grest)
        dk = dot(ds, qs) + dot(gsT[t * TJ:(t + 1) * TJ], cs)
        if h == 0:
            dv_o[sl, :] = dv
            dk_o[sl, :] = dk
        else:
            dv_o[sl, :] += dv
            dk_o[sl, :] += dk
        dqp = dot(kTh[:, t * TJ:(t + 1) * TJ], ds)
        if t == 0:
            dqt[64 * h:64 * h + 64, :] = dqp
        else:
            dqt[64 * h:64 * h + 64, :] += dqp
    dd = dot(jnp.where(ln < 100, s["mb"][hh], zero), gg)
    dd = dd[:, :128] + dd[:, 128:]
    if h == 0:
        dq_o[...] = dd
    else:
        dq_o[...] += dd


N2IN = ("act", "dg", "n2", "hid", "n1", "att", "qkv", "ex", "mb", "mt", "ns", "tm", "prob")


def k2_body(nb, custom, *refs):
    refs = list(refs)
    take = lambda n: [refs.pop(0) for _ in range(n)]
    ct, x, gr, w = take(4)
    ins = dict(zip(N2IN, take(len(N2IN))))
    tg, out_s, out_g = take(3)
    s = dict(zip(N2IN, take(len(N2IN))))
    names = ("aT", "ghs", "eb", "er", "gatt", "dqkv", "qaug", "kaug", "gaug", "vaug", "dqs", "dks", "dvs", "dqt", "gacc", "vb", "vr", "xs", "e3", "wg")
    b = dict(zip(names, take(len(names))))
    isem, wsem, xsem, es, ers, vs, vrs = take(7)
    aT, ghs, eb, er, gacc, wg = b["aT"], b["ghs"], b["eb"], b["er"], b["gacc"], b["wg"]
    s["gatt"] = b["gatt"]
    pc = Place(nb)
    loads = {n: pltpu.make_async_copy(ins[n], s[n], isem.at[i]) for i, n in enumerate(N2IN)}
    wl = {}
    for i, (k, a, e) in enumerate((("down", 8, 12), ("up", 4, 8), ("rest", 0, 4))):
        wl[k] = pltpu.make_async_copy(w.at[a:e], wg.at[a:e], wsem.at[i])
    half = L // 2
    xl = pltpu.make_async_copy(x.at[pl.ds(pl.multiple_of(pc.h * half, half), half)], b["xs"], xsem)
    wl["down"].start()
    for n in ("act", "dg"):
        loads[n].start()
    wl["up"].start()
    for n in ("n2", "hid", "att"):
        loads[n].start()
    wl["rest"].start()
    for n in N2IN:
        if n not in ("act", "dg", "n2", "hid", "att"):
            loads[n].start()
    xl.start()
    pc.barrier()
    if custom:
        gbuf, land, gland = refs[0], refs[1:6], refs[6:11]
        ss, rs, gss, grs = refs[11:15]
        S = Scatter(pc, wg, *land, ss, rs)
        Sg = Scatter(pc, gbuf, *gland, gss, grs)
        steps, gsteps = S.steps(out_s), Sg.steps(out_g)
        starts = list(range(9)) + [11, 14, 17]
        order = [8, 9, 10, 11, 4, 5, 6, 7, 3, 0, 1, 2]

        def tick(t):
            for i in range(len(steps) - 1, -1, -1):
                u = t - i
                if isinstance(u, int):
                    if u in starts:
                        steps[i](order[starts.index(u)])
                else:
                    ok = (u >= 0) & ((u <= 8) | ((u >= 11) & (u <= 17) & (lax.rem(u + 10, 3) == 0)))
                    part = jnp.where(u < 4, u + 8, jnp.where(u < 8, u, jnp.where(u == 8, 3, (u - 11) // 3)))
                    pl.when(ok)(lambda i=i, part=part: steps[i](part))
        nsteps = len(steps)
    else:
        tick = lambda t: None

    def put(p, left, right):
        v = dot(left, right).astype(BF)
        wg[p] = v.reshape(wg.shape[1:])

    def transpose_into(src):
        for i in range(L // RT):
            aT[:, i * RT:(i + 1) * RT] = jnp.transpose(src[i * RT:(i + 1) * RT, :])

    transpose_into(ct)
    wl["down"].wait()
    loads["act"].wait()
    loads["dg"].wait()
    act, dg, hid, n2 = s["act"], s["dg"], s["hid"], s["n2"]

    @pl.loop(0, 4)
    def _(q):
        @tiles(L // RT)
        def _(i):
            ga = dot(ct[rows_of(i), :], flat(wg, 8 + q))
            dg[q, rows_of(i), :] = (ga * dg[q, rows_of(i), :].astype(F32)).astype(BF)
        put(8 + q, aT[...], act[q])
        tick(q)

    wl["up"].wait()
    loads["n2"].wait()

    def send(i):
        return twin_copy(pc, eb.at[rows_of(i)], er.at[rows_of(i)], es.at[i], ers.at[i])

    @tiles(L // RT)
    def _(i):
        acc = dot(dg[0, rows_of(i), :], flat(wg, 4), NT)
        for q in range(1, 4):
            acc += dot(dg[q, rows_of(i), :], flat(wg, 4 + q), NT)
        eb[rows_of(i), :] = acc.astype(BF)
        send(i).start()

    transpose_into(n2)

    @pl.loop(0, 4)
    def _(q):
        put(4 + q, aT[...], dg[q])
        tick(4 + q)

    loads["hid"].wait()
    gacc[...] = jnp.zeros_like(gacc)
    nh = half // RT
    gat = n2

    @tiles(L // RT)
    def _(i):
        r = rows_of(i)
        send(i).wait_recv()
        gn = eb[r, :].astype(F32) + er[r, :].astype(F32)
        n, inv = norm_rows(hid[r, :])
        gacc[1:2, :] += jnp.sum(gn * n, axis=0, keepdims=True)
        a = gn * gr[1:2, :]
        back = (a - jnp.mean(a, axis=1, keepdims=True) - n * jnp.mean(a * n, axis=1, keepdims=True)) * inv
        gh = ct[r, :].astype(F32) + back
        gat[r, :] = gh.astype(BF)

        @pl.when((i >= pc.h * nh) & (i < pc.h * nh + nh))
        def _():
            ghs[rows_of(i - pc.h * nh), :] = gh

    wl["rest"].wait()
    loads["att"].wait()

    @tiles(L // RT)
    def _(i):
        b["gatt"][rows_of(i), :] = dot(gat[rows_of(i), :], flat(wg, 3)).astype(BF)

    transpose_into(gat)
    put(3, aT[...], s["att"][...])
    tick(8)
    loads["n1"].wait()
    transpose_into(s["n1"])
    for n in ("qkv", "ex", "mb", "mt", "ns", "tm", "prob"):
        loads[n].wait()
    nacc = hid
    dqkv = b["dqkv"]

    @pl.loop(0, 3)
    def _(p):
        for h in range(2):
            bwd_head(p, h, s, b["qaug"], b["kaug"], b["gaug"], b["vaug"], b["dqs"], b["dks"], b["dvs"], b["dqt"])
            if h == 0:
                tick(9 + 3 * p)
        dqkv[:, 0:128] = ((b["dqs"][...] + jnp.transpose(b["dqt"][...])) * 0.125).astype(BF)
        dqkv[:, 128:256] = b["dks"][...].astype(BF)
        dqkv[:, 256:384] = b["dvs"][...].astype(BF)
        tick(10 + 3 * p)

        @tiles(L // RT)
        def _(i):
            v = dot(dqkv[rows_of(i), :], flat(wg, p), NT)

            @pl.when(p == 0)
            def _():
                nacc[rows_of(i), :] = v

            @pl.when(p > 0)
            def _():
                nacc[rows_of(i), :] += v
        put(p, aT[...], dqkv[...])
        tick(11 + 3 * p)

    @tiles(L // RT)
    def _(i):
        send(i).wait_send()

    def send3(i):
        return twin_copy(pc, eb.at[rows_of(i)], b["e3"].at[rows_of(i)], es.at[4 + i], ers.at[4 + i])

    @tiles(nh)
    def _(i):
        eb[rows_of(i), :] = nacc[rows_of((1 - pc.h) * nh + i), :].astype(BF)
        send3(i).start()

    tick(18)
    xl.wait()

    @tiles(nh)
    def _(i):
        r = rows_of(i)
        send3(i).wait_recv()
        gn = nacc[rows_of(pc.h * nh + i), :].astype(BF).astype(F32) + b["e3"][r, :].astype(F32)
        n, inv = norm_rows(b["xs"][r, :].astype(F32))
        gacc[0:1, :] += jnp.sum(gn * n, axis=0, keepdims=True)
        a = gn * gr[0:1, :]
        back = (a - jnp.mean(a, axis=1, keepdims=True) - n * jnp.mean(a * n, axis=1, keepdims=True)) * inv
        tg[r, :] = ghs[r, :] + back

    b["vb"][...] = gacc[...]
    cv = twin_copy(pc, b["vb"], b["vr"], vs, vrs)
    cv.start()
    tick(19)
    cv.wait()
    one = gacc[0:1, :] + b["vr"][0:1, :]
    both = jnp.where(sub((8, 768)) == 0, jnp.broadcast_to(one, (8, 768)), gacc[...])
    if custom:
        wide = jnp.concatenate([both, jnp.zeros((120, 768), F32)], 0)
        gbuf[0] = jnp.transpose(wide).astype(BF).reshape(gbuf.shape[1:])
        for t in range(20, max(17, 20) + nsteps):
            tick(t)
            gsteps[t - 20](0)

        @pl.loop(0, 12)
        def _(p):
            S.drain(p)
        Sg.drain(0)
    else:
        c = pltpu.make_async_copy(wg, out_s, xsem)
        c.start()
        out_g[...] = both
        c.wait()

    @tiles(nh)
    def _(i):
        send3(i).wait_send()


def backward(nb, custom, ct, x, w, d):
    V = pl.BlockSpec(memory_space=pltpu.VMEM)
    A = pl.BlockSpec(memory_space=pl.ANY)
    nz = nb // 4
    dma = pltpu.SemaphoreType.DMA
    shapes = k1_shapes(None)
    out_shape = [jax.ShapeDtypeStruct((L // 2, 768), F32)]
    if custom:
        R = w.shape[3]
        out_shape += [jax.ShapeDtypeStruct((12, R, 384), F32), jax.ShapeDtypeStruct((1, R, 128), F32)]
        out_specs = [V, V, V]
    else:
        out_shape += [jax.ShapeDtypeStruct(w.shape, BF), jax.ShapeDtypeStruct((8, 768), F32)]
        out_specs = [V, A, V]
    vb = lambda *sh: pltpu.VMEM(sh, BF)
    vf = lambda *sh: pltpu.VMEM(sh, F32)
    scratch = [vm(shapes[n]) for n in N2IN] + [
        vb(768, L), vf(L // 2, 768), vb(L, 768), vb(L, 768), vb(L, 384), vb(L, 384), vb(L, 256), vb(L, 256), vb(L, 128), vb(L, 128),
        vf(L, 128), vf(L, 128), vf(L, 128), vf(128, L), vf(8, 768), vf(8, 768), vf(8, 768), vb(L // 2, 768), vb(L // 2, 768), pltpu.VMEM(w.shape, BF),
        dma((len(N2IN),)), dma((3,)), dma, dma((6,)), dma((6,)), dma, dma]
    if custom:
        ns = 4 + 2 * nz
        scratch += [vb(1, nz, 4, R, 128)] + [vb(12, nz, R, 384)] * 5 + [vb(1, nz, R, 128)] * 5 + [dma((12, ns)), dma((12, ns)), dma((1, ns)), dma((1, ns))]
    return pl.pallas_call(
        functools.partial(k2_body, nb, custom),
        out_shape=out_shape, in_specs=[V, A, V, A] + [A] * len(N2IN), out_specs=out_specs, scratch_shapes=scratch,
        compiler_params=pltpu.CompilerParams(collective_id=1, has_side_effects=True, vmem_limit_bytes=int(63.5 * (1 << 20))),
    )(ct, x, d["gr"], w, *[d[n] for n in N2IN])


def pack(q, o, u, d):
    R = q.shape[0]
    qp = q.reshape(R, 3, 3, 128).transpose(2, 0, 1, 3).reshape(3, R, 384)
    up = u.reshape(R, 4, 384).transpose(1, 0, 2)
    dn = d.T.reshape(R, 4, 384).transpose(1, 0, 2)
    return jnp.concatenate([qp, o.T[None], up, dn], 0)


def on_device(tokens, attn_gain, qkv_weight, out_weight, ffn_gain, up_weight, down_weight, cotangent, segment, cluster, top_keys):
    nb = lax.axis_size("batch")
    w = pack(qkv_weight, out_weight, up_weight, down_weight)
    R = w.shape[1]
    gw = jnp.pad(jnp.stack([attn_gain, ffn_gain], 1), ((0, 0), (0, 126)))
    custom = R % 16 == 0 and nb % 4 == 0
    if not custom:
        w = lax.all_gather(w, "batch", axis=1, tiled=True)
        gw = lax.all_gather(gw, "batch", axis=0, tiled=True)
    tk = top_keys[0]
    tt = jnp.pad(tk.transpose(0, 2, 1), ((0, 0), (0, 0), (0, 128 - tk.shape[1])), constant_values=-1)
    x, ct = tokens[0], cotangent[0]
    d, y, W = forward(nb, custom, x, w, gw, segment, cluster[0][:, None, :], tt)
    tg, S, gg = backward(nb, custom, ct, x, W, d)
    if custom:
        g1, g2 = gg[0, :, 0], gg[0, :, 1]
    else:
        S = lax.psum_scatter(S.astype(F32), "batch", scatter_dimension=1, tiled=True)
        g = lax.psum_scatter(gg, "batch", scatter_dimension=1, tiled=True)
        g1, g2 = g[0], g[1]
    cat = lambda a: a.transpose(1, 0, 2).reshape(R, -1)
    qg = S[0:3].reshape(3, R, 3, 128).transpose(1, 2, 0, 3).reshape(R, 3, 384)
    return y[None], tg[None], g1, qg, S[3].T, g2, cat(S[4:8]), cat(S[8:12]).T


def solution(mesh):
    in_specs = (P("batch", None, None), P("batch"), P("batch", None, "head"), P("head", "batch"), P("batch"), P("batch", "head"), P("head", "batch"), P("batch", None, None), P("batch", None), P("batch", "head", None), P("batch", "head", None, None))
    out_specs = (P("batch", "head", None), P("batch", "head", None), P("batch"), P("batch", None, "head"), P("head", "batch"), P("batch"), P("batch", "head"), P("head", "batch"))
    return jax.shard_map(on_device, mesh=mesh, in_specs=in_specs, out_specs=out_specs, check_vma=False)
```

```python
import functools

import jax
import jax.numpy as jnp
from jax import lax
from jax.experimental import pallas as pl
from jax.experimental.pallas import tpu as pltpu
from jax.sharding import PartitionSpec as P

F32=jnp.float32; BF=jnp.bfloat16
BIG=1e30
NT=(((1,),(1,)),((),()))
TN=(((0,),(0,)),((),()))
NN=(((1,),(0,)),((),()))
def dot(a,b,dims=NN): return lax.dot_general(a,b,dims,preferred_element_type=F32)
def split3(x):
    a=x.astype(BF); r=x-a.astype(F32); b=r.astype(BF); c=(r-b.astype(F32)).astype(BF)
    return a,b,c
def split2(x):
    a=x.astype(BF); return a,(x-a.astype(F32)).astype(BF)
L=1024
def lane(shape): return lax.broadcasted_iota(jnp.int32,shape,len(shape)-1)
def sub(shape): return lax.broadcasted_iota(jnp.int32,shape,len(shape)-2)

def build_masks(own_row, topT):
    mt=jnp.where(own_row==sub((128,L)),1.0,0.0).astype(BF)
    m=jnp.transpose(mt)
    hi=lax.shift_right_arithmetic(topT,5); bit=lax.shift_left(jnp.int32(1),topT&31)
    words=L//32
    a_iota=sub((words,128))
    w=jnp.zeros((words,128),jnp.int32)
    for t in range(topT.shape[0]):
        w=w|jnp.where(hi[t:t+1]==a_iota,bit[t:t+1],0)
    b_iota=sub((32,128)); ln=lane((32,128))
    extra=(ln>=100)&(ln<103)
    ns=[]
    for a in range(words):
        b=(lax.shift_right_logical(jnp.broadcast_to(w[a:a+1],(32,128)),b_iota)&1)
        ns.append(jnp.where(extra,-1.0,jnp.where(b==1,0.0,-BIG)))
    n=jnp.concatenate(ns,0).astype(BF)
    return m,n


TQ = 256
TJ = 256
MESH=pl.DeviceIdType.MESH


def NOP(p): pass
class Place:
    def __init__(self, nb):
        self.nz=nb//4
        self.b=lax.axis_index("batch"); self.h=lax.axis_index("head")
        self.z=self.b//4; self.r=lax.rem(self.b,4)
        even=lax.rem(self.r,2)==0
        self.rx=jnp.where(even,self.r+1,self.r-1)
        self.ry=jnp.where(self.r<2,self.r+2,self.r-2)
        self.rd=3-self.r
        self.X=(self.z*4+self.rx,self.h); self.Y=(self.z*4+self.ry,self.h)
        self.up=(self.b+4,self.h); self.dn=(self.b-4,self.h); self.twin=(self.b,1-self.h)
    def barrier(self):
        bar=pltpu.get_barrier_semaphore()
        for d in (self.X,self.Y,self.twin):
            pl.semaphore_signal(bar,inc=1,device_id=d,device_id_type=MESH)
        @pl.when(self.z<self.nz-1)
        def _(): pl.semaphore_signal(bar,inc=1,device_id=self.up,device_id_type=MESH)
        @pl.when(self.z>0)
        def _(): pl.semaphore_signal(bar,inc=1,device_id=self.dn,device_id_type=MESH)
        lines=jnp.where(self.z<self.nz-1,1,0)+jnp.where(self.z>0,1,0)
        pl.semaphore_wait(bar,3+lines)

def rc(src,dst,ss,rs,dev):
    return pltpu.make_async_remote_copy(src_ref=src,dst_ref=dst,send_sem=ss,recv_sem=rs,device_id=dev,device_id_type=MESH)

class Gather:
    def __init__(self, pc, g, ss, rs):
        self.pc=pc; self.g=g; self.ss=ss; self.rs=rs; self.n=2*(pc.nz-1)
    def cz(self,p,zz,k,dev):
        s=self.g.at[p,zz,self.pc.r]
        return rc(s,s,self.ss.at[p,k],self.rs.at[p,k],dev)
    def z0(self,p):
        c=self.pc
        @pl.when(c.z<c.nz-1)
        def _(): self.cz(p,c.z,0,c.up).start()
        @pl.when(c.z>0)
        def _(): self.cz(p,c.z,1,c.dn).start()
    def zk(self,p,d):
        c=self.pc
        @pl.when(c.z-d>=0)
        def _():
            self.cz(p,c.z-d,2*(d-1),c.up).wait_recv()
        if d<c.nz-1:
            @pl.when((c.z-d>=0)&(c.z<c.nz-1))
            def _(): self.cz(p,c.z-d,2*d,c.up).start()
        @pl.when(c.z+d<c.nz)
        def _():
            self.cz(p,c.z+d,2*(d-1)+1,c.dn).wait_recv()
        if d<c.nz-1:
            @pl.when((c.z+d<c.nz)&(c.z>0))
            def _(): self.cz(p,c.z+d,2*d+1,c.dn).start()
    def cb(self,p,r,k,dev):
        s=self.g.at[p,:,r]
        return rc(s,s,self.ss.at[p,self.n+k],self.rs.at[p,self.n+k],dev)
    def ch(self,p,r,lo,k,dev):
        h=self.pc.nz//2
        s=self.g.at[p,pl.ds(0,h),r] if lo else self.g.at[p,pl.ds(h,self.pc.nz-h),r]
        return rc(s,s,self.ss.at[p,self.n+k],self.rs.at[p,self.n+k],dev)
    def x0(self,p):
        c=self.pc
        self.cb(p,c.r,0,c.X).start(); self.cb(p,c.r,1,c.Y).start()
    def x1(self,p):
        c=self.pc
        self.cb(p,c.rx,0,c.X).wait_recv()
        self.ch(p,c.rx,True,2,c.Y).start()
        self.cb(p,c.ry,1,c.Y).wait_recv()
        self.ch(p,c.ry,False,3,c.X).start()
    def x2(self,p):
        c=self.pc
        self.ch(p,c.rd,True,2,c.Y).wait_recv()
        self.ch(p,c.rd,False,3,c.X).wait_recv()
    def drain(self,p):
        c=self.pc
        for d in range(c.nz-1):
            @pl.when((c.z-d>=0)&(c.z<c.nz-1))
            def _(): self.cz(p,c.z-d,2*d,c.up).wait_send()
            @pl.when((c.z+d<c.nz)&(c.z>0))
            def _(): self.cz(p,c.z+d,2*d+1,c.dn).wait_send()
        self.cb(p,c.r,0,c.X).wait_send(); self.cb(p,c.r,1,c.Y).wait_send()
        self.ch(p,c.rx,True,2,c.Y).wait_send(); self.ch(p,c.ry,False,3,c.X).wait_send()
    def steps(self):
        nz=self.pc.nz
        def last(p):
            self.zk(p,nz-1); self.x0(p)
        return [self.z0]+[functools.partial(lambda d,p:self.zk(p,d),d) for d in range(1,nz-1)]+[last]+[NOP]+[self.x1]+[NOP]+[self.x2]

class Scatter:
    def __init__(self, pc, g, d, rx, ry, ru, rd, ss, rs, slot=lambda p: p):
        self.pc=pc;self.g=g;self.d=d;self.bx=rx;self.by=ry;self.bu=ru;self.bd=rd;self.ss=ss;self.rs=rs
        self.h=pc.nz//2; self.slot=slot
    def half(self,p,r,lo):
        h=self.h; n=self.pc.nz
        return (self.g.at[p,pl.ds(0,h),r],self.d.at[self.slot(p),pl.ds(0,h)]) if lo else (self.g.at[p,pl.ds(h,n-h),r],self.d.at[self.slot(p),pl.ds(h,n-h)])
    def c0(self,p,lo):
        s,t=self.half(p,self.pc.rd,lo); k=0 if lo else 1
        return rc(s,t,self.ss.at[self.slot(p),k],self.rs.at[self.slot(p),k],self.pc.X if lo else self.pc.Y)
    def c1(self,p,x):
        c=self.pc
        return rc(self.g.at[p,:,c.rx if x else c.ry],(self.bx if x else self.by).at[self.slot(p)],self.ss.at[self.slot(p),2 if x else 3],self.rs.at[self.slot(p),2 if x else 3],c.X if x else c.Y)
    def cu(self,p,zz,up):
        c=self.pc; k=4+zz if up else 4+c.nz+zz
        return rc(self.g.at[p,zz,c.r],(self.bu if up else self.bd).at[self.slot(p),zz],self.ss.at[self.slot(p),k],self.rs.at[self.slot(p),k],c.up if up else c.dn)
    def add(self,dst,*srcs):
        v=dst[...].astype(F32)
        for s in srcs: v=v+s[...].astype(F32)
        dst[...]=v.astype(BF)
    def s0(self,p):
        self.c0(p,True).start(); self.c0(p,False).start()
    def s1(self,p):
        c=self.pc;h=self.h;n=c.nz
        self.c0(p,True).wait_recv()
        self.add(self.g.at[p,pl.ds(0,h),c.ry],self.d.at[self.slot(p),pl.ds(0,h)])
        self.c1(p,False).start()
        self.c0(p,False).wait_recv()
        self.add(self.g.at[p,pl.ds(h,n-h),c.rx],self.d.at[self.slot(p),pl.ds(h,n-h)])
        self.c1(p,True).start()
    def s2(self,p):
        c=self.pc
        self.c1(p,True).wait_recv(); self.c1(p,False).wait_recv()
        self.add(self.g.at[p,:,c.r],self.bx.at[self.slot(p)],self.by.at[self.slot(p)])
        self.zk(p,0)
    def zk(self,p,k):
        c=self.pc; nz=c.nz
        @pl.when(c.z==k)
        def _():
            for zz in range(nz-1,k,-1):
                if k>0:
                    self.cu(p,zz,True).wait_recv()
                    self.add(self.g.at[p,zz,c.r],self.bu.at[self.slot(p),zz])
                self.cu(p,zz,True).start()
        @pl.when(c.z==nz-1-k)
        def _():
            for zz in range(0,nz-1-k):
                if k>0:
                    self.cu(p,zz,False).wait_recv()
                    self.add(self.g.at[p,zz,c.r],self.bd.at[self.slot(p),zz])
                self.cu(p,zz,False).start()
    def fin(self,p,tot,place=None):
        c=self.pc
        tot[...]=self.g[p,c.z,c.r].astype(F32)
        @pl.when(c.z>0)
        def _():
            self.cu(p,c.z,True).wait_recv()
            tot[...]+=self.bu[self.slot(p),c.z].astype(F32)
        @pl.when(c.z<c.nz-1)
        def _():
            self.cu(p,c.z,False).wait_recv()
            tot[...]+=self.bd[self.slot(p),c.z].astype(F32)
        if place is not None: place(p)
    def drain(self,p):
        c=self.pc; nz=c.nz
        self.c0(p,True).wait_send(); self.c0(p,False).wait_send()
        self.c1(p,True).wait_send(); self.c1(p,False).wait_send()
        for zz in range(nz):
            @pl.when(zz>c.z)
            def _(): self.cu(p,zz,True).wait_send()
            @pl.when(zz<c.z)
            def _(): self.cu(p,zz,False).wait_send()
    def lines(self):
        return [functools.partial(lambda k,p:self.zk(p,k),k) for k in range(1,self.pc.nz-1)]
    def steps(self,place,tot):
        return [self.s0,NOP,self.s1,NOP,self.s2]+self.lines()+[lambda p:self.fin(p,tot,place)]
    def tight(self,out):
        return [self.s0,self.s1,self.s2]+self.lines()+[lambda p:self.fin(p,out.at[0])]


EPS = 1e-5
RT = 256


def pick(static, cond, body):
    if isinstance(cond, (bool, int)):
        if cond:
            body()
    else:
        pl.when(cond)(body)


def norm_rows(values):
    mean = jnp.mean(values, axis=1, keepdims=True)
    centred = values - mean
    inverse = lax.rsqrt(jnp.mean(centred * centred, axis=1, keepdims=True) + EPS)
    return centred * inverse, inverse


def gelu_both(u):
    c = 0.7978845608028654
    u2 = u * u
    t = jnp.tanh(c * u * (1.0 + 0.044715 * u2))
    half = 0.5 + 0.5 * t
    act = u * half
    grad = half + (0.5 * c) * u * (1.0 - t * t) * (1.0 + (3 * 0.044715) * u2)
    return act, grad


def flat(ref, p):
    v = ref[p]
    return v.reshape(-1, v.shape[-1])


def tiles(n):
    return lambda f: pl.loop(0, n)(f)


def rows_of(i, n=RT):
    return pl.ds(pl.multiple_of(i * n, n), n)


def twin_copy(pc, src, dst, ss, rs):
    return rc(src, dst, ss, rs, pc.twin)


def members(cl, hh):
    return jnp.where(cl[hh] == sub((128, L)), 1.0, 0.0).astype(BF)


def fwd_head(p, h, qkv, mb, cl, n_s, seg, qaug, kaug, att, ex, prob_o):
    odd = h == 1
    hh = 2 * p + h
    q = qkv[p, :, 0:128]
    k = qkv[p, :, 128:256]
    v = qkv[p, :, 256:384]
    ln = lane((L, 128))
    mine = (ln >= 64) if odd else (ln < 64)
    lc = lane((128, 128))
    minec = (lc >= 64) if odd else (lc < 64)
    zero = jnp.zeros((), BF)
    qm = jnp.where(mine, q, zero)
    vaug = jnp.where(mine, v, jnp.ones((), BF))
    mt = members(cl, hh)
    top = jnp.transpose(n_s[hh]).astype(F32) == 0.0
    cnt = jnp.maximum(jnp.sum(mt.astype(F32), axis=1, keepdims=True), 1.0)
    cen = (dot(mt, qm) / cnt).astype(BF)
    cs = (cen.astype(F32) * 0.125).astype(BF)
    s = dot(cs, k, NT)
    cm = lax.rem(sub((128, 1)), jnp.int32(10))
    s = jnp.where(seg[...] == cm, s, -BIG)
    mx = jnp.max(s, axis=1, keepdims=True)
    e = jnp.exp(s - mx)
    prob = e / jnp.sum(e, axis=1, keepdims=True)
    mass = jnp.sum(jnp.where(top, prob, 0.0), axis=1, keepdims=True)
    prob_o[hh] = jnp.where(top, -prob, prob).astype(BF)
    rest = dot(jnp.where(top, 0.0, prob).astype(BF), v)
    rh, rl = split2(jnp.where(minec, rest, jnp.broadcast_to(mass, (128, 128))))
    rr = jnp.concatenate([rh, rl], 1)
    qaug[:, :128] = (qm.astype(F32) * 0.125).astype(BF)
    qaug[:, 128:] = mb[hh]
    kaug[:, :128] = k
    kaug[:, 128:] = n_s[hh]
    lt = lane((TQ, 128))
    minet = (lt >= 64) if odd else (lt < 64)
    cols = pl.ds(pl.multiple_of(p * 128, 128), 128)
    for t in range(L // TQ):
        sl = pl.ds(t * TQ, TQ)
        sc = dot(qaug[sl, :], kaug[...], NT)
        mm = jnp.max(sc, axis=1, keepdims=True)
        pr = jnp.exp(sc - mm).astype(BF)
        o = dot(pr, vaug)
        mt_ = qaug[sl, 128:]
        ee = dot(mt_, rr)
        ee = ee[:, :128] + ee[:, 128:]
        osw = pltpu.roll(o, 64, 1)
        esw = pltpu.roll(ee, 64, 1)
        exact = o / osw
        a = exact * esw + ee
        tot = jnp.where(minet, osw, o)
        ms = jnp.where(minet, esw, ee)
        lse = mm + jnp.log(tot) - jnp.log(jnp.maximum(ms, 1e-37))
        h3, m3, l3 = split3(lse)
        mb[hh, sl, :] = jnp.where(lt == 100, h3.astype(F32), jnp.where(lt == 101, m3.astype(F32), jnp.where(lt == 102, l3.astype(F32), mt_.astype(F32)))).astype(BF)
        if odd:
            att[sl, cols] = jnp.where(lt < 64, att[sl, cols], a.astype(BF))
            ex[sl, cols] = jnp.where(lt < 64, ex[sl, cols], exact.astype(BF))
        else:
            att[sl, cols] = a.astype(BF)
            ex[sl, cols] = exact.astype(BF)


def as_column(row):
    n = row.shape[1]
    eye = sub((n, n)) == lane((n, n))
    return jnp.sum(jnp.where(eye, row.astype(F32), 0.0), axis=1, keepdims=True)


def fill_own(pc, g, gg, q3, oT, upw, dT, ga, gf):
    for p in range(3):
        for i in range(3):
            g[p, pc.z, pc.r, :, i * 128:(i + 1) * 128] = q3[i, :, p * 128:(p + 1) * 128]
    g[3, pc.z, pc.r] = oT[...]
    for q in range(4):
        g[4 + q, pc.z, pc.r] = upw[:, q * 384:(q + 1) * 384]
        g[8 + q, pc.z, pc.r] = dT[:, q * 384:(q + 1) * 384]
    R = oT.shape[0]
    ln = lane((R, 128))
    gg[0, pc.z, pc.r] = jnp.where(ln == 0, as_column(ga[...]), jnp.where(ln == 1, as_column(gf[...]), 0.0)).astype(BF)


def bwd_head(p, h, cl, s, qaug, kaug, gaug, vaug, dq_o, dk_o, dv_o, dqt):
    qkv, g, ex = s["qkv"], s["gatt"], s["ex"]
    hh = 2 * p + h
    cols = pl.ds(pl.multiple_of(p * 128, 128), 128)
    qv = qkv[p, :, 0:128]
    kv = qkv[p, :, 128:256]
    vv = qkv[p, :, 256:384]
    gv = g[:, cols]
    ln = lane((L, 128))
    zero = jnp.zeros((), BF)
    lc = lane((128, 128))
    kT = jnp.transpose(kv)
    prod = gv.astype(F32) * ex[:, cols].astype(F32)
    mine = (ln >= 64) if h else (ln < 64)
    minec = (lc >= 64) if h else (lc < 64)
    o = 0 if h else 64
    r = jnp.sum(jnp.where(mine, prod, 0.0), axis=1, keepdims=True)
    h3, m3, l3 = split3(r)
    gm = jnp.where(mine, gv, zero)
    ga = jnp.where(ln == o, h3.astype(F32), jnp.where(ln == o + 1, m3.astype(F32), jnp.where(ln == o + 2, l3.astype(F32), gm.astype(F32)))).astype(BF)
    gaug[...] = ga
    vaug[...] = jnp.where(mine, vv, jnp.where((ln >= o) & (ln < o + 3), jnp.full((), -1.0, BF), zero))
    qm = jnp.where(mine, qv, zero)
    qs = (qm.astype(F32) * 0.125).astype(BF)
    qaug[:, :128] = qs
    qaug[:, 128:] = s["mb"][hh]
    kaug[:, :128] = kv
    kaug[:, 128:] = s["ns"][hh]
    mt = members(cl, hh)
    signed = s["prob"][hh].astype(F32)
    top = signed < 0.0
    prob = jnp.abs(signed)
    cnt = jnp.maximum(jnp.sum(mt.astype(F32), axis=1, keepdims=True), 1.0)
    cen = (dot(mt, qm) / cnt).astype(BF)
    cs = (cen.astype(F32) * 0.125).astype(BF)
    gr = dot(mt, ga)
    gmass = jnp.sum(jnp.where((lc >= o) & (lc < o + 3), gr, 0.0), axis=1, keepdims=True)
    grest = jnp.where(minec, gr, 0.0).astype(BF)
    gp = jnp.where(top, gmass, dot(grest, vv, NT))
    gs = (prob * (gp - jnp.sum(prob * gp, axis=1, keepdims=True))).astype(BF)
    rw = jnp.where(top, 0.0, prob).astype(BF)
    gcen = dot(gs, jnp.where(mine, kv, zero)) / cnt
    gh, gl = split2(gcen)
    gg = jnp.concatenate([gh, gl], 1)
    gsT = jnp.transpose(gs)
    rwT = jnp.transpose(rw)
    kTh = kT[64 * h:64 * h + 64]
    for t in range(L // TJ):
        sl = pl.ds(t * TJ, TJ)
        st = dot(kaug[sl, :], qaug[...], NT)
        pr = jnp.exp(st)
        dp = dot(vaug[sl, :], gaug[...], NT)
        ds = (pr * dp).astype(BF)
        dv = dot(pr.astype(BF), gm) + dot(rwT[t * TJ:(t + 1) * TJ], grest)
        dk = dot(ds, qs) + dot(gsT[t * TJ:(t + 1) * TJ], cs)
        if h == 0:
            dv_o[sl, :] = dv
            dk_o[sl, :] = dk
        else:
            dv_o[sl, :] += dv
            dk_o[sl, :] += dk
        dqp = dot(kTh[:, t * TJ:(t + 1) * TJ], ds)
        if t == 0:
            dqt[64 * h:64 * h + 64, :] = dqp
        else:
            dqt[64 * h:64 * h + 64, :] += dqp
    dd = dot(jnp.where(ln < 100, s["mb"][hh], zero), gg)
    dd = dd[:, :128] + dd[:, 128:]
    if h == 0:
        dq_o[...] = dd
    else:
        dq_o[...] += dd


def place_sum(p, tot, outs):
    qg, og, ug, dg = outs

    def pair(p):
        for i in range(3):
            qg[i, :, pl.ds(pl.multiple_of(p * 128, 128), 128)] = tot[:, i * 128:(i + 1) * 128]

    def wide(ref, q):
        ref[:, pl.ds(pl.multiple_of(q * 384, 128), 384)] = tot[...]

    pick(None, p < 3, lambda: pair(p))
    pick(None, p == 3, lambda: og.__setitem__(..., tot[...]))
    pick(None, (3 < p < 8) if isinstance(p, int) else (p > 3) & (p < 8), lambda: wide(ug, p - 4))
    pick(None, p >= 12, lambda: wide(dg, p - 12))


def finish_body(*refs):
    ins, gg, outs, (g1, g2), bufs, (si, so) = refs[:6], refs[6], refs[7:13], refs[13:15], refs[15:21], refs[21:]
    ci = [pltpu.make_async_copy(a, b, si.at[i]) for i, (a, b) in enumerate(zip(ins, bufs))]
    co = [pltpu.make_async_copy(a, b, so.at[i]) for i, (a, b) in enumerate(zip(bufs, outs))]
    for c in ci:
        c.start()
    R = gg.shape[1]
    eye = sub((R, R)) == lane((R, R))
    for i, g in enumerate((g1, g2)):
        g[...] = jnp.sum(jnp.where(eye, gg[0, :, i:i + 1], 0.0), axis=0, keepdims=True)
    for a, b in zip(ci, co):
        a.wait()
        b.start()
    for c in co:
        c.wait()


def finish(*arrays):
    V = pl.BlockSpec(memory_space=pltpu.VMEM)
    A = pl.BlockSpec(memory_space=pl.ANY)
    R = arrays[6].shape[1]
    dma = pltpu.SemaphoreType.DMA
    return pl.pallas_call(
        finish_body,
        out_shape=[jax.ShapeDtypeStruct(a.shape, a.dtype) for a in arrays[:6]] + [jax.ShapeDtypeStruct((1, R), F32)] * 2,
        in_specs=[A] * 6 + [V], out_specs=[A] * 6 + [V] * 2,
        scratch_shapes=[pltpu.VMEM(a.shape, a.dtype) for a in arrays[:6]] + [dma((6,)), dma((6,))],
        compiler_params=pltpu.CompilerParams(vmem_limit_bytes=60 << 20),
    )(*arrays)


def scratch_shapes(custom, nz, R):
    f = lambda *s: (s, F32)
    b = lambda *s: (s, BF)
    wide = (16, nz, 4, R, 384) if custom else (16, 768, 384)
    return {
        "gr": f(8, 768), "n1": b(L, 768), "qkv": b(3, L, 384), "att": b(L, 384), "ex": b(L, 384), "mb": b(6, L, 128),
        "ns": b(6, L, 128), "prob": b(6, 128, L), "hid": f(L, 768), "n2": b(L, 768), "act": b(4, L, 384), "dg": b(4, L, 384),
        "aT": b(768, L), "ghs": f(L // 2, 768), "eb": b(L, 768), "er": b(L, 768), "fr": b(L // 2, 768), "gatt": b(L, 384),
        "dqkv": b(L, 384), "qaug": b(L, 256), "kaug": b(L, 256), "gaug": b(L, 128), "vaug": b(L, 128),
        "dqs": f(L, 128), "dks": f(L, 128), "dvs": f(L, 128), "dqt": f(128, L), "gacc": f(8, 768), "vb": f(8, 768), "vr": f(8, 768),
        "wg": b(*wide),
    }


def layer_body(nb, custom, names, *refs):
    refs = list(refs)
    take = lambda n: [refs.pop(0) for _ in range(n)]
    x, ct, seg, cl, tt = take(5)
    own = take(6 if custom else 2)
    y, tg, out_g = take(3)
    out_s = take(4) if custom else take(1)[0]
    s = dict(zip(names, take(len(names))))
    tpad, es, ers, vs, vrs = take(5)
    pc = Place(nb)
    wg, hid, n1, n2, qkv, att, ex, act, dg = (s[n] for n in ("wg", "hid", "n1", "n2", "qkv", "att", "ex", "act", "dg"))
    aT, eb, er, fr, gr, gacc = (s[n] for n in ("aT", "eb", "er", "fr", "gr", "gacc"))
    half, nh, nt = L // 2, L // 2 // RT, L // RT

    if custom:
        gg, tot, gbuf, ss, rs, gss, grs, ss2, rs2, gss2, grs2 = take(11)
        land, gland = take(5), take(5)
        G, Gg = Gather(pc, wg, ss, rs), Gather(pc, gg, gss, grs)
        S = Scatter(pc, wg, *land, ss2, rs2, slot=lambda p: p - 4 if isinstance(p, int) and p >= 12 else p if isinstance(p, int) else jnp.where(p >= 12, p - 4, p))
        Sg = Scatter(pc, gbuf, *gland, gss2, grs2)
        m = pc.nz - 1
        line = [(d, functools.partial(lambda d, p: G.zk(p, d), d), 0, 12) for d in range(1, m)]

        def last(p):
            G.zk(p, m)
            G.x0(p)
        gather = [(m + 3, G.x2, 3, 12), (m + 2, G.x2, 0, 3), (m + 2, G.x1, 3, 12), (m + 1, G.x1, 0, 3), (m, last, 0, 12)] + line[::-1] + [(0, G.z0, 0, 12)]
        gsteps = [Gg.z0] + [functools.partial(lambda d: Gg.zk(0, d), d) for d in range(1, m)] + [None, Gg.x1, Gg.x2]
        ssteps = S.steps(lambda p: place_sum(p, tot, out_s), tot)
        tails = Sg.tight(out_g)
        starts = {14: 12, 15: 13, 16: 14, 17: 15, 19: 4, 20: 5, 21: 6, 22: 7, 23: 3, 24: 0, 26: 1, 28: 2}

        def tick(t, span=None):
            fixed = isinstance(t, int)
            ts = [t] if fixed else list(range(*span))
            for i in range(len(ssteps) - 1, -1, -1):
                hits = [u - i for u in ts if u - i in starts]
                if not hits or ssteps[i] is NOP:
                    continue
                if fixed:
                    ssteps[i](starts[hits[0]])
                    continue
                u = t - i
                ok = functools.reduce(jnp.logical_or, [u == k for k in hits])
                part = functools.reduce(lambda a, k: jnp.where(u == k, starts[k], a), hits, 0)
                pl.when(ok)(lambda i=i, part=part: ssteps[i](part))
            for off, fn, lo, hi in gather:
                if not any(lo <= u - off < hi for u in ts):
                    continue
                p = t - off
                pick(None, True if fixed else (p >= lo) & (p < hi), lambda fn=fn, p=p: fn(p))
            if fixed and t < len(gsteps):
                if t == m:
                    Gg.zk(0, m)
                    Gg.x0(0)
                elif t == 0:
                    gsteps[0](0)
                elif t < m:
                    gsteps[t]()
                else:
                    gsteps[t](0)
    else:
        tick = lambda t, span=None: None

    tpad[...] = jnp.full_like(tpad, -1)
    pc.barrier()
    if custom:
        fill_own(pc, wg, gg, *own)
    tick(0)

    @tiles(nt)
    def _(i):
        hid[rows_of(i), :] = norm_rows(x[rows_of(i), :].astype(F32))[0]

    tick(1)

    def mask(h):
        tpad[:, 0:tt.shape[2]] = tt[h]
        a, n = build_masks(cl[h], tpad[...])
        s["mb"][h], s["ns"][h] = a, n

    def transpose_into(src):
        for i in range(nt):
            aT[:, i * RT:(i + 1) * RT] = jnp.transpose(src[i * RT:(i + 1) * RT, :])

    def put(p, left, right):
        wg[p] = dot(left, right).astype(BF).reshape(wg.shape[1:])

    pl.loop(0, 2)(mask)
    tick(2)
    pl.loop(2, 4)(mask)
    tick(3)
    pl.loop(4, 6)(mask)
    transpose_into(ct)
    tick(4)
    tick(5)
    if custom:
        gains = gg[0].reshape(768, 128)
    else:
        c = pltpu.make_async_copy(own[0], wg.at[0:12], vs)
        c.start()
        c.wait()
        gains = own[1][...]
    gr[...] = jnp.transpose(gains.astype(F32))[0:8]

    @tiles(nt)
    def _(i):
        n1[rows_of(i), :] = (hid[rows_of(i), :] * gr[0:1, :]).astype(BF)

    @pl.loop(0, 3)
    def _(p):
        @tiles(nt)
        def _(i):
            qkv[p, rows_of(i), :] = dot(n1[rows_of(i), :], flat(wg, p)).astype(BF)
        for h in range(2):
            tick(6 + 2 * p + h, (6 + h, 12, 2))
            fwd_head(p, h, qkv, s["mb"], cl, s["ns"], seg, s["qaug"], s["kaug"], att, ex, s["prob"])

    def send(k, src, dst, i):
        return twin_copy(pc, src.at[rows_of(i)], dst.at[rows_of(i)], es.at[k + i], ers.at[k + i])

    @tiles(nt)
    def _(i):
        eb[rows_of(i), :] = dot(att[rows_of(i), :], flat(wg, 3), NT).astype(BF)
        send(0, eb, er, i).start()

    tick(12)

    @tiles(nt)
    def _(i):
        r = rows_of(i)
        send(0, eb, er, i).wait()
        hv = x[r, :].astype(F32) + (eb[r, :].astype(F32) + er[r, :].astype(F32))
        hid[r, :] = hv
        n2[r, :] = (norm_rows(hv)[0] * gr[1:2, :]).astype(BF)

    def up(q):
        @tiles(nt)
        def _(i):
            a, d = gelu_both(dot(n2[rows_of(i), :], flat(wg, 4 + q)))
            act[q, rows_of(i), :] = a.astype(BF)
            dg[q, rows_of(i), :] = d.astype(BF)

    pl.loop(0, 2)(up)
    tick(13)
    pl.loop(2, 4)(up)

    def down_grad(q):
        put(12 + q, aT[...], act[q])

    pl.loop(0, 2)(down_grad)
    tick(14)
    pl.loop(2, 4)(down_grad)
    tick(15)
    transpose_into(n2)
    tick(16)
    tick(17)

    def part(i):
        acc = dot(act[0, rows_of(i), :], flat(wg, 8), NT)
        for q in range(1, 4):
            acc += dot(act[q, rows_of(i), :], flat(wg, 8 + q), NT)
        return acc

    @tiles(nh)
    def _(i):
        eb[rows_of(i), :] = part((1 - pc.h) * nh + i).astype(BF)
        send(4, eb, fr, i).start()

    @pl.loop(0, 4)
    def _(q):
        @tiles(nt)
        def _(i):
            ga = dot(ct[rows_of(i), :], flat(wg, 8 + q))
            dg[q, rows_of(i), :] = (ga * dg[q, rows_of(i), :].astype(F32)).astype(BF)

    @tiles(nh)
    def _(i):
        acc = part(pc.h * nh + i).astype(BF).astype(F32)
        send(4, eb, fr, i).wait()
        y[rows_of(i), :] = (hid[rows_of(pc.h * nh + i), :] + (acc + fr[rows_of(i), :].astype(F32))).astype(BF)

    tick(18)
    if custom:
        @pl.loop(0, 12)
        def _(p):
            G.drain(p)
        Gg.drain(0)

    @tiles(nt)
    def _(i):
        acc = dot(dg[0, rows_of(i), :], flat(wg, 4), NT)
        for q in range(1, 4):
            acc += dot(dg[q, rows_of(i), :], flat(wg, 4 + q), NT)
        eb[rows_of(i), :] = acc.astype(BF)
        send(6, eb, er, i).start()

    def up_grad(q):
        put(4 + q, aT[...], dg[q])

    pl.loop(0, 2)(up_grad)
    tick(19)
    pl.loop(2, 4)(up_grad)
    gacc[...] = jnp.zeros_like(gacc)
    gat = n2

    @tiles(nt)
    def _(i):
        r = rows_of(i)
        send(6, eb, er, i).wait()
        gn = eb[r, :].astype(F32) + er[r, :].astype(F32)
        n, inv = norm_rows(hid[r, :])
        gacc[1:2, :] += jnp.sum(gn * n, axis=0, keepdims=True)
        a = gn * gr[1:2, :]
        back = (a - jnp.mean(a, axis=1, keepdims=True) - n * jnp.mean(a * n, axis=1, keepdims=True)) * inv
        gh = ct[r, :].astype(F32) + back
        gat[r, :] = gh.astype(BF)

        @pl.when((i >= pc.h * nh) & (i < pc.h * nh + nh))
        def _():
            s["ghs"][rows_of(i - pc.h * nh), :] = gh

    tick(20)

    @tiles(nt)
    def _(i):
        s["gatt"][rows_of(i), :] = dot(gat[rows_of(i), :], flat(wg, 3)).astype(BF)

    transpose_into(gat)
    put(3, aT[...], att[...])
    tick(21)
    transpose_into(n1)
    tick(22)
    nacc = hid
    dqkv = s["dqkv"]

    @pl.loop(0, 3)
    def _(p):
        bwd_head(p, 0, cl, s, s["qaug"], s["kaug"], s["gaug"], s["vaug"], s["dqs"], s["dks"], s["dvs"], s["dqt"])
        tick(23 + 2 * p, (23, 29, 2))
        bwd_head(p, 1, cl, s, s["qaug"], s["kaug"], s["gaug"], s["vaug"], s["dqs"], s["dks"], s["dvs"], s["dqt"])
        dqkv[:, 0:128] = ((s["dqs"][...] + jnp.transpose(s["dqt"][...])) * 0.125).astype(BF)
        dqkv[:, 128:256] = s["dks"][...].astype(BF)
        dqkv[:, 256:384] = s["dvs"][...].astype(BF)

        @tiles(nt)
        def _(i):
            v = dot(dqkv[rows_of(i), :], flat(wg, p), NT)

            @pl.when(p == 0)
            def _():
                nacc[rows_of(i), :] = v

            @pl.when(p > 0)
            def _():
                nacc[rows_of(i), :] += v
        put(p, aT[...], dqkv[...])
        tick(24 + 2 * p, (24, 30, 2))

    @tiles(nh)
    def _(i):
        eb[rows_of(i), :] = nacc[rows_of((1 - pc.h) * nh + i), :].astype(BF)
        send(10, eb, fr, i).start()

    tick(29)

    @tiles(nh)
    def _(i):
        r = rows_of(i)
        send(10, eb, fr, i).wait()
        gn = nacc[rows_of(pc.h * nh + i), :].astype(BF).astype(F32) + fr[r, :].astype(F32)
        n, inv = norm_rows(x[rows_of(pc.h * nh + i), :].astype(F32))
        gacc[0:1, :] += jnp.sum(gn * n, axis=0, keepdims=True)
        a = gn * gr[0:1, :]
        back = (a - jnp.mean(a, axis=1, keepdims=True) - n * jnp.mean(a * n, axis=1, keepdims=True)) * inv
        tg[r, :] = s["ghs"][r, :] + back

    s["vb"][...] = gacc[...]
    cv = twin_copy(pc, s["vb"], s["vr"], vs, vrs)
    cv.start()
    tick(30)
    cv.wait()
    one = gacc[0:1, :] + s["vr"][0:1, :]
    both = jnp.where(sub((8, 768)) == 0, jnp.broadcast_to(one, (8, 768)), gacc[...])
    if custom:
        wide = jnp.concatenate([both, jnp.zeros((120, 768), F32)], 0)
        gbuf[0] = jnp.transpose(wide).astype(BF).reshape(gbuf.shape[1:])
        for t in range(31, max(28 + len(ssteps), 31 + len(tails))):
            tick(t)
            if t - 31 < len(tails):
                tails[t - 31](0)

        @pl.loop(0, 12)
        def _(i):
            S.drain(jnp.where(i < 8, i, i + 4))
        Sg.drain(0)
    else:
        c = pltpu.make_async_copy(wg, out_s, vs)
        c.start()
        out_g[...] = both
        c.wait()


def layer(nb, custom, *args):
    V = pl.BlockSpec(memory_space=pltpu.VMEM)
    A = pl.BlockSpec(memory_space=pl.ANY)
    nz = nb // 4
    dma = pltpu.SemaphoreType.DMA
    tt, ws = args[4], args[5:]
    R = ws[1].shape[0]
    shapes = scratch_shapes(custom, nz, R)
    out_shape = [jax.ShapeDtypeStruct((L // 2, 768), BF), jax.ShapeDtypeStruct((L // 2, 768), F32)]
    if custom:
        out_shape += [jax.ShapeDtypeStruct(sh, F32) for sh in ((1, R, 128), (3, R, 384), (R, 384), (R, 1536), (R, 1536))]
        out_specs = [V] * 7
        in_specs = [V] * len(args)
    else:
        out_shape += [jax.ShapeDtypeStruct((8, 768), F32), jax.ShapeDtypeStruct(shapes["wg"][0], BF)]
        out_specs = [V, V, V, A]
        in_specs = [V] * 5 + [A, V]
    scratch = [pltpu.VMEM(*sd) for sd in shapes.values()] + [pltpu.VMEM((tt.shape[1], 128), jnp.int32), dma((12,)), dma((12,)), dma, dma]
    if custom:
        ns, n2 = 2 * (nz - 1) + 4, 4 + 2 * nz
        vb = lambda *sh: pltpu.VMEM(sh, BF)
        scratch += [vb(1, nz, 4, R, 128), pltpu.VMEM((R, 384), F32), vb(1, nz, 4, R, 128), dma((12, ns)), dma((12, ns)), dma((1, ns)), dma((1, ns)),
                    dma((12, n2)), dma((12, n2)), dma((1, n2)), dma((1, n2))] + [vb(12, nz, R, 384)] * 5 + [vb(1, nz, R, 128)] * 5
    return pl.pallas_call(
        functools.partial(layer_body, nb, custom, tuple(shapes)),
        out_shape=out_shape, in_specs=in_specs, out_specs=out_specs, scratch_shapes=scratch,
        compiler_params=pltpu.CompilerParams(collective_id=0, has_side_effects=True, vmem_limit_bytes=int(63.9 * (1 << 20))),
    )(*args)


def on_device(tokens, attn_gain, qkv_weight, out_weight, ffn_gain, up_weight, down_weight, cotangent, segment, cluster, top_keys):
    nb = lax.axis_size("batch")
    R = qkv_weight.shape[0]
    custom = R % 16 == 0 and nb % 4 == 0
    x, ct = tokens[0], cotangent[0]
    tt = top_keys[0].transpose(0, 2, 1)
    if custom:
        ws = (qkv_weight.transpose(1, 0, 2), out_weight.T, up_weight, down_weight.T, attn_gain[None], ffn_gain[None])
    else:
        w = pack(qkv_weight, out_weight, up_weight, down_weight)
        gw = jnp.pad(jnp.stack([attn_gain, ffn_gain], 1), ((0, 0), (0, 126)))
        ws = (lax.all_gather(w, "batch", axis=1, tiled=True), lax.all_gather(gw, "batch", axis=0, tiled=True))
    y, tg, gg, *S = layer(nb, custom, x, ct, segment, cluster[0][:, None, :], tt, *ws)
    if custom:
        y, tg, qg, og, ug, dg, g1, g2 = finish(y, tg, *S, gg)
        return y[None], tg[None], g1[0], qg.transpose(1, 0, 2), og.T, g2[0], ug, dg.T
    S = lax.psum_scatter(S[0].astype(F32), "batch", scatter_dimension=1, tiled=True)
    g = lax.psum_scatter(gg, "batch", scatter_dimension=1, tiled=True)
    cat = lambda a: a.transpose(1, 0, 2).reshape(R, -1)
    qg = S[0:3].reshape(3, R, 3, 128).transpose(1, 2, 0, 3).reshape(R, 3, 384)
    return y[None], tg[None], g[0], qg, S[3].T, g[1], cat(S[4:8]), cat(S[12:16]).T


def pack(q, o, u, d):
    R = q.shape[0]
    qp = q.reshape(R, 3, 3, 128).transpose(2, 0, 1, 3).reshape(3, R, 384)
    up = u.reshape(R, 4, 384).transpose(1, 0, 2)
    dn = d.T.reshape(R, 4, 384).transpose(1, 0, 2)
    return jnp.concatenate([qp, o.T[None], up, dn], 0)


def solution(mesh):
    in_specs = (P("batch", None, None), P("batch"), P("batch", None, "head"), P("head", "batch"), P("batch"), P("batch", "head"), P("head", "batch"), P("batch", None, None), P("batch", None), P("batch", "head", None), P("batch", "head", None, None))
    out_specs = (P("batch", "head", None), P("batch", "head", None), P("batch"), P("batch", None, "head"), P("head", "batch"), P("batch"), P("batch", "head"), P("head", "batch"))
    return jax.shard_map(on_device, mesh=mesh, in_specs=in_specs, out_specs=out_specs, check_vma=False)
```

```python
import functools

import jax
import jax.numpy as jnp
from jax import lax
from jax.experimental import pallas as pl
from jax.experimental.pallas import tpu as pltpu
from jax.sharding import PartitionSpec as P

F32=jnp.float32; BF=jnp.bfloat16
BIG=1e30
NT=(((1,),(1,)),((),()))
TN=(((0,),(0,)),((),()))
NN=(((1,),(0,)),((),()))
def dot(a,b,dims=NN): return lax.dot_general(a,b,dims,preferred_element_type=F32)
def split3(x):
    a=x.astype(BF); r=x-a.astype(F32); b=r.astype(BF); c=(r-b.astype(F32)).astype(BF)
    return a,b,c
def split2(x):
    a=x.astype(BF); return a,(x-a.astype(F32)).astype(BF)
L=1024
def lane(shape): return lax.broadcasted_iota(jnp.int32,shape,len(shape)-1)
def sub(shape): return lax.broadcasted_iota(jnp.int32,shape,len(shape)-2)

def build_masks(own_row, topT):
    mt=jnp.where(own_row==sub((128,L)),1.0,0.0).astype(BF)
    m=jnp.transpose(mt)
    hi=lax.shift_right_arithmetic(topT,5); bit=lax.shift_left(jnp.int32(1),topT&31)
    words=L//32
    a_iota=sub((words,128))
    w=jnp.zeros((words,128),jnp.int32)
    for t in range(topT.shape[0]):
        w=w|jnp.where(hi[t:t+1]==a_iota,bit[t:t+1],0)
    b_iota=sub((32,128)); ln=lane((32,128))
    extra=(ln>=100)&(ln<103)
    ns=[]
    for a in range(words):
        b=(lax.shift_right_logical(jnp.broadcast_to(w[a:a+1],(32,128)),b_iota)&1)
        ns.append(jnp.where(extra,-1.0,jnp.where(b==1,0.0,-BIG)))
    n=jnp.concatenate(ns,0).astype(BF)
    return m,n


TQ = 256
TJ = 256
MESH=pl.DeviceIdType.MESH


def NOP(p): pass
class Place:
    def __init__(self, nb):
        self.nz=nb//4
        self.b=lax.axis_index("batch"); self.h=lax.axis_index("head")
        self.z=self.b//4; self.r=lax.rem(self.b,4)
        even=lax.rem(self.r,2)==0
        self.rx=jnp.where(even,self.r+1,self.r-1)
        self.ry=jnp.where(self.r<2,self.r+2,self.r-2)
        self.rd=3-self.r
        self.X=(self.z*4+self.rx,self.h); self.Y=(self.z*4+self.ry,self.h)
        self.up=(self.b+4,self.h); self.dn=(self.b-4,self.h); self.twin=(self.b,1-self.h)
    def barrier(self):
        bar=pltpu.get_barrier_semaphore()
        for d in (self.X,self.Y,self.twin):
            pl.semaphore_signal(bar,inc=1,device_id=d,device_id_type=MESH)
        @pl.when(self.z<self.nz-1)
        def _(): pl.semaphore_signal(bar,inc=1,device_id=self.up,device_id_type=MESH)
        @pl.when(self.z>0)
        def _(): pl.semaphore_signal(bar,inc=1,device_id=self.dn,device_id_type=MESH)
        lines=jnp.where(self.z<self.nz-1,1,0)+jnp.where(self.z>0,1,0)
        pl.semaphore_wait(bar,3+lines)

def rc(src,dst,ss,rs,dev):
    return pltpu.make_async_remote_copy(src_ref=src,dst_ref=dst,send_sem=ss,recv_sem=rs,device_id=dev,device_id_type=MESH)

class Gather:
    def __init__(self, pc, g, ss, rs):
        self.pc=pc; self.g=g; self.ss=ss; self.rs=rs; self.n=2*(pc.nz-1)
    def cz(self,p,zz,k,dev):
        s=self.g.at[p,zz,self.pc.r]
        return rc(s,s,self.ss.at[p,k],self.rs.at[p,k],dev)
    def z0(self,p):
        c=self.pc
        @pl.when(c.z<c.nz-1)
        def _(): self.cz(p,c.z,0,c.up).start()
        @pl.when(c.z>0)
        def _(): self.cz(p,c.z,1,c.dn).start()
    def zk(self,p,d):
        c=self.pc
        @pl.when(c.z-d>=0)
        def _():
            self.cz(p,c.z-d,2*(d-1),c.up).wait_recv()
        if d<c.nz-1:
            @pl.when((c.z-d>=0)&(c.z<c.nz-1))
            def _(): self.cz(p,c.z-d,2*d,c.up).start()
        @pl.when(c.z+d<c.nz)
        def _():
            self.cz(p,c.z+d,2*(d-1)+1,c.dn).wait_recv()
        if d<c.nz-1:
            @pl.when((c.z+d<c.nz)&(c.z>0))
            def _(): self.cz(p,c.z+d,2*d+1,c.dn).start()
    def cb(self,p,r,k,dev):
        s=self.g.at[p,:,r]
        return rc(s,s,self.ss.at[p,self.n+k],self.rs.at[p,self.n+k],dev)
    def ch(self,p,r,lo,k,dev):
        h=self.pc.nz//2
        s=self.g.at[p,pl.ds(0,h),r] if lo else self.g.at[p,pl.ds(h,self.pc.nz-h),r]
        return rc(s,s,self.ss.at[p,self.n+k],self.rs.at[p,self.n+k],dev)
    def x0(self,p):
        c=self.pc
        self.cb(p,c.r,0,c.X).start(); self.cb(p,c.r,1,c.Y).start()
    def x1(self,p):
        c=self.pc
        self.cb(p,c.rx,0,c.X).wait_recv()
        self.ch(p,c.rx,True,2,c.Y).start()
        self.cb(p,c.ry,1,c.Y).wait_recv()
        self.ch(p,c.ry,False,3,c.X).start()
    def x2(self,p):
        c=self.pc
        self.ch(p,c.rd,True,2,c.Y).wait_recv()
        self.ch(p,c.rd,False,3,c.X).wait_recv()
    def drain(self,p):
        c=self.pc
        for d in range(c.nz-1):
            @pl.when((c.z-d>=0)&(c.z<c.nz-1))
            def _(): self.cz(p,c.z-d,2*d,c.up).wait_send()
            @pl.when((c.z+d<c.nz)&(c.z>0))
            def _(): self.cz(p,c.z+d,2*d+1,c.dn).wait_send()
        self.cb(p,c.r,0,c.X).wait_send(); self.cb(p,c.r,1,c.Y).wait_send()
        self.ch(p,c.rx,True,2,c.Y).wait_send(); self.ch(p,c.ry,False,3,c.X).wait_send()
    def steps(self):
        nz=self.pc.nz
        def last(p):
            self.zk(p,nz-1); self.x0(p)
        return [self.z0]+[functools.partial(lambda d,p:self.zk(p,d),d) for d in range(1,nz-1)]+[last]+[NOP]+[self.x1]+[NOP]+[self.x2]

class PlaneFirst(Gather):
    def cz(self,p,zz,k,dev):
        s=self.g.at[p,zz]
        return rc(s,s,self.ss.at[p,k],self.rs.at[p,k],dev)
    def cb(self,p,r,k,dev):
        s=self.g.at[p,self.pc.z,r]
        return rc(s,s,self.ss.at[p,self.n+k],self.rs.at[p,self.n+k],dev)
    def ch(self,p,r,lo,k,dev):
        n=self.g.shape[3]; h=(n//32)*16
        s=self.g.at[p,self.pc.z,r,pl.ds(0,h)] if lo else self.g.at[p,self.pc.z,r,pl.ds(h,n-h)]
        return rc(s,s,self.ss.at[p,self.n+k],self.rs.at[p,self.n+k],dev)

class Scatter:
    def __init__(self, pc, g, d, rx, ry, ru, rd, ss, rs, slot=lambda p: p):
        self.pc=pc;self.g=g;self.d=d;self.bx=rx;self.by=ry;self.bu=ru;self.bd=rd;self.ss=ss;self.rs=rs
        self.h=pc.nz//2; self.slot=slot
    def half(self,p,r,lo):
        h=self.h; n=self.pc.nz
        return (self.g.at[p,pl.ds(0,h),r],self.d.at[self.slot(p),pl.ds(0,h)]) if lo else (self.g.at[p,pl.ds(h,n-h),r],self.d.at[self.slot(p),pl.ds(h,n-h)])
    def c0(self,p,lo):
        s,t=self.half(p,self.pc.rd,lo); k=0 if lo else 1
        return rc(s,t,self.ss.at[self.slot(p),k],self.rs.at[self.slot(p),k],self.pc.X if lo else self.pc.Y)
    def c1(self,p,x):
        c=self.pc
        return rc(self.g.at[p,:,c.rx if x else c.ry],(self.bx if x else self.by).at[self.slot(p)],self.ss.at[self.slot(p),2 if x else 3],self.rs.at[self.slot(p),2 if x else 3],c.X if x else c.Y)
    def cu(self,p,zz,up):
        c=self.pc; k=4+zz if up else 4+c.nz+zz
        return rc(self.g.at[p,zz,c.r],(self.bu if up else self.bd).at[self.slot(p),zz],self.ss.at[self.slot(p),k],self.rs.at[self.slot(p),k],c.up if up else c.dn)
    def add(self,dst,*srcs):
        v=dst[...].astype(F32)
        for s in srcs: v=v+s[...].astype(F32)
        dst[...]=v.astype(BF)
    def s0(self,p):
        self.c0(p,True).start(); self.c0(p,False).start()
    def s1(self,p):
        c=self.pc;h=self.h;n=c.nz
        self.c0(p,True).wait_recv()
        self.add(self.g.at[p,pl.ds(0,h),c.ry],self.d.at[self.slot(p),pl.ds(0,h)])
        self.c1(p,False).start()
        self.c0(p,False).wait_recv()
        self.add(self.g.at[p,pl.ds(h,n-h),c.rx],self.d.at[self.slot(p),pl.ds(h,n-h)])
        self.c1(p,True).start()
    def s2(self,p):
        c=self.pc
        self.c1(p,True).wait_recv(); self.c1(p,False).wait_recv()
        self.add(self.g.at[p,:,c.r],self.bx.at[self.slot(p)],self.by.at[self.slot(p)])
        self.zk(p,0)
    def zk(self,p,k):
        c=self.pc; nz=c.nz
        @pl.when(c.z==k)
        def _():
            for zz in range(nz-1,k,-1):
                if k>0:
                    self.cu(p,zz,True).wait_recv()
                    self.add(self.g.at[p,zz,c.r],self.bu.at[self.slot(p),zz])
                self.cu(p,zz,True).start()
        @pl.when(c.z==nz-1-k)
        def _():
            for zz in range(0,nz-1-k):
                if k>0:
                    self.cu(p,zz,False).wait_recv()
                    self.add(self.g.at[p,zz,c.r],self.bd.at[self.slot(p),zz])
                self.cu(p,zz,False).start()
    def fin(self,p,tot,place=None):
        c=self.pc
        tot[...]=self.g[p,c.z,c.r].astype(F32)
        @pl.when(c.z>0)
        def _():
            self.cu(p,c.z,True).wait_recv()
            tot[...]+=self.bu[self.slot(p),c.z].astype(F32)
        @pl.when(c.z<c.nz-1)
        def _():
            self.cu(p,c.z,False).wait_recv()
            tot[...]+=self.bd[self.slot(p),c.z].astype(F32)
        if place is not None: place(p)
    def drain(self,p):
        c=self.pc; nz=c.nz
        self.c0(p,True).wait_send(); self.c0(p,False).wait_send()
        self.c1(p,True).wait_send(); self.c1(p,False).wait_send()
        for zz in range(nz):
            @pl.when(zz>c.z)
            def _(): self.cu(p,zz,True).wait_send()
            @pl.when(zz<c.z)
            def _(): self.cu(p,zz,False).wait_send()
    def lines(self):
        return [functools.partial(lambda k,p:self.zk(p,k),k) for k in range(1,self.pc.nz-1)]
    def steps(self,place,tot):
        return [self.s0,NOP,self.s1,NOP,self.s2]+self.lines()+[lambda p:self.fin(p,tot,place)]
    def tight(self,out):
        return [self.s0,self.s1,self.s2]+self.lines()+[lambda p:self.fin(p,out.at[0])]


EPS = 1e-5
RT = 256


def pick(static, cond, body):
    if isinstance(cond, (bool, int)):
        if cond:
            body()
    else:
        pl.when(cond)(body)


def norm_rows(values):
    mean = jnp.mean(values, axis=1, keepdims=True)
    centred = values - mean
    inverse = lax.rsqrt(jnp.mean(centred * centred, axis=1, keepdims=True) + EPS)
    return centred * inverse, inverse


def gelu_both(u):
    c = 0.7978845608028654
    u2 = u * u
    t = jnp.tanh(c * u * (1.0 + 0.044715 * u2))
    half = 0.5 + 0.5 * t
    act = u * half
    grad = half + (0.5 * c) * u * (1.0 - t * t) * (1.0 + (3 * 0.044715) * u2)
    return act, grad


def flat(ref, p):
    v = ref[p]
    return v.reshape(-1, v.shape[-1])


def tiles(n):
    return lambda f: pl.loop(0, n)(f)


def rows_of(i, n=RT):
    return pl.ds(pl.multiple_of(i * n, n), n)


def twin_copy(pc, src, dst, ss, rs):
    return rc(src, dst, ss, rs, pc.twin)


def members(cl, hh):
    return jnp.where(cl[hh] == sub((128, L)), 1.0, 0.0).astype(BF)


def fwd_head(p, h, qkv, mb, cl, n_s, seg, qaug, kaug, att, ex, prob_o):
    odd = h == 1
    hh = 2 * p + h
    q = qkv[p, :, 0:128]
    k = qkv[p, :, 128:256]
    v = qkv[p, :, 256:384]
    ln = lane((L, 128))
    mine = (ln >= 64) if odd else (ln < 64)
    lc = lane((128, 128))
    minec = (lc >= 64) if odd else (lc < 64)
    zero = jnp.zeros((), BF)
    qm = jnp.where(mine, q, zero)
    vaug = jnp.where(mine, v, jnp.ones((), BF))
    mt = members(cl, hh)
    top = jnp.transpose(n_s[hh]).astype(F32) == 0.0
    cnt = jnp.maximum(jnp.sum(mt.astype(F32), axis=1, keepdims=True), 1.0)
    cen = (dot(mt, qm) / cnt).astype(BF)
    cs = (cen.astype(F32) * 0.125).astype(BF)
    s = dot(cs, k, NT)
    cm = lax.rem(sub((128, 1)), jnp.int32(10))
    s = jnp.where(seg[...] == cm, s, -BIG)
    mx = jnp.max(s, axis=1, keepdims=True)
    e = jnp.exp(s - mx)
    prob = e / jnp.sum(e, axis=1, keepdims=True)
    mass = jnp.sum(jnp.where(top, prob, 0.0), axis=1, keepdims=True)
    prob_o[hh] = jnp.where(top, -prob, prob).astype(BF)
    rest = dot(jnp.where(top, 0.0, prob).astype(BF), v)
    rh, rl = split2(jnp.where(minec, rest, jnp.broadcast_to(mass, (128, 128))))
    rr = jnp.concatenate([rh, rl], 1)
    qaug[:, :128] = (qm.astype(F32) * 0.125).astype(BF)
    qaug[:, 128:] = mb[hh]
    kaug[:, :128] = k
    kaug[:, 128:] = n_s[hh]
    lt = lane((TQ, 128))
    minet = (lt >= 64) if odd else (lt < 64)
    cols = pl.ds(pl.multiple_of(p * 128, 128), 128)
    for t in range(L // TQ):
        sl = pl.ds(t * TQ, TQ)
        sc = dot(qaug[sl, :], kaug[...], NT)
        mm = jnp.max(sc, axis=1, keepdims=True)
        pr = jnp.exp(sc - mm).astype(BF)
        o = dot(pr, vaug)
        mt_ = qaug[sl, 128:]
        ee = dot(mt_, rr)
        ee = ee[:, :128] + ee[:, 128:]
        osw = pltpu.roll(o, 64, 1)
        esw = pltpu.roll(ee, 64, 1)
        exact = o / osw
        a = exact * esw + ee
        tot = jnp.where(minet, osw, o)
        ms = jnp.where(minet, esw, ee)
        lse = mm + jnp.log(tot) - jnp.log(jnp.maximum(ms, 1e-37))
        h3, m3, l3 = split3(lse)
        mb[hh, sl, :] = jnp.where(lt == 100, h3.astype(F32), jnp.where(lt == 101, m3.astype(F32), jnp.where(lt == 102, l3.astype(F32), mt_.astype(F32)))).astype(BF)
        if odd:
            att[sl, cols] = jnp.where(lt < 64, att[sl, cols], a.astype(BF))
            ex[sl, cols] = jnp.where(lt < 64, ex[sl, cols], exact.astype(BF))
        else:
            att[sl, cols] = a.astype(BF)
            ex[sl, cols] = exact.astype(BF)


def as_column(row):
    n = row.shape[1]
    eye = sub((n, n)) == lane((n, n))
    return jnp.sum(jnp.where(eye, row.astype(F32), 0.0), axis=1, keepdims=True)


def fill_own(pc, g, gg, q3, oT, upw, dT, ga, gf):
    for p in range(3):
        for i in range(3):
            g[p, pc.z, pc.r, :, i * 128:(i + 1) * 128] = q3[i, :, p * 128:(p + 1) * 128]
    g[3, pc.z, pc.r] = oT[...]
    for q in range(4):
        g[4 + q, pc.z, pc.r] = upw[:, q * 384:(q + 1) * 384]
        g[8 + q, pc.z, pc.r] = dT[:, q * 384:(q + 1) * 384]
    R = oT.shape[0]
    ln = lane((R, 128))
    gg[0, pc.z, pc.r] = jnp.where(ln == 0, as_column(ga[...]), jnp.where(ln == 1, as_column(gf[...]), 0.0)).astype(BF)


def bwd_head(p, h, cl, s, qaug, kaug, gaug, vaug, dq_o, dk_o, dv_o, dqt):
    qkv, g, ex = s["qkv"], s["gatt"], s["ex"]
    hh = 2 * p + h
    cols = pl.ds(pl.multiple_of(p * 128, 128), 128)
    qv = qkv[p, :, 0:128]
    kv = qkv[p, :, 128:256]
    vv = qkv[p, :, 256:384]
    gv = g[:, cols]
    ln = lane((L, 128))
    zero = jnp.zeros((), BF)
    lc = lane((128, 128))
    kT = jnp.transpose(kv)
    prod = gv.astype(F32) * ex[:, cols].astype(F32)
    mine = (ln >= 64) if h else (ln < 64)
    minec = (lc >= 64) if h else (lc < 64)
    o = 0 if h else 64
    r = jnp.sum(jnp.where(mine, prod, 0.0), axis=1, keepdims=True)
    h3, m3, l3 = split3(r)
    gm = jnp.where(mine, gv, zero)
    ga = jnp.where(ln == o, h3.astype(F32), jnp.where(ln == o + 1, m3.astype(F32), jnp.where(ln == o + 2, l3.astype(F32), gm.astype(F32)))).astype(BF)
    gaug[...] = ga
    vaug[...] = jnp.where(mine, vv, jnp.where((ln >= o) & (ln < o + 3), jnp.full((), -1.0, BF), zero))
    qm = jnp.where(mine, qv, zero)
    qs = (qm.astype(F32) * 0.125).astype(BF)
    qaug[:, :128] = qs
    qaug[:, 128:] = s["mb"][hh]
    kaug[:, :128] = kv
    kaug[:, 128:] = s["ns"][hh]
    mt = members(cl, hh)
    signed = s["prob"][hh].astype(F32)
    top = signed < 0.0
    prob = jnp.abs(signed)
    cnt = jnp.maximum(jnp.sum(mt.astype(F32), axis=1, keepdims=True), 1.0)
    cen = (dot(mt, qm) / cnt).astype(BF)
    cs = (cen.astype(F32) * 0.125).astype(BF)
    gr = dot(mt, ga)
    gmass = jnp.sum(jnp.where((lc >= o) & (lc < o + 3), gr, 0.0), axis=1, keepdims=True)
    grest = jnp.where(minec, gr, 0.0).astype(BF)
    gp = jnp.where(top, gmass, dot(grest, vv, NT))
    gs = (prob * (gp - jnp.sum(prob * gp, axis=1, keepdims=True))).astype(BF)
    rw = jnp.where(top, 0.0, prob).astype(BF)
    gcen = dot(gs, jnp.where(mine, kv, zero)) / cnt
    gh, gl = split2(gcen)
    gg = jnp.concatenate([gh, gl], 1)
    gsT = jnp.transpose(gs)
    rwT = jnp.transpose(rw)
    kTh = kT[64 * h:64 * h + 64]
    for t in range(L // TJ):
        sl = pl.ds(t * TJ, TJ)
        st = dot(kaug[sl, :], qaug[...], NT)
        pr = jnp.exp(st)
        dp = dot(vaug[sl, :], gaug[...], NT)
        ds = (pr * dp).astype(BF)
        dv = dot(pr.astype(BF), gm) + dot(rwT[t * TJ:(t + 1) * TJ], grest)
        dk = dot(ds, qs) + dot(gsT[t * TJ:(t + 1) * TJ], cs)
        if h == 0:
            dv_o[sl, :] = dv
            dk_o[sl, :] = dk
        else:
            dv_o[sl, :] += dv
            dk_o[sl, :] += dk
        dqp = dot(kTh[:, t * TJ:(t + 1) * TJ], ds)
        if t == 0:
            dqt[64 * h:64 * h + 64, :] = dqp
        else:
            dqt[64 * h:64 * h + 64, :] += dqp
    dd = dot(jnp.where(ln < 100, s["mb"][hh], zero), gg)
    dd = dd[:, :128] + dd[:, 128:]
    if h == 0:
        dq_o[...] = dd
    else:
        dq_o[...] += dd


def place_sum(p, tot, outs):
    qg, og, ug, dg = outs

    def pair(p):
        for i in range(3):
            qg[i, :, pl.ds(pl.multiple_of(p * 128, 128), 128)] = tot[:, i * 128:(i + 1) * 128]

    def wide(ref, q):
        ref[:, pl.ds(pl.multiple_of(q * 384, 128), 384)] = tot[...]

    pick(None, p < 3, lambda: pair(p))
    pick(None, p == 3, lambda: og.__setitem__(..., tot[...]))
    pick(None, (3 < p < 8) if isinstance(p, int) else (p > 3) & (p < 8), lambda: wide(ug, p - 4))
    pick(None, p >= 12, lambda: wide(dg, p - 12))


def finish_body(*refs):
    ins, gg, outs, (g1, g2), bufs, (si, so) = refs[:6], refs[6], refs[7:13], refs[13:15], refs[15:21], refs[21:]
    ci = [pltpu.make_async_copy(a, b, si.at[i]) for i, (a, b) in enumerate(zip(ins, bufs))]
    co = [pltpu.make_async_copy(a, b, so.at[i]) for i, (a, b) in enumerate(zip(bufs, outs))]
    for c in ci:
        c.start()
    R = gg.shape[1]
    eye = sub((R, R)) == lane((R, R))
    for i, g in enumerate((g1, g2)):
        g[...] = jnp.sum(jnp.where(eye, gg[0, :, i:i + 1], 0.0), axis=0, keepdims=True)
    for a, b in zip(ci, co):
        a.wait()
        b.start()
    for c in co:
        c.wait()


def finish(*arrays):
    V = pl.BlockSpec(memory_space=pltpu.VMEM)
    A = pl.BlockSpec(memory_space=pl.ANY)
    R = arrays[6].shape[1]
    dma = pltpu.SemaphoreType.DMA
    return pl.pallas_call(
        finish_body,
        out_shape=[jax.ShapeDtypeStruct(a.shape, a.dtype) for a in arrays[:6]] + [jax.ShapeDtypeStruct((1, R), F32)] * 2,
        in_specs=[A] * 6 + [V], out_specs=[A] * 6 + [V] * 2,
        scratch_shapes=[pltpu.VMEM(a.shape, a.dtype) for a in arrays[:6]] + [dma((6,)), dma((6,))],
        compiler_params=pltpu.CompilerParams(vmem_limit_bytes=60 << 20),
    )(*arrays)


def scratch_shapes(custom, nz, R):
    f = lambda *s: (s, F32)
    b = lambda *s: (s, BF)
    wide = (16, nz, 4, R, 384) if custom else (16, 768, 384)
    return {
        "gr": f(8, 768), "n1": b(L, 768), "qkv": b(3, L, 384), "att": b(L, 384), "ex": b(L, 384), "mb": b(6, L, 128),
        "ns": b(6, L, 128), "prob": b(6, 128, L), "hid": f(L, 768), "n2": b(L, 768), "act": b(4, L, 384), "dg": b(4, L, 384),
        "aT": b(768, L), "ghs": f(L // 2, 768), "eb": b(L, 768), "er": b(L, 768), "fr": b(L // 2, 768), "gatt": b(L, 384),
        "dqkv": b(L, 384), "qaug": b(L, 256), "kaug": b(L, 256), "gaug": b(L, 128), "vaug": b(L, 128),
        "dqs": f(L, 128), "dks": f(L, 128), "dvs": f(L, 128), "dqt": f(128, L), "gacc": f(8, 768), "vb": f(8, 768), "vr": f(8, 768),
        "wg": b(*wide),
    }


def layer_body(nb, custom, names, *refs):
    refs = list(refs)
    take = lambda n: [refs.pop(0) for _ in range(n)]
    x, ct, seg, cl, tt = take(5)
    own = take(6 if custom else 2)
    y, tg, out_g = take(3)
    out_s = take(4) if custom else take(1)[0]
    s = dict(zip(names, take(len(names))))
    tpad, es, ers, vs, vrs = take(5)
    pc = Place(nb)
    wg, hid, n1, n2, qkv, att, ex, act, dg = (s[n] for n in ("wg", "hid", "n1", "n2", "qkv", "att", "ex", "act", "dg"))
    aT, eb, er, fr, gr, gacc = (s[n] for n in ("aT", "eb", "er", "fr", "gr", "gacc"))
    half, nh, nt = L // 2, L // 2 // RT, L // RT

    if custom:
        gg, tot, gbuf, ss, rs, gss, grs, ss2, rs2, gss2, grs2 = take(11)
        land, gland = take(5), take(5)
        G, Gg = Gather(pc, wg, ss, rs), Gather(pc, gg, gss, grs)
        S = Scatter(pc, wg, *land, ss2, rs2, slot=lambda p: p - 4 if isinstance(p, int) and p >= 12 else p if isinstance(p, int) else jnp.where(p >= 12, p - 4, p))
        Sg = Scatter(pc, gbuf, *gland, gss2, grs2)
        Gp = PlaneFirst(pc, wg, ss, rs)
        m = pc.nz - 1

        def last(p):
            G.zk(p, m)
            G.x0(p)

        def turn(p):
            Gp.x2(p)
            Gp.z0(p)
        line = lambda g, off: [(off + d, functools.partial(lambda d, p: g.zk(p, d), d)) for d in range(1, m)][::-1]
        nine = lambda k: k + k // 3
        three = lambda k: k + 3
        rest = list(range(1, 9))
        gather = [(m + 2, G.x2, [0], nine), (m + 1, G.x1, [0], nine), (m + 3, G.x2, rest, nine), (m + 2, G.x1, rest, nine)]
        gather += [(e, fn, list(range(9)), nine) for e, fn in [(m, last)] + line(G, 0) + [(0, G.z0)]]
        gather += [(e, fn, [0, 4, 8], three) for e, fn in [(m + 3, lambda p: Gp.zk(p, m))] + line(Gp, 3) + [(2, turn), (1, Gp.x1), (0, Gp.x0)]]
        gsteps = [Gg.z0] + [functools.partial(lambda d: Gg.zk(0, d), d) for d in range(1, m)] + [None, Gg.x1, Gg.x2]
        ssteps = S.steps(lambda p: place_sum(p, tot, out_s), tot)
        tails = Sg.tight(out_g)
        starts = {13: 12, 14: 13, 15: 14, 16: 15, 18: 4, 19: 5, 20: 6, 21: 7, 22: 3, 24: 0, 26: 1, 28: 2}

        def tick(t, span=None):
            fixed = isinstance(t, int)
            ts = [t] if fixed else list(range(*span))
            for i in range(len(ssteps) - 1, -1, -1):
                hits = [u - i for u in ts if u - i in starts]
                if not hits or ssteps[i] is NOP:
                    continue
                if fixed:
                    ssteps[i](starts[hits[0]])
                    continue
                u = t - i
                ok = functools.reduce(jnp.logical_or, [u == k for k in hits])
                part = functools.reduce(lambda a, k: jnp.where(u == k, starts[k], a), hits, 0)
                pl.when(ok)(lambda i=i, part=part: ssteps[i](part))
            for off, fn, at, to in gather:
                hits = [u - off for u in ts if u - off in at]
                if not hits:
                    continue
                u = t - off
                ok = True if fixed else functools.reduce(jnp.logical_or, [u == k for k in hits])
                pick(None, ok, lambda fn=fn, p=to(u): fn(p))
            if fixed and t < len(gsteps):
                if t == m:
                    Gg.zk(0, m)
                    Gg.x0(0)
                elif t == 0:
                    gsteps[0](0)
                elif t < m:
                    gsteps[t]()
                else:
                    gsteps[t](0)
    else:
        tick = lambda t, span=None: None

    tpad[...] = jnp.full_like(tpad, -1)
    pc.barrier()
    if custom:
        fill_own(pc, wg, gg, *own)
    tick(0)

    @tiles(nt)
    def _(i):
        hid[rows_of(i), :] = norm_rows(x[rows_of(i), :].astype(F32))[0]

    tick(1)

    def mask(h):
        tpad[:, 0:tt.shape[2]] = tt[h]
        a, n = build_masks(cl[h], tpad[...])
        s["mb"][h], s["ns"][h] = a, n

    def transpose_into(src):
        for i in range(nt):
            aT[:, i * RT:(i + 1) * RT] = jnp.transpose(src[i * RT:(i + 1) * RT, :])

    def put(p, left, right):
        wg[p] = dot(left, right).astype(BF).reshape(wg.shape[1:])

    pl.loop(0, 2)(mask)
    tick(2)
    pl.loop(2, 4)(mask)
    tick(3)
    pl.loop(4, 6)(mask)
    transpose_into(ct)
    tick(4)
    tick(5)
    if custom:
        gains = gg[0].reshape(768, 128)
    else:
        c = pltpu.make_async_copy(own[0], wg.at[0:12], vs)
        c.start()
        c.wait()
        gains = own[1][...]
    gr[...] = jnp.transpose(gains.astype(F32))[0:8]

    @tiles(nt)
    def _(i):
        n1[rows_of(i), :] = (hid[rows_of(i), :] * gr[0:1, :]).astype(BF)

    @pl.loop(0, 3)
    def _(p):
        @tiles(nt)
        def _(i):
            qkv[p, rows_of(i), :] = dot(n1[rows_of(i), :], flat(wg, p)).astype(BF)
        for h in range(2):
            tick(6 + 2 * p + h, (6 + h, 12, 2))
            fwd_head(p, h, qkv, s["mb"], cl, s["ns"], seg, s["qaug"], s["kaug"], att, ex, s["prob"])

    def send(k, src, dst, i):
        return twin_copy(pc, src.at[rows_of(i)], dst.at[rows_of(i)], es.at[k + i], ers.at[k + i])

    @tiles(nt)
    def _(i):
        eb[rows_of(i), :] = dot(att[rows_of(i), :], flat(wg, 3), NT).astype(BF)
        send(0, eb, er, i).start()

    tick(12)

    @tiles(nt)
    def _(i):
        r = rows_of(i)
        send(0, eb, er, i).wait()
        hv = x[r, :].astype(F32) + (eb[r, :].astype(F32) + er[r, :].astype(F32))
        hid[r, :] = hv
        n2[r, :] = (norm_rows(hv)[0] * gr[1:2, :]).astype(BF)

    def up(q):
        @tiles(nt)
        def _(i):
            a, d = gelu_both(dot(n2[rows_of(i), :], flat(wg, 4 + q)))
            act[q, rows_of(i), :] = a.astype(BF)
            dg[q, rows_of(i), :] = d.astype(BF)

    def down_grad(q):
        up(q)
        put(12 + q, aT[...], act[q])

    pl.loop(0, 2)(down_grad)
    tick(13)
    pl.loop(2, 4)(down_grad)
    tick(14)
    transpose_into(n2)

    def part(i):
        acc = dot(act[0, rows_of(i), :], flat(wg, 8), NT)
        for q in range(1, 4):
            acc += dot(act[q, rows_of(i), :], flat(wg, 8 + q), NT)
        return acc

    @tiles(nh)
    def _(i):
        eb[rows_of(i), :] = part((1 - pc.h) * nh + i).astype(BF)
        send(4, eb, fr, i).start()

    tick(15)

    @pl.loop(0, 4)
    def _(q):
        @tiles(nt)
        def _(i):
            ga = dot(ct[rows_of(i), :], flat(wg, 8 + q))
            dg[q, rows_of(i), :] = (ga * dg[q, rows_of(i), :].astype(F32)).astype(BF)

    @tiles(nh)
    def _(i):
        acc = part(pc.h * nh + i).astype(BF).astype(F32)
        send(4, eb, fr, i).wait()
        y[rows_of(i), :] = (hid[rows_of(pc.h * nh + i), :] + (acc + fr[rows_of(i), :].astype(F32))).astype(BF)

    tick(16)
    if custom:
        @pl.loop(0, 9)
        def _(k):
            G.drain(nine(k))

        @pl.loop(0, 3)
        def _(k):
            Gp.drain(4 * k + 3)
        Gg.drain(0)

    @tiles(nt)
    def _(i):
        acc = dot(dg[0, rows_of(i), :], flat(wg, 4), NT)
        for q in range(1, 4):
            acc += dot(dg[q, rows_of(i), :], flat(wg, 4 + q), NT)
        eb[rows_of(i), :] = acc.astype(BF)
        send(6, eb, er, i).start()

    def up_grad(q):
        put(4 + q, aT[...], dg[q])

    tick(17)
    pl.loop(0, 2)(up_grad)
    tick(18)
    pl.loop(2, 4)(up_grad)
    tick(19)
    gacc[...] = jnp.zeros_like(gacc)
    gat = n2

    @tiles(nt)
    def _(i):
        r = rows_of(i)
        send(6, eb, er, i).wait()
        gn = eb[r, :].astype(F32) + er[r, :].astype(F32)
        n, inv = norm_rows(hid[r, :])
        gacc[1:2, :] += jnp.sum(gn * n, axis=0, keepdims=True)
        a = gn * gr[1:2, :]
        back = (a - jnp.mean(a, axis=1, keepdims=True) - n * jnp.mean(a * n, axis=1, keepdims=True)) * inv
        gh = ct[r, :].astype(F32) + back
        gat[r, :] = gh.astype(BF)

        @pl.when((i >= pc.h * nh) & (i < pc.h * nh + nh))
        def _():
            s["ghs"][rows_of(i - pc.h * nh), :] = gh

    tick(20)

    @tiles(nt)
    def _(i):
        s["gatt"][rows_of(i), :] = dot(gat[rows_of(i), :], flat(wg, 3)).astype(BF)

    transpose_into(gat)
    put(3, aT[...], att[...])
    tick(21)
    transpose_into(n1)
    tick(22)
    nacc = hid
    dqkv = s["dqkv"]

    @pl.loop(0, 3)
    def _(p):
        bwd_head(p, 0, cl, s, s["qaug"], s["kaug"], s["gaug"], s["vaug"], s["dqs"], s["dks"], s["dvs"], s["dqt"])
        tick(23 + 2 * p, (23, 29, 2))
        bwd_head(p, 1, cl, s, s["qaug"], s["kaug"], s["gaug"], s["vaug"], s["dqs"], s["dks"], s["dvs"], s["dqt"])
        dqkv[:, 0:128] = ((s["dqs"][...] + jnp.transpose(s["dqt"][...])) * 0.125).astype(BF)
        dqkv[:, 128:256] = s["dks"][...].astype(BF)
        dqkv[:, 256:384] = s["dvs"][...].astype(BF)

        @tiles(nt)
        def _(i):
            v = dot(dqkv[rows_of(i), :], flat(wg, p), NT)

            @pl.when(p == 0)
            def _():
                nacc[rows_of(i), :] = v

            @pl.when(p > 0)
            def _():
                nacc[rows_of(i), :] += v
        put(p, aT[...], dqkv[...])
        tick(24 + 2 * p, (24, 30, 2))

    @tiles(nh)
    def _(i):
        eb[rows_of(i), :] = nacc[rows_of((1 - pc.h) * nh + i), :].astype(BF)
        send(10, eb, fr, i).start()

    tick(29)

    @tiles(nh)
    def _(i):
        r = rows_of(i)
        send(10, eb, fr, i).wait()
        gn = nacc[rows_of(pc.h * nh + i), :].astype(BF).astype(F32) + fr[r, :].astype(F32)
        n, inv = norm_rows(x[rows_of(pc.h * nh + i), :].astype(F32))
        gacc[0:1, :] += jnp.sum(gn * n, axis=0, keepdims=True)
        a = gn * gr[0:1, :]
        back = (a - jnp.mean(a, axis=1, keepdims=True) - n * jnp.mean(a * n, axis=1, keepdims=True)) * inv
        tg[r, :] = s["ghs"][r, :] + back

    s["vb"][...] = gacc[...]
    cv = twin_copy(pc, s["vb"], s["vr"], vs, vrs)
    cv.start()
    tick(30)
    cv.wait()
    one = gacc[0:1, :] + s["vr"][0:1, :]
    both = jnp.where(sub((8, 768)) == 0, jnp.broadcast_to(one, (8, 768)), gacc[...])
    if custom:
        wide = jnp.concatenate([both, jnp.zeros((120, 768), F32)], 0)
        gbuf[0] = jnp.transpose(wide).astype(BF).reshape(gbuf.shape[1:])
        for t in range(31, max(28 + len(ssteps), 31 + len(tails))):
            tick(t)
            if t - 31 < len(tails):
                tails[t - 31](0)

        @pl.loop(0, 12)
        def _(i):
            S.drain(jnp.where(i < 8, i, i + 4))
        Sg.drain(0)
    else:
        c = pltpu.make_async_copy(wg, out_s, vs)
        c.start()
        out_g[...] = both
        c.wait()


def layer(nb, custom, *args):
    V = pl.BlockSpec(memory_space=pltpu.VMEM)
    A = pl.BlockSpec(memory_space=pl.ANY)
    nz = nb // 4
    dma = pltpu.SemaphoreType.DMA
    tt, ws = args[4], args[5:]
    R = ws[1].shape[0]
    shapes = scratch_shapes(custom, nz, R)
    out_shape = [jax.ShapeDtypeStruct((L // 2, 768), BF), jax.ShapeDtypeStruct((L // 2, 768), F32)]
    if custom:
        out_shape += [jax.ShapeDtypeStruct(sh, F32) for sh in ((1, R, 128), (3, R, 384), (R, 384), (R, 1536), (R, 1536))]
        out_specs = [V] * 7
        in_specs = [V] * len(args)
    else:
        out_shape += [jax.ShapeDtypeStruct((8, 768), F32), jax.ShapeDtypeStruct(shapes["wg"][0], BF)]
        out_specs = [V, V, V, A]
        in_specs = [V] * 5 + [A, V]
    scratch = [pltpu.VMEM(*sd) for sd in shapes.values()] + [pltpu.VMEM((tt.shape[1], 128), jnp.int32), dma((12,)), dma((12,)), dma, dma]
    if custom:
        ns, n2 = 2 * (nz - 1) + 4, 4 + 2 * nz
        vb = lambda *sh: pltpu.VMEM(sh, BF)
        scratch += [vb(1, nz, 4, R, 128), pltpu.VMEM((R, 384), F32), vb(1, nz, 4, R, 128), dma((12, ns)), dma((12, ns)), dma((1, ns)), dma((1, ns)),
                    dma((12, n2)), dma((12, n2)), dma((1, n2)), dma((1, n2))] + [vb(12, nz, R, 384)] * 5 + [vb(1, nz, R, 128)] * 5
    return pl.pallas_call(
        functools.partial(layer_body, nb, custom, tuple(shapes)),
        out_shape=out_shape, in_specs=in_specs, out_specs=out_specs, scratch_shapes=scratch,
        compiler_params=pltpu.CompilerParams(collective_id=0, has_side_effects=True, vmem_limit_bytes=int(63.9 * (1 << 20))),
    )(*args)


def on_device(tokens, attn_gain, qkv_weight, out_weight, ffn_gain, up_weight, down_weight, cotangent, segment, cluster, top_keys):
    nb = lax.axis_size("batch")
    R = qkv_weight.shape[0]
    custom = R % 16 == 0 and nb % 4 == 0
    x, ct = tokens[0], cotangent[0]
    tt = top_keys[0].transpose(0, 2, 1)
    if custom:
        ws = (qkv_weight.transpose(1, 0, 2), out_weight.T, up_weight, down_weight.T, attn_gain[None], ffn_gain[None])
    else:
        w = pack(qkv_weight, out_weight, up_weight, down_weight)
        gw = jnp.pad(jnp.stack([attn_gain, ffn_gain], 1), ((0, 0), (0, 126)))
        ws = (lax.all_gather(w, "batch", axis=1, tiled=True), lax.all_gather(gw, "batch", axis=0, tiled=True))
    y, tg, gg, *S = layer(nb, custom, x, ct, segment, cluster[0][:, None, :], tt, *ws)
    if custom:
        y, tg, qg, og, ug, dg, g1, g2 = finish(y, tg, *S, gg)
        return y[None], tg[None], g1[0], qg.transpose(1, 0, 2), og.T, g2[0], ug, dg.T
    S = lax.psum_scatter(S[0].astype(F32), "batch", scatter_dimension=1, tiled=True)
    g = lax.psum_scatter(gg, "batch", scatter_dimension=1, tiled=True)
    cat = lambda a: a.transpose(1, 0, 2).reshape(R, -1)
    qg = S[0:3].reshape(3, R, 3, 128).transpose(1, 2, 0, 3).reshape(R, 3, 384)
    return y[None], tg[None], g[0], qg, S[3].T, g[1], cat(S[4:8]), cat(S[12:16]).T


def pack(q, o, u, d):
    R = q.shape[0]
    qp = q.reshape(R, 3, 3, 128).transpose(2, 0, 1, 3).reshape(3, R, 384)
    up = u.reshape(R, 4, 384).transpose(1, 0, 2)
    dn = d.T.reshape(R, 4, 384).transpose(1, 0, 2)
    return jnp.concatenate([qp, o.T[None], up, dn], 0)


def solution(mesh):
    in_specs = (P("batch", None, None), P("batch"), P("batch", None, "head"), P("head", "batch"), P("batch"), P("batch", "head"), P("head", "batch"), P("batch", None, None), P("batch", None), P("batch", "head", None), P("batch", "head", None, None))
    out_specs = (P("batch", "head", None), P("batch", "head", None), P("batch"), P("batch", None, "head"), P("head", "batch"), P("batch"), P("batch", "head"), P("head", "batch"))
    return jax.shard_map(on_device, mesh=mesh, in_specs=in_specs, out_specs=out_specs, check_vma=False)
```

```python
import functools

import jax
import jax.numpy as jnp
from jax import lax
from jax.experimental import pallas as pl
from jax.experimental.pallas import tpu as pltpu
from jax.sharding import PartitionSpec as P

F32=jnp.float32; BF=jnp.bfloat16
BIG=1e30
NT=(((1,),(1,)),((),()))
TN=(((0,),(0,)),((),()))
NN=(((1,),(0,)),((),()))
def dot(a,b,dims=NN): return lax.dot_general(a,b,dims,preferred_element_type=F32)
def split3(x):
    a=x.astype(BF); r=x-a.astype(F32); b=r.astype(BF); c=(r-b.astype(F32)).astype(BF)
    return a,b,c
def split2(x):
    a=x.astype(BF); return a,(x-a.astype(F32)).astype(BF)
L=1024
def lane(shape): return lax.broadcasted_iota(jnp.int32,shape,len(shape)-1)
def sub(shape): return lax.broadcasted_iota(jnp.int32,shape,len(shape)-2)

def build_masks(own_row, topT):
    mt=jnp.where(own_row==sub((128,L)),1.0,0.0).astype(BF)
    m=jnp.transpose(mt)
    hi=lax.shift_right_arithmetic(topT,5); bit=lax.shift_left(jnp.int32(1),topT&31)
    words=L//32
    a_iota=sub((words,128))
    w=jnp.zeros((words,128),jnp.int32)
    for t in range(topT.shape[0]):
        w=w|jnp.where(hi[t:t+1]==a_iota,bit[t:t+1],0)
    b_iota=sub((32,128)); ln=lane((32,128))
    extra=(ln>=100)&(ln<103)
    ns=[]
    for a in range(words):
        b=(lax.shift_right_logical(jnp.broadcast_to(w[a:a+1],(32,128)),b_iota)&1)
        ns.append(jnp.where(extra,-1.0,jnp.where(b==1,0.0,-BIG)))
    n=jnp.concatenate(ns,0).astype(BF)
    return m,n


TQ = 512
TJ = 512
MESH=pl.DeviceIdType.MESH


def NOP(p): pass
class Place:
    def __init__(self, nb):
        self.nz=nb//4
        self.b=lax.axis_index("batch"); self.h=lax.axis_index("head")
        self.z=self.b//4; self.r=lax.rem(self.b,4)
        even=lax.rem(self.r,2)==0
        self.rx=jnp.where(even,self.r+1,self.r-1)
        self.ry=jnp.where(self.r<2,self.r+2,self.r-2)
        self.rd=3-self.r
        self.X=(self.z*4+self.rx,self.h); self.Y=(self.z*4+self.ry,self.h)
        self.up=(self.b+4,self.h); self.dn=(self.b-4,self.h); self.twin=(self.b,1-self.h)
    def barrier(self):
        bar=pltpu.get_barrier_semaphore()
        for d in (self.X,self.Y,self.twin):
            pl.semaphore_signal(bar,inc=1,device_id=d,device_id_type=MESH)
        @pl.when(self.z<self.nz-1)
        def _(): pl.semaphore_signal(bar,inc=1,device_id=self.up,device_id_type=MESH)
        @pl.when(self.z>0)
        def _(): pl.semaphore_signal(bar,inc=1,device_id=self.dn,device_id_type=MESH)
        lines=jnp.where(self.z<self.nz-1,1,0)+jnp.where(self.z>0,1,0)
        pl.semaphore_wait(bar,3+lines)

def rc(src,dst,ss,rs,dev):
    return pltpu.make_async_remote_copy(src_ref=src,dst_ref=dst,send_sem=ss,recv_sem=rs,device_id=dev,device_id_type=MESH)

class Gather:
    def __init__(self, pc, g, ss, rs):
        self.pc=pc; self.g=g; self.ss=ss; self.rs=rs; self.n=2*(pc.nz-1)
    def cz(self,p,zz,k,dev):
        s=self.g.at[p,zz,self.pc.r]
        return rc(s,s,self.ss.at[p,k],self.rs.at[p,k],dev)
    def z0(self,p):
        c=self.pc
        @pl.when(c.z<c.nz-1)
        def _(): self.cz(p,c.z,0,c.up).start()
        @pl.when(c.z>0)
        def _(): self.cz(p,c.z,1,c.dn).start()
    def zk(self,p,d):
        c=self.pc
        @pl.when(c.z-d>=0)
        def _():
            self.cz(p,c.z-d,2*(d-1),c.up).wait_recv()
        if d<c.nz-1:
            @pl.when((c.z-d>=0)&(c.z<c.nz-1))
            def _(): self.cz(p,c.z-d,2*d,c.up).start()
        @pl.when(c.z+d<c.nz)
        def _():
            self.cz(p,c.z+d,2*(d-1)+1,c.dn).wait_recv()
        if d<c.nz-1:
            @pl.when((c.z+d<c.nz)&(c.z>0))
            def _(): self.cz(p,c.z+d,2*d+1,c.dn).start()
    def cb(self,p,r,k,dev):
        s=self.g.at[p,:,r]
        return rc(s,s,self.ss.at[p,self.n+k],self.rs.at[p,self.n+k],dev)
    def ch(self,p,r,lo,k,dev):
        h=self.pc.nz//2
        s=self.g.at[p,pl.ds(0,h),r] if lo else self.g.at[p,pl.ds(h,self.pc.nz-h),r]
        return rc(s,s,self.ss.at[p,self.n+k],self.rs.at[p,self.n+k],dev)
    def x0(self,p):
        c=self.pc
        self.cb(p,c.r,0,c.X).start(); self.cb(p,c.r,1,c.Y).start()
    def x1(self,p):
        c=self.pc
        self.cb(p,c.rx,0,c.X).wait_recv()
        self.ch(p,c.rx,True,2,c.Y).start()
        self.cb(p,c.ry,1,c.Y).wait_recv()
        self.ch(p,c.ry,False,3,c.X).start()
    def x2(self,p):
        c=self.pc
        self.ch(p,c.rd,True,2,c.Y).wait_recv()
        self.ch(p,c.rd,False,3,c.X).wait_recv()
    def drain(self,p):
        c=self.pc
        for d in range(c.nz-1):
            @pl.when((c.z-d>=0)&(c.z<c.nz-1))
            def _(): self.cz(p,c.z-d,2*d,c.up).wait_send()
            @pl.when((c.z+d<c.nz)&(c.z>0))
            def _(): self.cz(p,c.z+d,2*d+1,c.dn).wait_send()
        self.cb(p,c.r,0,c.X).wait_send(); self.cb(p,c.r,1,c.Y).wait_send()
        self.ch(p,c.rx,True,2,c.Y).wait_send(); self.ch(p,c.ry,False,3,c.X).wait_send()
    def steps(self):
        nz=self.pc.nz
        def last(p):
            self.zk(p,nz-1); self.x0(p)
        return [self.z0]+[functools.partial(lambda d,p:self.zk(p,d),d) for d in range(1,nz-1)]+[last]+[NOP]+[self.x1]+[NOP]+[self.x2]

class PlaneFirst(Gather):
    def cz(self,p,zz,k,dev):
        s=self.g.at[p,zz]
        return rc(s,s,self.ss.at[p,k],self.rs.at[p,k],dev)
    def cb(self,p,r,k,dev):
        s=self.g.at[p,self.pc.z,r]
        return rc(s,s,self.ss.at[p,self.n+k],self.rs.at[p,self.n+k],dev)
    def ch(self,p,r,lo,k,dev):
        n=self.g.shape[3]; h=(n//32)*16
        s=self.g.at[p,self.pc.z,r,pl.ds(0,h)] if lo else self.g.at[p,self.pc.z,r,pl.ds(h,n-h)]
        return rc(s,s,self.ss.at[p,self.n+k],self.rs.at[p,self.n+k],dev)

class Scatter:
    def __init__(self, pc, g, d, rx, ry, ru, rd, ss, rs, slot=lambda p: p):
        self.pc=pc;self.g=g;self.d=d;self.bx=rx;self.by=ry;self.bu=ru;self.bd=rd;self.ss=ss;self.rs=rs
        self.h=pc.nz//2; self.slot=slot
    def half(self,p,r,lo):
        h=self.h; n=self.pc.nz
        return (self.g.at[p,pl.ds(0,h),r],self.d.at[self.slot(p),pl.ds(0,h)]) if lo else (self.g.at[p,pl.ds(h,n-h),r],self.d.at[self.slot(p),pl.ds(h,n-h)])
    def c0(self,p,lo):
        s,t=self.half(p,self.pc.rd,lo); k=0 if lo else 1
        return rc(s,t,self.ss.at[self.slot(p),k],self.rs.at[self.slot(p),k],self.pc.X if lo else self.pc.Y)
    def c1(self,p,x):
        c=self.pc
        return rc(self.g.at[p,:,c.rx if x else c.ry],(self.bx if x else self.by).at[self.slot(p)],self.ss.at[self.slot(p),2 if x else 3],self.rs.at[self.slot(p),2 if x else 3],c.X if x else c.Y)
    def cu(self,p,zz,up):
        c=self.pc; k=4+zz if up else 4+c.nz+zz
        return rc(self.g.at[p,zz,c.r],(self.bu if up else self.bd).at[self.slot(p),zz],self.ss.at[self.slot(p),k],self.rs.at[self.slot(p),k],c.up if up else c.dn)
    def add(self,dst,*srcs):
        v=dst[...].astype(F32)
        for s in srcs: v=v+s[...].astype(F32)
        dst[...]=v.astype(BF)
    def s0(self,p):
        self.c0(p,True).start(); self.c0(p,False).start()
    def s1(self,p):
        c=self.pc;h=self.h;n=c.nz
        self.c0(p,True).wait_recv()
        self.add(self.g.at[p,pl.ds(0,h),c.ry],self.d.at[self.slot(p),pl.ds(0,h)])
        self.c1(p,False).start()
        self.c0(p,False).wait_recv()
        self.add(self.g.at[p,pl.ds(h,n-h),c.rx],self.d.at[self.slot(p),pl.ds(h,n-h)])
        self.c1(p,True).start()
    def s2(self,p):
        c=self.pc
        self.c1(p,True).wait_recv(); self.c1(p,False).wait_recv()
        self.add(self.g.at[p,:,c.r],self.bx.at[self.slot(p)],self.by.at[self.slot(p)])
        self.zk(p,0)
    def zk(self,p,k):
        c=self.pc; nz=c.nz
        @pl.when(c.z==k)
        def _():
            for zz in range(nz-1,k,-1):
                if k>0:
                    self.cu(p,zz,True).wait_recv()
                    self.add(self.g.at[p,zz,c.r],self.bu.at[self.slot(p),zz])
                self.cu(p,zz,True).start()
        @pl.when(c.z==nz-1-k)
        def _():
            for zz in range(0,nz-1-k):
                if k>0:
                    self.cu(p,zz,False).wait_recv()
                    self.add(self.g.at[p,zz,c.r],self.bd.at[self.slot(p),zz])
                self.cu(p,zz,False).start()
    def fin(self,p,tot,place=None):
        c=self.pc
        tot[...]=self.g[p,c.z,c.r].astype(F32)
        @pl.when(c.z>0)
        def _():
            self.cu(p,c.z,True).wait_recv()
            tot[...]+=self.bu[self.slot(p),c.z].astype(F32)
        @pl.when(c.z<c.nz-1)
        def _():
            self.cu(p,c.z,False).wait_recv()
            tot[...]+=self.bd[self.slot(p),c.z].astype(F32)
        if place is not None: place(p)
    def drain(self,p):
        c=self.pc; nz=c.nz
        self.c0(p,True).wait_send(); self.c0(p,False).wait_send()
        self.c1(p,True).wait_send(); self.c1(p,False).wait_send()
        for zz in range(nz):
            @pl.when(zz>c.z)
            def _(): self.cu(p,zz,True).wait_send()
            @pl.when(zz<c.z)
            def _(): self.cu(p,zz,False).wait_send()
    def lines(self):
        return [functools.partial(lambda k,p:self.zk(p,k),k) for k in range(1,self.pc.nz-1)]
    def steps(self,place,tot):
        return [self.s0,NOP,self.s1,NOP,self.s2]+self.lines()+[lambda p:self.fin(p,tot,place)]
    def tight(self,out):
        return [self.s0,self.s1,self.s2]+self.lines()+[lambda p:self.fin(p,out.at[0])]


EPS = 1e-5
RT = 256


def pick(static, cond, body):
    if isinstance(cond, (bool, int)):
        if cond:
            body()
    else:
        pl.when(cond)(body)


def norm_rows(values):
    mean = jnp.mean(values, axis=1, keepdims=True)
    centred = values - mean
    inverse = lax.rsqrt(jnp.mean(centred * centred, axis=1, keepdims=True) + EPS)
    return centred * inverse, inverse


def gelu_both(u):
    c = 0.7978845608028654
    u2 = u * u
    t = jnp.tanh(c * u * (1.0 + 0.044715 * u2))
    half = 0.5 + 0.5 * t
    act = u * half
    grad = half + (0.5 * c) * u * (1.0 - t * t) * (1.0 + (3 * 0.044715) * u2)
    return act, grad


def flat(ref, p):
    v = ref[p]
    return v.reshape(-1, v.shape[-1])


def tiles(n):
    return lambda f: pl.loop(0, n)(f)


def rows_of(i, n=RT):
    return pl.ds(pl.multiple_of(i * n, n), n)


def twin_copy(pc, src, dst, ss, rs):
    return rc(src, dst, ss, rs, pc.twin)


def members(cl, hh):
    return jnp.where(cl[hh] == sub((128, L)), 1.0, 0.0).astype(BF)


def pair_members(cl, p):
    return jnp.concatenate([members(cl, 2 * p), members(cl, 2 * p + 1)], 0)


def pair_own():
    return (lane((256, 128)) >= 64) == (sub((256, 128)) >= 128)


def fwd_clusters(p, qkv, cl, n_s, seg, prob_o):
    q = qkv[p, :, 0:128]
    k = qkv[p, :, 128:256]
    v = qkv[p, :, 256:384]
    own = pair_own()
    mt = pair_members(cl, p)
    cnt = jnp.maximum(jnp.sum(mt.astype(F32), axis=1, keepdims=True), 1.0)
    cen = jnp.where(own, dot(mt, q) / cnt, 0.0).astype(BF)
    s = dot((cen.astype(F32) * 0.125).astype(BF), k, NT)
    top = jnp.concatenate([jnp.transpose(n_s[2 * p + h]).astype(F32) for h in range(2)], 0) == 0.0
    c = sub((256, 1))
    cm = lax.rem(jnp.where(c < 128, c, c - 128), jnp.int32(10))
    s = jnp.where(seg[...] == cm, s, -BIG)
    e = jnp.exp(s - jnp.max(s, axis=1, keepdims=True))
    prob = e / jnp.sum(e, axis=1, keepdims=True)
    mass = jnp.sum(jnp.where(top, prob, 0.0), axis=1, keepdims=True)
    signed = jnp.where(top, -prob, prob).astype(BF)
    prob_o[2 * p] = signed[0:128]
    prob_o[2 * p + 1] = signed[128:256]
    rest = dot(jnp.where(top, 0.0, prob).astype(BF), v)
    rh, rl = split2(jnp.where(own, rest, jnp.broadcast_to(mass, (256, 128))))
    rr = jnp.concatenate([rh, rl], 1)
    return rr[0:128], rr[128:256]


def fwd_head(p, h, rr, qkv, mb, n_s, qaug, kaug, att, ex):
    odd = h == 1
    hh = 2 * p + h
    k = qkv[p, :, 128:256]
    ln = lane((L, 128))
    mine = (ln >= 64) if odd else (ln < 64)
    zero = jnp.zeros((), BF)
    vaug = jnp.where(mine, qkv[p, :, 256:384], jnp.ones((), BF))
    qaug[:, :128] = (jnp.where(mine, qkv[p, :, 0:128], zero).astype(F32) * 0.125).astype(BF)
    qaug[:, 128:] = mb[hh]
    kaug[:, :128] = k
    kaug[:, 128:] = n_s[hh]
    lt = lane((TQ, 128))
    minet = (lt >= 64) if odd else (lt < 64)
    cols = pl.ds(pl.multiple_of(p * 128, 128), 128)
    for t in range(L // TQ):
        sl = pl.ds(t * TQ, TQ)
        sc = dot(qaug[sl, :], kaug[...], NT)
        mm = jnp.max(sc, axis=1, keepdims=True)
        pr = jnp.exp(sc - mm).astype(BF)
        o = dot(pr, vaug)
        mt_ = qaug[sl, 128:]
        ee = dot(mt_, rr)
        ee = ee[:, :128] + ee[:, 128:]
        osw = pltpu.roll(o, 64, 1)
        esw = pltpu.roll(ee, 64, 1)
        exact = o / osw
        a = exact * esw + ee
        tot = jnp.where(minet, osw, o)
        ms = jnp.where(minet, esw, ee)
        lse = mm + jnp.log(tot) - jnp.log(jnp.maximum(ms, 1e-37))
        h3, m3, l3 = split3(lse)
        mb[hh, sl, :] = jnp.where(lt == 100, h3.astype(F32), jnp.where(lt == 101, m3.astype(F32), jnp.where(lt == 102, l3.astype(F32), mt_.astype(F32)))).astype(BF)
        if odd:
            att[sl, cols] = jnp.where(lt < 64, att[sl, cols], a.astype(BF))
            ex[sl, cols] = jnp.where(lt < 64, ex[sl, cols], exact.astype(BF))
        else:
            att[sl, cols] = a.astype(BF)
            ex[sl, cols] = exact.astype(BF)


def as_column(row):
    n = row.shape[1]
    eye = sub((n, n)) == lane((n, n))
    return jnp.sum(jnp.where(eye, row.astype(F32), 0.0), axis=1, keepdims=True)


def fill_own(pc, g, gg, q3, oT, upw, dT, ga, gf):
    for p in range(3):
        for i in range(3):
            g[p, pc.z, pc.r, :, i * 128:(i + 1) * 128] = q3[i, :, p * 128:(p + 1) * 128]
    g[3, pc.z, pc.r] = oT[...]
    for q in range(4):
        g[4 + q, pc.z, pc.r] = upw[:, q * 384:(q + 1) * 384]
        g[8 + q, pc.z, pc.r] = dT[:, q * 384:(q + 1) * 384]
    R = oT.shape[0]
    ln = lane((R, 128))
    gg[0, pc.z, pc.r] = jnp.where(ln == 0, as_column(ga[...]), jnp.where(ln == 1, as_column(gf[...]), 0.0)).astype(BF)


def bwd_clusters(p, cl, s, gaugs, dq_o, dk_o, dv_o):
    qkv = s["qkv"]
    cols = pl.ds(pl.multiple_of(p * 128, 128), 128)
    qv = qkv[p, :, 0:128]
    kv = qkv[p, :, 128:256]
    vv = qkv[p, :, 256:384]
    gv = s["gatt"][:, cols]
    ln = lane((L, 128))
    lc = lane((256, 128))
    row = sub((256, 128))
    own = pair_own()
    prod = gv.astype(F32) * s["ex"][:, cols].astype(F32)
    dots = jnp.zeros((L, 128), F32)
    for h in range(2):
        mine = (ln >= 64) if h else (ln < 64)
        o = 0 if h else 64
        three = [a.astype(F32) for a in split3(jnp.sum(jnp.where(mine, prod, 0.0), axis=1, keepdims=True))]
        ga = jnp.where(mine, gv.astype(F32), 0.0)
        for i, a in enumerate(three):
            ga = jnp.where(ln == o + i, a, ga)
            dots = jnp.where(ln == 3 * h + i, a, dots)
        gaugs[h][...] = ga.astype(BF)
    mt = pair_members(cl, p)
    cnt = jnp.maximum(jnp.sum(mt.astype(F32), axis=1, keepdims=True), 1.0)
    cq = dot(mt, jnp.concatenate([qv, gv], 1))
    cen = jnp.where(own, cq[:, 0:128] / cnt, 0.0).astype(BF)
    cs = (cen.astype(F32) * 0.125).astype(BF)
    grest = jnp.where(own, cq[:, 128:256], 0.0).astype(BF)
    gm = dot(mt, dots.astype(BF))
    lo = jnp.where(row >= 128, 3, 0)
    gmass = jnp.sum(jnp.where((lc >= lo) & (lc < lo + 3), gm, 0.0), axis=1, keepdims=True)
    signed = jnp.concatenate([s["prob"][2 * p], s["prob"][2 * p + 1]], 0).astype(F32)
    top = signed < 0.0
    prob = jnp.abs(signed)
    gp = jnp.where(top, gmass, dot(grest, vv, NT))
    gs = (prob * (gp - jnp.sum(prob * gp, axis=1, keepdims=True))).astype(BF)
    rw = jnp.where(top, 0.0, prob).astype(BF)
    gcen = jnp.where(own, dot(gs, kv) / cnt, 0.0)
    gh, gl = split2(gcen)
    dk_o[...] = dot(jnp.transpose(gs), cs)
    dv_o[...] = dot(jnp.transpose(rw), grest)
    zero = jnp.zeros((), BF)
    two = jnp.concatenate([jnp.where(ln < 100, s["mb"][2 * p + h], zero) for h in range(2)], 1)
    dd = dot(two, jnp.concatenate([gh, gl], 1))
    dq_o[...] = dd[:, :128] + dd[:, 128:]


def bwd_head(p, h, s, qaug, kaug, gaug, vaug, dk_o, dv_o, dqt):
    qkv = s["qkv"]
    hh = 2 * p + h
    cols = pl.ds(pl.multiple_of(p * 128, 128), 128)
    kv = qkv[p, :, 128:256]
    ln = lane((L, 128))
    zero = jnp.zeros((), BF)
    mine = (ln >= 64) if h else (ln < 64)
    o = 0 if h else 64
    gm = jnp.where(mine, s["gatt"][:, cols], zero)
    vaug[...] = jnp.where(mine, qkv[p, :, 256:384], jnp.where((ln >= o) & (ln < o + 3), jnp.full((), -1.0, BF), zero))
    qs = (jnp.where(mine, qkv[p, :, 0:128], zero).astype(F32) * 0.125).astype(BF)
    qaug[:, :128] = qs
    qaug[:, 128:] = s["mb"][hh]
    kaug[:, :128] = kv
    kaug[:, 128:] = s["ns"][hh]
    kTh = jnp.transpose(kv)[64 * h:64 * h + 64]
    for t in range(L // TJ):
        sl = pl.ds(t * TJ, TJ)
        pr = jnp.exp(dot(kaug[sl, :], qaug[...], NT))
        ds = (pr * dot(vaug[sl, :], gaug[...], NT)).astype(BF)
        dv_o[sl, :] += dot(pr.astype(BF), gm)
        dk_o[sl, :] += dot(ds, qs)
        dqp = dot(kTh[:, t * TJ:(t + 1) * TJ], ds)
        if t == 0:
            dqt[64 * h:64 * h + 64, :] = dqp
        else:
            dqt[64 * h:64 * h + 64, :] += dqp


def place_sum(p, tot, outs):
    qg, og, ug, dg = outs

    def pair(p):
        for i in range(3):
            qg[i, :, pl.ds(pl.multiple_of(p * 128, 128), 128)] = tot[:, i * 128:(i + 1) * 128]

    def wide(ref, q):
        ref[:, pl.ds(pl.multiple_of(q * 384, 128), 384)] = tot[...]

    pick(None, p < 3, lambda: pair(p))
    pick(None, p == 3, lambda: og.__setitem__(..., tot[...]))
    pick(None, (3 < p < 8) if isinstance(p, int) else (p > 3) & (p < 8), lambda: wide(ug, p - 4))
    pick(None, p >= 12, lambda: wide(dg, p - 12))


def finish_body(*refs):
    ins, gg, outs, (g1, g2), bufs, (si, so) = refs[:6], refs[6], refs[7:13], refs[13:15], refs[15:21], refs[21:]
    ci = [pltpu.make_async_copy(a, b, si.at[i]) for i, (a, b) in enumerate(zip(ins, bufs))]
    co = [pltpu.make_async_copy(a, b, so.at[i]) for i, (a, b) in enumerate(zip(bufs, outs))]
    for c in ci:
        c.start()
    R = gg.shape[1]
    eye = sub((R, R)) == lane((R, R))
    for i, g in enumerate((g1, g2)):
        g[...] = jnp.sum(jnp.where(eye, gg[0, :, i:i + 1], 0.0), axis=0, keepdims=True)
    for a, b in zip(ci, co):
        a.wait()
        b.start()
    for c in co:
        c.wait()


def finish(*arrays):
    V = pl.BlockSpec(memory_space=pltpu.VMEM)
    A = pl.BlockSpec(memory_space=pl.ANY)
    R = arrays[6].shape[1]
    dma = pltpu.SemaphoreType.DMA
    return pl.pallas_call(
        finish_body,
        out_shape=[jax.ShapeDtypeStruct(a.shape, a.dtype) for a in arrays[:6]] + [jax.ShapeDtypeStruct((1, R), F32)] * 2,
        in_specs=[A] * 6 + [V], out_specs=[A] * 6 + [V] * 2,
        scratch_shapes=[pltpu.VMEM(a.shape, a.dtype) for a in arrays[:6]] + [dma((6,)), dma((6,))],
        compiler_params=pltpu.CompilerParams(vmem_limit_bytes=60 << 20),
    )(*arrays)


def scratch_shapes(custom, nz, R):
    f = lambda *s: (s, F32)
    b = lambda *s: (s, BF)
    wide = (16, nz, 4, R, 384) if custom else (16, 768, 384)
    return {
        "gr": f(8, 768), "n1": b(L, 768), "qkv": b(3, L, 384), "att": b(L, 384), "ex": b(L, 384), "mb": b(6, L, 128),
        "ns": b(6, L, 128), "prob": b(6, 128, L), "hid": f(L, 768), "n2": b(L, 768), "act": b(4, L, 384), "dg": b(4, L, 384),
        "aT": b(768, L), "ghs": f(L // 2, 768), "eb": b(L, 768), "er": b(L, 768), "fr": b(L // 2, 768), "gatt": b(L, 384),
        "dqkv": b(L, 384), "qaug": b(L, 256), "kaug": b(L, 256), "gaug": b(L, 128), "gaug1": b(L, 128), "vaug": b(L, 128),
        "dqs": f(L, 128), "dks": f(L, 128), "dvs": f(L, 128), "dqt": f(128, L), "gacc": f(8, 768),
        "wg": b(*wide),
    }


def layer_body(nb, custom, names, *refs):
    refs = list(refs)
    take = lambda n: [refs.pop(0) for _ in range(n)]
    x, ct, seg, cl, tt = take(5)
    own = take(6 if custom else 2)
    y, tg, out_g = take(3)
    out_s = take(4) if custom else take(1)[0]
    s = dict(zip(names, take(len(names))))
    tpad, es, ers, vs, vrs = take(5)
    pc = Place(nb)
    wg, hid, n1, n2, qkv, att, ex, act, dg = (s[n] for n in ("wg", "hid", "n1", "n2", "qkv", "att", "ex", "act", "dg"))
    aT, eb, er, fr, gr, gacc = (s[n] for n in ("aT", "eb", "er", "fr", "gr", "gacc"))
    half, nh, nt = L // 2, L // 2 // RT, L // RT

    if custom:
        gg, tot, gbuf, ss, rs, gss, grs, ss2, rs2, gss2, grs2, gown, gtwin = take(13)
        land, gland = take(5), take(5)
        G, Gg = Gather(pc, wg, ss, rs), Gather(pc, gg, gss, grs)
        S = Scatter(pc, wg, *land, ss2, rs2, slot=lambda p: p - 4 if isinstance(p, int) and p >= 12 else p if isinstance(p, int) else jnp.where(p >= 12, p - 4, p))
        Sg = Scatter(pc, gbuf, *gland, gss2, grs2)
        Gp = PlaneFirst(pc, wg, ss, rs)
        m = pc.nz - 1

        def last(p):
            G.zk(p, m)
            G.x0(p)

        def turn(p):
            Gp.x2(p)
            Gp.z0(p)
        line = lambda g, off: [(off + d, functools.partial(lambda d, p: g.zk(p, d), d)) for d in range(1, m)][::-1]
        nine = lambda k: k + k // 3
        three = lambda k: k + 3
        rest = list(range(1, 9))
        gather = [(m + 2, G.x2, [0], nine), (m + 1, G.x1, [0], nine), (m + 3, G.x2, rest, nine), (m + 2, G.x1, rest, nine)]
        gather += [(e, fn, list(range(9)), nine) for e, fn in [(m, last)] + line(G, 0) + [(0, G.z0)]]
        gather += [(e, fn, [0, 4, 8], three) for e, fn in [(m + 3, lambda p: Gp.zk(p, m))] + line(Gp, 3) + [(2, turn), (1, Gp.x1), (0, Gp.x0)]]
        gsteps = [Gg.z0] + [functools.partial(lambda d: Gg.zk(0, d), d) for d in range(1, m)] + [None, Gg.x1, Gg.x2]
        ssteps = S.steps(lambda p: place_sum(p, tot, out_s), tot)
        tails = Sg.tight(gown)
        starts = {13: 12, 14: 13, 15: 14, 16: 15, 17: 4, 18: 5, 19: 6, 20: 7, 21: 3, 22: 0, 23: 1, 25: 2}

        def tick(t, span=None):
            fixed = isinstance(t, int)
            ts = [t] if fixed else list(range(*span))
            for i in range(len(ssteps) - 1, -1, -1):
                hits = [u - i for u in ts if u - i in starts]
                if not hits or ssteps[i] is NOP:
                    continue
                if fixed:
                    ssteps[i](starts[hits[0]])
                    continue
                u = t - i
                ok = functools.reduce(jnp.logical_or, [u == k for k in hits])
                part = functools.reduce(lambda a, k: jnp.where(u == k, starts[k], a), hits, 0)
                pl.when(ok)(lambda i=i, part=part: ssteps[i](part))
            for off, fn, at, to in gather:
                hits = [u - off for u in ts if u - off in at]
                if not hits:
                    continue
                u = t - off
                ok = True if fixed else functools.reduce(jnp.logical_or, [u == k for k in hits])
                pick(None, ok, lambda fn=fn, p=to(u): fn(p))
            if fixed and t < len(gsteps):
                if t == m:
                    Gg.zk(0, m)
                    Gg.x0(0)
                elif t == 0:
                    gsteps[0](0)
                elif t < m:
                    gsteps[t]()
                else:
                    gsteps[t](0)
    else:
        tick = lambda t, span=None: None

    tpad[...] = jnp.full_like(tpad, -1)
    pc.barrier()
    if custom:
        fill_own(pc, wg, gg, *own)
    tick(0)

    @tiles(nt)
    def _(i):
        hid[rows_of(i), :] = norm_rows(x[rows_of(i), :].astype(F32))[0]

    tick(1)

    def mask(h):
        tpad[:, 0:tt.shape[2]] = tt[h]
        a, n = build_masks(cl[h], tpad[...])
        s["mb"][h], s["ns"][h] = a, n

    def transpose_into(src):
        for i in range(nt):
            aT[:, i * RT:(i + 1) * RT] = jnp.transpose(src[i * RT:(i + 1) * RT, :])

    def put(p, left, right):
        wg[p] = dot(left, right).astype(BF).reshape(wg.shape[1:])

    pl.loop(0, 2)(mask)
    tick(2)
    pl.loop(2, 4)(mask)
    tick(3)
    pl.loop(4, 6)(mask)
    transpose_into(ct)
    tick(4)
    tick(5)
    if custom:
        gains = gg[0].reshape(768, 128)
    else:
        c = pltpu.make_async_copy(own[0], wg.at[0:12], vs)
        c.start()
        c.wait()
        gains = own[1][...]
    gr[...] = jnp.transpose(gains.astype(F32))[0:8]

    @tiles(nt)
    def _(i):
        n1[rows_of(i), :] = (hid[rows_of(i), :] * gr[0:1, :]).astype(BF)

    @pl.loop(0, 3)
    def _(p):
        @tiles(nt)
        def _(i):
            qkv[p, rows_of(i), :] = dot(n1[rows_of(i), :], flat(wg, p)).astype(BF)
        rr = fwd_clusters(p, qkv, cl, s["ns"], seg, s["prob"])
        for h in range(2):
            tick(6 + 2 * p + h, (6 + h, 12, 2))
            fwd_head(p, h, rr[h], qkv, s["mb"], s["ns"], s["qaug"], s["kaug"], att, ex)

    def send(k, src, dst, i):
        return twin_copy(pc, src.at[rows_of(i)], dst.at[rows_of(i)], es.at[k + i], ers.at[k + i])

    @tiles(nt)
    def _(i):
        eb[rows_of(i), :] = dot(att[rows_of(i), :], flat(wg, 3), NT).astype(BF)
        send(0, eb, er, i).start()

    tick(12)

    @tiles(nt)
    def _(i):
        r = rows_of(i)
        send(0, eb, er, i).wait()
        hv = x[r, :].astype(F32) + (eb[r, :].astype(F32) + er[r, :].astype(F32))
        hid[r, :] = hv
        n2[r, :] = (norm_rows(hv)[0] * gr[1:2, :]).astype(BF)

    def up(q):
        @tiles(nt)
        def _(i):
            a, d = gelu_both(dot(n2[rows_of(i), :], flat(wg, 4 + q)))
            act[q, rows_of(i), :] = a.astype(BF)
            dg[q, rows_of(i), :] = d.astype(BF)

    def down_grad(q):
        up(q)
        put(12 + q, aT[...], act[q])

    pl.loop(0, 2)(down_grad)
    tick(13)
    pl.loop(2, 4)(down_grad)
    tick(14)
    transpose_into(n2)

    def part(i):
        acc = dot(act[0, rows_of(i), :], flat(wg, 8), NT)
        for q in range(1, 4):
            acc += dot(act[q, rows_of(i), :], flat(wg, 8 + q), NT)
        return acc

    @tiles(nh)
    def _(i):
        eb[rows_of(i), :] = part((1 - pc.h) * nh + i).astype(BF)
        send(4, eb, fr, i).start()

    tick(15)

    @pl.loop(0, 4)
    def _(q):
        @tiles(nt)
        def _(i):
            ga = dot(ct[rows_of(i), :], flat(wg, 8 + q))
            dg[q, rows_of(i), :] = (ga * dg[q, rows_of(i), :].astype(F32)).astype(BF)

    @tiles(nh)
    def _(i):
        acc = part(pc.h * nh + i).astype(BF).astype(F32)
        send(4, eb, fr, i).wait()
        y[rows_of(i), :] = (hid[rows_of(pc.h * nh + i), :] + (acc + fr[rows_of(i), :].astype(F32))).astype(BF)

    tick(16)
    if custom:
        @pl.loop(0, 9)
        def _(k):
            G.drain(nine(k))

        @pl.loop(0, 3)
        def _(k):
            Gp.drain(4 * k + 3)
        Gg.drain(0)

    @tiles(nt)
    def _(i):
        acc = dot(dg[0, rows_of(i), :], flat(wg, 4), NT)
        for q in range(1, 4):
            acc += dot(dg[q, rows_of(i), :], flat(wg, 4 + q), NT)
        eb[rows_of(i), :] = acc.astype(BF)
        send(6, eb, er, i).start()

    def up_grad(q):
        put(4 + q, aT[...], dg[q])

    pl.loop(0, 4)(up_grad)
    tick(17)
    gacc[...] = jnp.zeros_like(gacc)
    gat = n2

    @tiles(nt)
    def _(i):
        r = rows_of(i)
        send(6, eb, er, i).wait()
        gn = eb[r, :].astype(F32) + er[r, :].astype(F32)
        n, inv = norm_rows(hid[r, :])
        a = gn * gr[1:2, :]
        back = (a - jnp.mean(a, axis=1, keepdims=True) - n * jnp.mean(a * n, axis=1, keepdims=True)) * inv
        gh = ct[r, :].astype(F32) + back
        gat[r, :] = gh.astype(BF)

        @pl.when((i >= pc.h * nh) & (i < pc.h * nh + nh))
        def _():
            s["ghs"][rows_of(i - pc.h * nh), :] = gh
            gacc[1:2, :] += jnp.sum(gn * n, axis=0, keepdims=True)

    tick(18)

    @tiles(nt)
    def _(i):
        s["gatt"][rows_of(i), :] = dot(gat[rows_of(i), :], flat(wg, 3)).astype(BF)

    transpose_into(gat)
    put(3, aT[...], att[...])
    tick(19)
    transpose_into(n1)
    nacc = hid
    dqkv = s["dqkv"]

    @pl.loop(0, 3)
    def _(p):
        bwd_clusters(p, cl, s, (s["gaug"], s["gaug1"]), s["dqs"], s["dks"], s["dvs"])
        bwd_head(p, 0, s, s["qaug"], s["kaug"], s["gaug"], s["vaug"], s["dks"], s["dvs"], s["dqt"])
        tick(20 + 2 * p, (20, 26, 2))
        bwd_head(p, 1, s, s["qaug"], s["kaug"], s["gaug1"], s["vaug"], s["dks"], s["dvs"], s["dqt"])
        dqkv[:, 0:128] = ((s["dqs"][...] + jnp.transpose(s["dqt"][...])) * 0.125).astype(BF)
        dqkv[:, 128:256] = s["dks"][...].astype(BF)
        dqkv[:, 256:384] = s["dvs"][...].astype(BF)

        @tiles(nt)
        def _(i):
            v = dot(dqkv[rows_of(i), :], flat(wg, p), NT)

            @pl.when(p == 0)
            def _():
                nacc[rows_of(i), :] = v

            @pl.when(p > 0)
            def _():
                nacc[rows_of(i), :] += v
        put(p, aT[...], dqkv[...])
        tick(21 + 2 * p, (21, 27, 2))

    @tiles(nh)
    def _(i):
        eb[rows_of(i), :] = nacc[rows_of((1 - pc.h) * nh + i), :].astype(BF)
        send(10, eb, fr, i).start()

    @tiles(nt)
    def _(i):
        n = norm_rows(x[rows_of(i), :].astype(F32))[0]
        gacc[0:1, :] += jnp.sum(nacc[rows_of(i), :] * n, axis=0, keepdims=True)

    if custom:
        wide = jnp.concatenate([gacc[...], jnp.zeros((120, 768), F32)], 0)
        gbuf[0] = jnp.transpose(wide).astype(BF).reshape(gbuf.shape[1:])

    def late(t):
        tick(t)
        if custom and t - 26 < len(tails):
            tails[t - 26](0)

    late(26)
    late(27)

    @tiles(nh)
    def _(i):
        r = rows_of(i)
        send(10, eb, fr, i).wait()
        gn = nacc[rows_of(pc.h * nh + i), :].astype(BF).astype(F32) + fr[r, :].astype(F32)
        n, inv = norm_rows(x[rows_of(pc.h * nh + i), :].astype(F32))
        a = gn * gr[0:1, :]
        back = (a - jnp.mean(a, axis=1, keepdims=True) - n * jnp.mean(a * n, axis=1, keepdims=True)) * inv
        tg[r, :] = s["ghs"][r, :] + back

    if custom:
        for t in range(28, max(25 + len(ssteps), 26 + len(tails))):
            late(t)
            if t == 25 + len(tails):
                cv = twin_copy(pc, gown, gtwin, vs, vrs)
                cv.start()

        @pl.loop(0, 12)
        def _(i):
            S.drain(jnp.where(i < 8, i, i + 4))
        Sg.drain(0)
        cv.wait()
        out_g[0] = gown[0] + gtwin[0]
    else:
        c = pltpu.make_async_copy(wg, out_s, vs)
        c.start()
        out_g[...] = gacc[...]
        c.wait()


def layer(nb, custom, *args):
    V = pl.BlockSpec(memory_space=pltpu.VMEM)
    A = pl.BlockSpec(memory_space=pl.ANY)
    nz = nb // 4
    dma = pltpu.SemaphoreType.DMA
    tt, ws = args[4], args[5:]
    R = ws[1].shape[0]
    shapes = scratch_shapes(custom, nz, R)
    out_shape = [jax.ShapeDtypeStruct((L // 2, 768), BF), jax.ShapeDtypeStruct((L // 2, 768), F32)]
    if custom:
        out_shape += [jax.ShapeDtypeStruct(sh, F32) for sh in ((1, R, 128), (3, R, 384), (R, 384), (R, 1536), (R, 1536))]
        out_specs = [V] * 7
        in_specs = [V] * len(args)
    else:
        out_shape += [jax.ShapeDtypeStruct((8, 768), F32), jax.ShapeDtypeStruct(shapes["wg"][0], BF)]
        out_specs = [V, V, V, A]
        in_specs = [V] * 5 + [A, V]
    scratch = [pltpu.VMEM(*sd) for sd in shapes.values()] + [pltpu.VMEM((tt.shape[1], 128), jnp.int32), dma((12,)), dma((12,)), dma, dma]
    if custom:
        ns, n2 = 2 * (nz - 1) + 4, 4 + 2 * nz
        vb = lambda *sh: pltpu.VMEM(sh, BF)
        scratch += [vb(1, nz, 4, R, 128), pltpu.VMEM((R, 384), F32), vb(1, nz, 4, R, 128), dma((12, ns)), dma((12, ns)), dma((1, ns)), dma((1, ns)),
                    dma((12, n2)), dma((12, n2)), dma((1, n2)), dma((1, n2)), pltpu.VMEM((1, R, 128), F32), pltpu.VMEM((1, R, 128), F32)] + [vb(12, nz, R, 384)] * 5 + [vb(1, nz, R, 128)] * 5
    return pl.pallas_call(
        functools.partial(layer_body, nb, custom, tuple(shapes)),
        out_shape=out_shape, in_specs=in_specs, out_specs=out_specs, scratch_shapes=scratch,
        compiler_params=pltpu.CompilerParams(collective_id=0, has_side_effects=True, vmem_limit_bytes=int(63.9 * (1 << 20))),
    )(*args)


def on_device(tokens, attn_gain, qkv_weight, out_weight, ffn_gain, up_weight, down_weight, cotangent, segment, cluster, top_keys):
    nb = lax.axis_size("batch")
    R = qkv_weight.shape[0]
    custom = R % 16 == 0 and nb % 4 == 0
    x, ct = tokens[0], cotangent[0]
    tt = top_keys[0].transpose(0, 2, 1)
    if custom:
        ws = (qkv_weight.transpose(1, 0, 2), out_weight.T, up_weight, down_weight.T, attn_gain[None], ffn_gain[None])
    else:
        w = pack(qkv_weight, out_weight, up_weight, down_weight)
        gw = jnp.pad(jnp.stack([attn_gain, ffn_gain], 1), ((0, 0), (0, 126)))
        ws = (lax.all_gather(w, "batch", axis=1, tiled=True), lax.all_gather(gw, "batch", axis=0, tiled=True))
    y, tg, gg, *S = layer(nb, custom, x, ct, segment, cluster[0][:, None, :], tt, *ws)
    if custom:
        y, tg, qg, og, ug, dg, g1, g2 = finish(y, tg, *S, gg)
        return y[None], tg[None], g1[0], qg.transpose(1, 0, 2), og.T, g2[0], ug, dg.T
    S = lax.psum_scatter(S[0].astype(F32), "batch", scatter_dimension=1, tiled=True)
    g = lax.psum_scatter(lax.psum(gg, "head"), "batch", scatter_dimension=1, tiled=True)
    cat = lambda a: a.transpose(1, 0, 2).reshape(R, -1)
    qg = S[0:3].reshape(3, R, 3, 128).transpose(1, 2, 0, 3).reshape(R, 3, 384)
    return y[None], tg[None], g[0], qg, S[3].T, g[1], cat(S[4:8]), cat(S[12:16]).T


def pack(q, o, u, d):
    R = q.shape[0]
    qp = q.reshape(R, 3, 3, 128).transpose(2, 0, 1, 3).reshape(3, R, 384)
    up = u.reshape(R, 4, 384).transpose(1, 0, 2)
    dn = d.T.reshape(R, 4, 384).transpose(1, 0, 2)
    return jnp.concatenate([qp, o.T[None], up, dn], 0)


def solution(mesh):
    in_specs = (P("batch", None, None), P("batch"), P("batch", None, "head"), P("head", "batch"), P("batch"), P("batch", "head"), P("head", "batch"), P("batch", None, None), P("batch", None), P("batch", "head", None), P("batch", "head", None, None))
    out_specs = (P("batch", "head", None), P("batch", "head", None), P("batch"), P("batch", None, "head"), P("head", "batch"), P("batch"), P("batch", "head"), P("head", "batch"))
    return jax.shard_map(on_device, mesh=mesh, in_specs=in_specs, out_specs=out_specs, check_vma=False)
```

```python
import functools

import jax
import jax.numpy as jnp
from jax import lax
from jax.experimental import pallas as pl
from jax.experimental.pallas import tpu as pltpu
from jax.sharding import PartitionSpec as P

F32=jnp.float32; BF=jnp.bfloat16
BIG=1e30
NT=(((1,),(1,)),((),()))
TN=(((0,),(0,)),((),()))
NN=(((1,),(0,)),((),()))
def dot(a,b,dims=NN): return lax.dot_general(a,b,dims,preferred_element_type=F32)
def split3(x):
    a=x.astype(BF); r=x-a.astype(F32); b=r.astype(BF); c=(r-b.astype(F32)).astype(BF)
    return a,b,c
def split2(x):
    a=x.astype(BF); return a,(x-a.astype(F32)).astype(BF)
L=1024
def lane(shape): return lax.broadcasted_iota(jnp.int32,shape,len(shape)-1)
def sub(shape): return lax.broadcasted_iota(jnp.int32,shape,len(shape)-2)

def build_masks(own_row, topT):
    mt=jnp.where(own_row==sub((128,L)),1.0,0.0).astype(BF)
    m=jnp.transpose(mt)
    hi=lax.shift_right_arithmetic(topT,5); bit=lax.shift_left(jnp.int32(1),topT&31)
    words=L//32
    a_iota=sub((words,128))
    w=jnp.zeros((words,128),jnp.int32)
    for t in range(topT.shape[0]):
        w=w|jnp.where(hi[t:t+1]==a_iota,bit[t:t+1],0)
    b_iota=sub((32,128)); ln=lane((32,128))
    extra=(ln>=100)&(ln<103)
    ns=[]
    for a in range(words):
        b=(lax.shift_right_logical(jnp.broadcast_to(w[a:a+1],(32,128)),b_iota)&1)
        ns.append(jnp.where(extra,-1.0,jnp.where(b==1,0.0,-BIG)))
    n=jnp.concatenate(ns,0).astype(BF)
    return m,n


TQ = 512
TJ = 512
MESH=pl.DeviceIdType.MESH


def NOP(p): pass
class Place:
    def __init__(self, nb):
        self.nz=nb//4
        self.b=lax.axis_index("batch"); self.h=lax.axis_index("head")
        self.z=self.b//4; self.r=lax.rem(self.b,4)
        even=lax.rem(self.r,2)==0
        self.rx=jnp.where(even,self.r+1,self.r-1)
        self.ry=jnp.where(self.r<2,self.r+2,self.r-2)
        self.rd=3-self.r
        self.X=(self.z*4+self.rx,self.h); self.Y=(self.z*4+self.ry,self.h)
        self.up=(self.b+4,self.h); self.dn=(self.b-4,self.h); self.twin=(self.b,1-self.h)
    def barrier(self):
        bar=pltpu.get_barrier_semaphore()
        for d in (self.X,self.Y,self.twin):
            pl.semaphore_signal(bar,inc=1,device_id=d,device_id_type=MESH)
        @pl.when(self.z<self.nz-1)
        def _(): pl.semaphore_signal(bar,inc=1,device_id=self.up,device_id_type=MESH)
        @pl.when(self.z>0)
        def _(): pl.semaphore_signal(bar,inc=1,device_id=self.dn,device_id_type=MESH)
        lines=jnp.where(self.z<self.nz-1,1,0)+jnp.where(self.z>0,1,0)
        pl.semaphore_wait(bar,3+lines)

def rc(src,dst,ss,rs,dev):
    return pltpu.make_async_remote_copy(src_ref=src,dst_ref=dst,send_sem=ss,recv_sem=rs,device_id=dev,device_id_type=MESH)

class Gather:
    def __init__(self, pc, g, ss, rs):
        self.pc=pc; self.g=g; self.ss=ss; self.rs=rs; self.n=2*(pc.nz-1)
    def cz(self,p,zz,k,dev):
        s=self.g.at[p,zz,self.pc.r]
        return rc(s,s,self.ss.at[p,k],self.rs.at[p,k],dev)
    def z0(self,p):
        c=self.pc
        @pl.when(c.z<c.nz-1)
        def _(): self.cz(p,c.z,0,c.up).start()
        @pl.when(c.z>0)
        def _(): self.cz(p,c.z,1,c.dn).start()
    def zk(self,p,d):
        c=self.pc
        @pl.when(c.z-d>=0)
        def _():
            self.cz(p,c.z-d,2*(d-1),c.up).wait_recv()
        if d<c.nz-1:
            @pl.when((c.z-d>=0)&(c.z<c.nz-1))
            def _(): self.cz(p,c.z-d,2*d,c.up).start()
        @pl.when(c.z+d<c.nz)
        def _():
            self.cz(p,c.z+d,2*(d-1)+1,c.dn).wait_recv()
        if d<c.nz-1:
            @pl.when((c.z+d<c.nz)&(c.z>0))
            def _(): self.cz(p,c.z+d,2*d+1,c.dn).start()
    def cb(self,p,r,k,dev):
        s=self.g.at[p,:,r]
        return rc(s,s,self.ss.at[p,self.n+k],self.rs.at[p,self.n+k],dev)
    def ch(self,p,r,lo,k,dev):
        h=self.pc.nz//2
        s=self.g.at[p,pl.ds(0,h),r] if lo else self.g.at[p,pl.ds(h,self.pc.nz-h),r]
        return rc(s,s,self.ss.at[p,self.n+k],self.rs.at[p,self.n+k],dev)
    def x0(self,p):
        c=self.pc
        self.cb(p,c.r,0,c.X).start(); self.cb(p,c.r,1,c.Y).start()
    def x1(self,p):
        c=self.pc
        self.cb(p,c.rx,0,c.X).wait_recv()
        self.ch(p,c.rx,True,2,c.Y).start()
        self.cb(p,c.ry,1,c.Y).wait_recv()
        self.ch(p,c.ry,False,3,c.X).start()
    def x2(self,p):
        c=self.pc
        self.ch(p,c.rd,True,2,c.Y).wait_recv()
        self.ch(p,c.rd,False,3,c.X).wait_recv()
    def drain(self,p):
        c=self.pc
        for d in range(c.nz-1):
            @pl.when((c.z-d>=0)&(c.z<c.nz-1))
            def _(): self.cz(p,c.z-d,2*d,c.up).wait_send()
            @pl.when((c.z+d<c.nz)&(c.z>0))
            def _(): self.cz(p,c.z+d,2*d+1,c.dn).wait_send()
        self.cb(p,c.r,0,c.X).wait_send(); self.cb(p,c.r,1,c.Y).wait_send()
        self.ch(p,c.rx,True,2,c.Y).wait_send(); self.ch(p,c.ry,False,3,c.X).wait_send()
    def steps(self):
        nz=self.pc.nz
        def last(p):
            self.zk(p,nz-1); self.x0(p)
        return [self.z0]+[functools.partial(lambda d,p:self.zk(p,d),d) for d in range(1,nz-1)]+[last]+[NOP]+[self.x1]+[NOP]+[self.x2]

class PlaneFirst(Gather):
    def cz(self,p,zz,k,dev):
        s=self.g.at[p,zz]
        return rc(s,s,self.ss.at[p,k],self.rs.at[p,k],dev)
    def cb(self,p,r,k,dev):
        s=self.g.at[p,self.pc.z,r]
        return rc(s,s,self.ss.at[p,self.n+k],self.rs.at[p,self.n+k],dev)
    def ch(self,p,r,lo,k,dev):
        n=self.g.shape[3]; h=(n//32)*16
        s=self.g.at[p,self.pc.z,r,pl.ds(0,h)] if lo else self.g.at[p,self.pc.z,r,pl.ds(h,n-h)]
        return rc(s,s,self.ss.at[p,self.n+k],self.rs.at[p,self.n+k],dev)

class Scatter:
    def __init__(self, pc, g, d, rx, ry, ru, rd, ss, rs, slot=lambda p: p):
        self.pc=pc;self.g=g;self.d=d;self.bx=rx;self.by=ry;self.bu=ru;self.bd=rd;self.ss=ss;self.rs=rs
        self.h=pc.nz//2; self.slot=slot
    def half(self,p,r,lo):
        h=self.h; n=self.pc.nz
        return (self.g.at[p,pl.ds(0,h),r],self.d.at[self.slot(p),pl.ds(0,h)]) if lo else (self.g.at[p,pl.ds(h,n-h),r],self.d.at[self.slot(p),pl.ds(h,n-h)])
    def c0(self,p,lo):
        s,t=self.half(p,self.pc.rd,lo); k=0 if lo else 1
        return rc(s,t,self.ss.at[self.slot(p),k],self.rs.at[self.slot(p),k],self.pc.X if lo else self.pc.Y)
    def c1(self,p,x):
        c=self.pc
        return rc(self.g.at[p,:,c.rx if x else c.ry],(self.bx if x else self.by).at[self.slot(p)],self.ss.at[self.slot(p),2 if x else 3],self.rs.at[self.slot(p),2 if x else 3],c.X if x else c.Y)
    def cu(self,p,zz,up):
        c=self.pc; k=4+zz if up else 4+c.nz+zz
        return rc(self.g.at[p,zz,c.r],(self.bu if up else self.bd).at[self.slot(p),zz],self.ss.at[self.slot(p),k],self.rs.at[self.slot(p),k],c.up if up else c.dn)
    def add(self,dst,*srcs):
        v=dst[...].astype(F32)
        for s in srcs: v=v+s[...].astype(F32)
        dst[...]=v.astype(BF)
    def s0(self,p):
        self.c0(p,True).start(); self.c0(p,False).start()
    def s1(self,p):
        c=self.pc;h=self.h;n=c.nz
        self.c0(p,True).wait_recv()
        self.add(self.g.at[p,pl.ds(0,h),c.ry],self.d.at[self.slot(p),pl.ds(0,h)])
        self.c1(p,False).start()
        self.c0(p,False).wait_recv()
        self.add(self.g.at[p,pl.ds(h,n-h),c.rx],self.d.at[self.slot(p),pl.ds(h,n-h)])
        self.c1(p,True).start()
    def s2(self,p):
        c=self.pc
        self.c1(p,True).wait_recv(); self.c1(p,False).wait_recv()
        self.add(self.g.at[p,:,c.r],self.bx.at[self.slot(p)],self.by.at[self.slot(p)])
        self.zk(p,0)
    def zk(self,p,k):
        c=self.pc; nz=c.nz
        @pl.when(c.z==k)
        def _():
            for zz in range(nz-1,k,-1):
                if k>0:
                    self.cu(p,zz,True).wait_recv()
                    self.add(self.g.at[p,zz,c.r],self.bu.at[self.slot(p),zz])
                self.cu(p,zz,True).start()
        @pl.when(c.z==nz-1-k)
        def _():
            for zz in range(0,nz-1-k):
                if k>0:
                    self.cu(p,zz,False).wait_recv()
                    self.add(self.g.at[p,zz,c.r],self.bd.at[self.slot(p),zz])
                self.cu(p,zz,False).start()
    def fin(self,p,tot,place=None):
        c=self.pc
        tot[...]=self.g[p,c.z,c.r].astype(F32)
        @pl.when(c.z>0)
        def _():
            self.cu(p,c.z,True).wait_recv()
            tot[...]+=self.bu[self.slot(p),c.z].astype(F32)
        @pl.when(c.z<c.nz-1)
        def _():
            self.cu(p,c.z,False).wait_recv()
            tot[...]+=self.bd[self.slot(p),c.z].astype(F32)
        if place is not None: place(p)
    def drain(self,p):
        c=self.pc; nz=c.nz
        self.c0(p,True).wait_send(); self.c0(p,False).wait_send()
        self.c1(p,True).wait_send(); self.c1(p,False).wait_send()
        for zz in range(nz):
            @pl.when(zz>c.z)
            def _(): self.cu(p,zz,True).wait_send()
            @pl.when(zz<c.z)
            def _(): self.cu(p,zz,False).wait_send()
    def lines(self):
        return [functools.partial(lambda k,p:self.zk(p,k),k) for k in range(1,self.pc.nz-1)]
    def steps(self,place,tot):
        return [self.s0,NOP,self.s1,NOP,self.s2]+self.lines()+[lambda p:self.fin(p,tot,place)]
    def tight(self,out):
        return [self.s0,self.s1,self.s2]+self.lines()+[lambda p:self.fin(p,out.at[0])]


EPS = 1e-5
RT = 512


def pick(static, cond, body):
    if isinstance(cond, (bool, int)):
        if cond:
            body()
    else:
        pl.when(cond)(body)


def norm_rows(values):
    mean = jnp.mean(values, axis=1, keepdims=True)
    centred = values - mean
    inverse = lax.rsqrt(jnp.mean(centred * centred, axis=1, keepdims=True) + EPS)
    return centred * inverse, inverse


def gelu_both(u):
    c = 0.7978845608028654
    u2 = u * u
    t = jnp.tanh(c * u * (1.0 + 0.044715 * u2))
    half = 0.5 + 0.5 * t
    act = u * half
    grad = half + (0.5 * c) * u * (1.0 - t * t) * (1.0 + (3 * 0.044715) * u2)
    return act, grad


def flat(ref, p):
    v = ref[p]
    return v.reshape(-1, v.shape[-1])


def tiles(n):
    return lambda f: pl.loop(0, n)(f)


def rows_of(i, n=RT):
    return pl.ds(pl.multiple_of(i * n, n), n)


def twin_copy(pc, src, dst, ss, rs):
    return rc(src, dst, ss, rs, pc.twin)


def members(cl, hh):
    return jnp.where(cl[hh] == sub((128, L)), 1.0, 0.0).astype(BF)


def pair_members(cl, p):
    return jnp.concatenate([members(cl, 2 * p), members(cl, 2 * p + 1)], 0)


def pair_own():
    return (lane((256, 128)) >= 64) == (sub((256, 128)) >= 128)


def fwd_clusters(p, qkv, cl, n_s, seg, prob_o):
    q = qkv[p, :, 0:128]
    k = qkv[p, :, 128:256]
    v = qkv[p, :, 256:384]
    own = pair_own()
    mt = pair_members(cl, p)
    cnt = jnp.maximum(jnp.sum(mt.astype(F32), axis=1, keepdims=True), 1.0)
    cen = jnp.where(own, dot(mt, q) / cnt, 0.0).astype(BF)
    s = dot((cen.astype(F32) * 0.125).astype(BF), k, NT)
    top = jnp.concatenate([jnp.transpose(n_s[2 * p + h]).astype(F32) for h in range(2)], 0) == 0.0
    c = sub((256, 1))
    cm = lax.rem(jnp.where(c < 128, c, c - 128), jnp.int32(10))
    s = jnp.where(seg[...] == cm, s, -BIG)
    e = jnp.exp(s - jnp.max(s, axis=1, keepdims=True))
    prob = e / jnp.sum(e, axis=1, keepdims=True)
    mass = jnp.sum(jnp.where(top, prob, 0.0), axis=1, keepdims=True)
    signed = jnp.where(top, -prob, prob).astype(BF)
    prob_o[2 * p] = signed[0:128]
    prob_o[2 * p + 1] = signed[128:256]
    rest = dot(jnp.where(top, 0.0, prob).astype(BF), v)
    rh, rl = split2(jnp.where(own, rest, jnp.broadcast_to(mass, (256, 128))))
    rr = jnp.concatenate([rh, rl], 1)
    return rr[0:128], rr[128:256]


def fwd_head(p, h, rr, qkv, mb, n_s, qaug, kaug, att, ex):
    odd = h == 1
    hh = 2 * p + h
    k = qkv[p, :, 128:256]
    ln = lane((L, 128))
    mine = (ln >= 64) if odd else (ln < 64)
    zero = jnp.zeros((), BF)
    vaug = jnp.where(mine, qkv[p, :, 256:384], jnp.ones((), BF))
    qaug[:, :128] = (jnp.where(mine, qkv[p, :, 0:128], zero).astype(F32) * 0.125).astype(BF)
    qaug[:, 128:] = mb[hh]
    kaug[:, :128] = k
    kaug[:, 128:] = n_s[hh]
    lt = lane((TQ, 128))
    minet = (lt >= 64) if odd else (lt < 64)
    cols = pl.ds(pl.multiple_of(p * 128, 128), 128)
    for t in range(L // TQ):
        sl = pl.ds(t * TQ, TQ)
        sc = dot(qaug[sl, :], kaug[...], NT)
        mm = jnp.max(sc, axis=1, keepdims=True)
        pr = jnp.exp(sc - mm).astype(BF)
        o = dot(pr, vaug)
        mt_ = qaug[sl, 128:]
        ee = dot(mt_, rr)
        ee = ee[:, :128] + ee[:, 128:]
        osw = pltpu.roll(o, 64, 1)
        esw = pltpu.roll(ee, 64, 1)
        exact = o / osw
        a = exact * esw + ee
        tot = jnp.where(minet, osw, o)
        ms = jnp.where(minet, esw, ee)
        lse = mm + jnp.log(tot) - jnp.log(jnp.maximum(ms, 1e-37))
        h3, m3, l3 = split3(lse)
        mb[hh, sl, :] = jnp.where(lt == 100, h3.astype(F32), jnp.where(lt == 101, m3.astype(F32), jnp.where(lt == 102, l3.astype(F32), mt_.astype(F32)))).astype(BF)
        if odd:
            att[sl, cols] = jnp.where(lt < 64, att[sl, cols], a.astype(BF))
            ex[sl, cols] = jnp.where(lt < 64, ex[sl, cols], exact.astype(BF))
        else:
            att[sl, cols] = a.astype(BF)
            ex[sl, cols] = exact.astype(BF)


def as_column(row):
    n = row.shape[1]
    eye = sub((n, n)) == lane((n, n))
    return jnp.sum(jnp.where(eye, row.astype(F32), 0.0), axis=1, keepdims=True)


def fill_own(pc, g, gg, q3, oT, upw, dT, ga, gf):
    for p in range(3):
        for i in range(3):
            g[p, pc.z, pc.r, :, i * 128:(i + 1) * 128] = q3[i, :, p * 128:(p + 1) * 128]
    g[3, pc.z, pc.r] = oT[...]
    for q in range(4):
        g[4 + q, pc.z, pc.r] = upw[:, q * 384:(q + 1) * 384]
        g[8 + q, pc.z, pc.r] = dT[:, q * 384:(q + 1) * 384]
    R = oT.shape[0]
    ln = lane((R, 128))
    gg[0, pc.z, pc.r] = jnp.where(ln == 0, as_column(ga[...]), jnp.where(ln == 1, as_column(gf[...]), 0.0)).astype(BF)


def bwd_clusters(p, cl, s, gaugs, dq_o, dk_o, dv_o):
    qkv = s["qkv"]
    cols = pl.ds(pl.multiple_of(p * 128, 128), 128)
    qv = qkv[p, :, 0:128]
    kv = qkv[p, :, 128:256]
    vv = qkv[p, :, 256:384]
    gv = s["gatt"][:, cols]
    ln = lane((L, 128))
    lc = lane((256, 128))
    row = sub((256, 128))
    own = pair_own()
    prod = gv.astype(F32) * s["ex"][:, cols].astype(F32)
    dots = jnp.zeros((L, 128), F32)
    for h in range(2):
        mine = (ln >= 64) if h else (ln < 64)
        o = 0 if h else 64
        three = [a.astype(F32) for a in split3(jnp.sum(jnp.where(mine, prod, 0.0), axis=1, keepdims=True))]
        ga = jnp.where(mine, gv.astype(F32), 0.0)
        for i, a in enumerate(three):
            ga = jnp.where(ln == o + i, a, ga)
            dots = jnp.where(ln == 3 * h + i, a, dots)
        gaugs[h][...] = ga.astype(BF)
    mt = pair_members(cl, p)
    cnt = jnp.maximum(jnp.sum(mt.astype(F32), axis=1, keepdims=True), 1.0)
    cq = dot(mt, jnp.concatenate([qv, gv], 1))
    cen = jnp.where(own, cq[:, 0:128] / cnt, 0.0).astype(BF)
    cs = (cen.astype(F32) * 0.125).astype(BF)
    grest = jnp.where(own, cq[:, 128:256], 0.0).astype(BF)
    gm = dot(mt, dots.astype(BF))
    lo = jnp.where(row >= 128, 3, 0)
    gmass = jnp.sum(jnp.where((lc >= lo) & (lc < lo + 3), gm, 0.0), axis=1, keepdims=True)
    signed = jnp.concatenate([s["prob"][2 * p], s["prob"][2 * p + 1]], 0).astype(F32)
    top = signed < 0.0
    prob = jnp.abs(signed)
    gp = jnp.where(top, gmass, dot(grest, vv, NT))
    gs = (prob * (gp - jnp.sum(prob * gp, axis=1, keepdims=True))).astype(BF)
    rw = jnp.where(top, 0.0, prob).astype(BF)
    gcen = jnp.where(own, dot(gs, kv) / cnt, 0.0)
    gh, gl = split2(gcen)
    dk_o[...] = dot(jnp.transpose(gs), cs)
    dv_o[...] = dot(jnp.transpose(rw), grest)
    zero = jnp.zeros((), BF)
    two = jnp.concatenate([jnp.where(ln < 100, s["mb"][2 * p + h], zero) for h in range(2)], 1)
    dd = dot(two, jnp.concatenate([gh, gl], 1))
    dq_o[...] = dd[:, :128] + dd[:, 128:]


def bwd_head(p, h, s, qaug, kaug, gaug, vaug, dk_o, dv_o, dqt):
    qkv = s["qkv"]
    hh = 2 * p + h
    cols = pl.ds(pl.multiple_of(p * 128, 128), 128)
    kv = qkv[p, :, 128:256]
    ln = lane((L, 128))
    zero = jnp.zeros((), BF)
    mine = (ln >= 64) if h else (ln < 64)
    o = 0 if h else 64
    gm = jnp.where(mine, s["gatt"][:, cols], zero)
    vaug[...] = jnp.where(mine, qkv[p, :, 256:384], jnp.where((ln >= o) & (ln < o + 3), jnp.full((), -1.0, BF), zero))
    qs = (jnp.where(mine, qkv[p, :, 0:128], zero).astype(F32) * 0.125).astype(BF)
    qaug[:, :128] = qs
    qaug[:, 128:] = s["mb"][hh]
    kaug[:, :128] = kv
    kaug[:, 128:] = s["ns"][hh]
    kTh = jnp.transpose(kv)[64 * h:64 * h + 64]
    for t in range(L // TJ):
        sl = pl.ds(t * TJ, TJ)
        pr = jnp.exp(dot(kaug[sl, :], qaug[...], NT))
        ds = (pr * dot(vaug[sl, :], gaug[...], NT)).astype(BF)
        dv_o[sl, :] += dot(pr.astype(BF), gm)
        dk_o[sl, :] += dot(ds, qs)
        dqp = dot(kTh[:, t * TJ:(t + 1) * TJ], ds)
        if t == 0:
            dqt[64 * h:64 * h + 64, :] = dqp
        else:
            dqt[64 * h:64 * h + 64, :] += dqp


def place_sum(p, tot, outs):
    qg, og, ug, dg = outs

    def pair(p):
        for i in range(3):
            qg[i, :, pl.ds(pl.multiple_of(p * 128, 128), 128)] = tot[:, i * 128:(i + 1) * 128]

    def wide(ref, q):
        ref[:, pl.ds(pl.multiple_of(q * 384, 128), 384)] = tot[...]

    pick(None, (8 <= p < 12) if isinstance(p, int) else (p >= 8) & (p < 12), lambda: pair(p - 8))
    pick(None, p == 3, lambda: og.__setitem__(..., tot[...]))
    pick(None, (3 < p < 8) if isinstance(p, int) else (p > 3) & (p < 8), lambda: wide(ug, p - 4))
    pick(None, p >= 12, lambda: wide(dg, p - 12))


def finish_body(*refs):
    ins, gg, outs, (g1, g2), bufs, (si, so) = refs[:6], refs[6], refs[7:13], refs[13:15], refs[15:21], refs[21:]
    ci = [pltpu.make_async_copy(a, b, si.at[i]) for i, (a, b) in enumerate(zip(ins, bufs))]
    co = [pltpu.make_async_copy(a, b, so.at[i]) for i, (a, b) in enumerate(zip(bufs, outs))]
    for c in ci:
        c.start()
    R = gg.shape[1]
    eye = sub((R, R)) == lane((R, R))
    for i, g in enumerate((g1, g2)):
        g[...] = jnp.sum(jnp.where(eye, gg[0, :, i:i + 1], 0.0), axis=0, keepdims=True)
    for a, b in zip(ci, co):
        a.wait()
        b.start()
    for c in co:
        c.wait()


def finish(*arrays):
    V = pl.BlockSpec(memory_space=pltpu.VMEM)
    A = pl.BlockSpec(memory_space=pl.ANY)
    R = arrays[6].shape[1]
    dma = pltpu.SemaphoreType.DMA
    return pl.pallas_call(
        finish_body,
        out_shape=[jax.ShapeDtypeStruct(a.shape, a.dtype) for a in arrays[:6]] + [jax.ShapeDtypeStruct((1, R), F32)] * 2,
        in_specs=[A] * 6 + [V], out_specs=[A] * 6 + [V] * 2,
        scratch_shapes=[pltpu.VMEM(a.shape, a.dtype) for a in arrays[:6]] + [dma((6,)), dma((6,))],
        compiler_params=pltpu.CompilerParams(vmem_limit_bytes=60 << 20),
    )(*arrays)


def scratch_shapes(custom, nz, R):
    f = lambda *s: (s, F32)
    b = lambda *s: (s, BF)
    wide = (16, nz, 4, R, 384) if custom else (16, 768, 384)
    return {
        "gr": f(8, 768), "n1": b(L, 768), "qkv": b(3, L, 384), "att": b(L, 384), "ex": b(L, 384), "mb": b(6, L, 128),
        "ns": b(6, L, 128), "prob": b(6, 128, L), "hid": f(L, 768), "n2": b(L, 768), "act": b(4, L, 384), "dg": b(4, L, 384),
        "aT": b(768, L), "eb": b(L, 768), "er": b(L, 768), "fr": b(L // 2, 768), "gatt": b(L, 384),
        "qaug": b(L, 256), "kaug": b(L, 256), "gaug": b(L, 128), "gaug1": b(L, 128), "vaug": b(L, 128),
        "dqs": f(L, 128), "dks": f(L, 128), "dvs": f(L, 128), "dqt": f(128, L), "gacc": f(8, 768),
        "wg": b(*wide),
    }


def layer_body(nb, custom, names, *refs):
    refs = list(refs)
    take = lambda n: [refs.pop(0) for _ in range(n)]
    x, ct, seg, cl, tt = take(5)
    own = take(6 if custom else 2)
    y, tg, out_g = take(3)
    out_s = take(4) if custom else take(1)[0]
    s = dict(zip(names, take(len(names))))
    tpad, es, ers, vs, vrs = take(5)
    pc = Place(nb)
    wg, hid, n1, n2, qkv, att, ex, act, dg = (s[n] for n in ("wg", "hid", "n1", "n2", "qkv", "att", "ex", "act", "dg"))
    aT, eb, er, fr, gr, gacc = (s[n] for n in ("aT", "eb", "er", "fr", "gr", "gacc"))
    half, nh, nt = L // 2, L // 2 // RT, L // RT

    if custom:
        gg, tot, gbuf, ss, rs, gss, grs, ss2, rs2, gss2, grs2, gown, gtwin = take(13)
        land, gland = take(5), take(5)
        G, Gg = Gather(pc, wg, ss, rs), Gather(pc, gg, gss, grs)
        S = Scatter(pc, wg, *land, ss2, rs2, slot=lambda p: (p - 4 if p >= 12 else p - 8 if p >= 8 else p) if isinstance(p, int) else jnp.where(p >= 12, p - 4, jnp.where(p >= 8, p - 8, p)))
        Sg = Scatter(pc, gbuf, *gland, gss2, grs2)
        Gp = PlaneFirst(pc, wg, ss, rs)
        m = pc.nz - 1

        def last(p):
            G.zk(p, m)
            G.x0(p)

        def turn(p):
            Gp.x2(p)
            Gp.z0(p)
        line = lambda g, off: [(off + d, functools.partial(lambda d, p: g.zk(p, d), d)) for d in range(1, m)][::-1]
        nine = lambda k: k + k // 3
        three = lambda k: k + 3
        rest = list(range(1, 9))
        gather = [(m + 2, G.x2, [0], nine), (m + 1, G.x1, [0], nine), (m + 3, G.x2, rest, nine), (m + 2, G.x1, rest, nine)]
        gather += [(e, fn, list(range(9)), nine) for e, fn in [(m, last)] + line(G, 0) + [(0, G.z0)]]
        gather += [(e, fn, [0, 4, 8], three) for e, fn in [(m + 3, lambda p: Gp.zk(p, m))] + line(Gp, 3) + [(2, turn), (1, Gp.x1), (0, Gp.x0)]]
        gsteps = [Gg.z0] + [functools.partial(lambda d: Gg.zk(0, d), d) for d in range(1, m)] + [None, Gg.x1, Gg.x2]
        ssteps = S.steps(lambda p: place_sum(p, tot, out_s), tot)
        tails = Sg.tight(gown)
        starts = {13: 12, 14: 13, 15: 14, 16: 15, 17: 4, 18: 5, 19: 6, 20: 7, 21: 3, 22: 8, 23: 9, 25: 10}

        def tick(t, span=None):
            fixed = isinstance(t, int)
            ts = [t] if fixed else list(range(*span))
            for i in range(len(ssteps) - 1, -1, -1):
                hits = [u - i for u in ts if u - i in starts]
                if not hits or ssteps[i] is NOP:
                    continue
                if fixed:
                    ssteps[i](starts[hits[0]])
                    continue
                u = t - i
                ok = functools.reduce(jnp.logical_or, [u == k for k in hits])
                part = functools.reduce(lambda a, k: jnp.where(u == k, starts[k], a), hits, 0)
                pl.when(ok)(lambda i=i, part=part: ssteps[i](part))
            for off, fn, at, to in gather:
                hits = [u - off for u in ts if u - off in at]
                if not hits:
                    continue
                u = t - off
                ok = True if fixed else functools.reduce(jnp.logical_or, [u == k for k in hits])
                pick(None, ok, lambda fn=fn, p=to(u): fn(p))
            if fixed and t < len(gsteps):
                if t == m:
                    Gg.zk(0, m)
                    Gg.x0(0)
                elif t == 0:
                    gsteps[0](0)
                elif t < m:
                    gsteps[t]()
                else:
                    gsteps[t](0)
    else:
        tick = lambda t, span=None: None

    tpad[...] = jnp.full_like(tpad, -1)
    pc.barrier()
    if custom:
        fill_own(pc, wg, gg, *own)
    tick(0)

    @tiles(nt)
    def _(i):
        hid[rows_of(i), :] = norm_rows(x[rows_of(i), :].astype(F32))[0]

    tick(1)

    def mask(h):
        tpad[:, 0:tt.shape[2]] = tt[h]
        a, n = build_masks(cl[h], tpad[...])
        s["mb"][h], s["ns"][h] = a, n

    def transpose_into(src):
        for i in range(nt):
            aT[:, i * RT:(i + 1) * RT] = jnp.transpose(src[i * RT:(i + 1) * RT, :])

    def put(p, left, right):
        wg[p] = dot(left, right).astype(BF).reshape(wg.shape[1:])

    pl.loop(0, 2)(mask)
    tick(2)
    pl.loop(2, 4)(mask)
    tick(3)
    pl.loop(4, 6)(mask)
    transpose_into(ct)
    tick(4)
    tick(5)
    if custom:
        gains = gg[0].reshape(768, 128)
    else:
        c = pltpu.make_async_copy(own[0], wg.at[0:12], vs)
        c.start()
        c.wait()
        gains = own[1][...]
    gr[...] = jnp.transpose(gains.astype(F32))[0:8]

    @tiles(nt)
    def _(i):
        n1[rows_of(i), :] = (hid[rows_of(i), :] * gr[0:1, :]).astype(BF)

    @pl.loop(0, 3)
    def _(p):
        @tiles(nt)
        def _(i):
            qkv[p, rows_of(i), :] = dot(n1[rows_of(i), :], flat(wg, p)).astype(BF)
        rr = fwd_clusters(p, qkv, cl, s["ns"], seg, s["prob"])
        for h in range(2):
            tick(6 + 2 * p + h, (6 + h, 12, 2))
            fwd_head(p, h, rr[h], qkv, s["mb"], s["ns"], s["qaug"], s["kaug"], att, ex)

    def send(k, src, dst, i):
        return twin_copy(pc, src.at[rows_of(i)], dst.at[rows_of(i)], es.at[k + i], ers.at[k + i])

    @tiles(nt)
    def _(i):
        eb[rows_of(i), :] = dot(att[rows_of(i), :], flat(wg, 3), NT).astype(BF)
        send(0, eb, er, i).start()

    tick(12)

    @tiles(nt)
    def _(i):
        r = rows_of(i)
        send(0, eb, er, i).wait()
        hv = x[r, :].astype(F32) + (eb[r, :].astype(F32) + er[r, :].astype(F32))
        hid[r, :] = hv
        n2[r, :] = (norm_rows(hv)[0] * gr[1:2, :]).astype(BF)

    def up(q):
        @tiles(nt)
        def _(i):
            a, d = gelu_both(dot(n2[rows_of(i), :], flat(wg, 4 + q)))
            act[q, rows_of(i), :] = a.astype(BF)
            dg[q, rows_of(i), :] = d.astype(BF)

    def down_grad(q):
        up(q)
        put(12 + q, aT[...], act[q])

    pl.loop(0, 2)(down_grad)
    tick(13)
    def gate(q):
        @tiles(nt)
        def _(i):
            ga = dot(ct[rows_of(i), :], flat(wg, 8 + q))
            dg[q, rows_of(i), :] = (ga * dg[q, rows_of(i), :].astype(F32)).astype(BF)

    pl.loop(2, 4)(down_grad)
    pl.loop(0, 2)(gate)
    tick(14)
    transpose_into(n2)

    def part(i):
        acc = dot(act[0, rows_of(i), :], flat(wg, 8), NT)
        for q in range(1, 4):
            acc += dot(act[q, rows_of(i), :], flat(wg, 8 + q), NT)
        return acc

    @tiles(nh)
    def _(i):
        eb[rows_of(i), :] = part((1 - pc.h) * nh + i).astype(BF)
        send(4, eb, fr, i).start()

    tick(15)

    pl.loop(2, 4)(gate)

    @tiles(nh)
    def _(i):
        acc = part(pc.h * nh + i).astype(BF).astype(F32)
        send(4, eb, fr, i).wait()
        y[rows_of(i), :] = (hid[rows_of(pc.h * nh + i), :] + (acc + fr[rows_of(i), :].astype(F32))).astype(BF)

    tick(16)
    if custom:
        @pl.loop(0, 9)
        def _(k):
            G.drain(nine(k))

        @pl.loop(0, 3)
        def _(k):
            Gp.drain(4 * k + 3)
        Gg.drain(0)

    @tiles(nt)
    def _(i):
        acc = dot(dg[0, rows_of(i), :], flat(wg, 4), NT)
        for q in range(1, 4):
            acc += dot(dg[q, rows_of(i), :], flat(wg, 4 + q), NT)
        eb[rows_of(i), :] = acc.astype(BF)
        send(6, eb, er, i).start()

    def up_grad(q):
        put(4 + q, aT[...], dg[q])

    pl.loop(0, 4)(up_grad)
    tick(17)
    gacc[...] = jnp.zeros_like(gacc)
    gat = n2

    @tiles(nt)
    def _(i):
        r = rows_of(i)
        send(6, eb, er, i).wait()
        gn = eb[r, :].astype(F32) + er[r, :].astype(F32)
        n, inv = norm_rows(hid[r, :])
        a = gn * gr[1:2, :]
        back = (a - jnp.mean(a, axis=1, keepdims=True) - n * jnp.mean(a * n, axis=1, keepdims=True)) * inv
        gh = ct[r, :].astype(F32) + back
        gat[r, :] = gh.astype(BF)

        @pl.when((i >= pc.h * nh) & (i < pc.h * nh + nh))
        def _():
            tg[rows_of(i - pc.h * nh), :] = gh
            gacc[1:2, :] += jnp.sum(gn * n, axis=0, keepdims=True)

    tick(18)

    @tiles(nt)
    def _(i):
        s["gatt"][rows_of(i), :] = dot(gat[rows_of(i), :], flat(wg, 3)).astype(BF)

    transpose_into(gat)
    put(3, aT[...], att[...])
    tick(19)
    transpose_into(n1)
    nacc = hid
    dqkv = att

    @pl.loop(0, 3)
    def _(p):
        bwd_clusters(p, cl, s, (s["gaug"], s["gaug1"]), s["dqs"], s["dks"], s["dvs"])
        bwd_head(p, 0, s, s["qaug"], s["kaug"], s["gaug"], s["vaug"], s["dks"], s["dvs"], s["dqt"])
        tick(20 + 2 * p, (20, 26, 2))
        bwd_head(p, 1, s, s["qaug"], s["kaug"], s["gaug1"], s["vaug"], s["dks"], s["dvs"], s["dqt"])
        dqkv[:, 0:128] = ((s["dqs"][...] + jnp.transpose(s["dqt"][...])) * 0.125).astype(BF)
        dqkv[:, 128:256] = s["dks"][...].astype(BF)
        dqkv[:, 256:384] = s["dvs"][...].astype(BF)

        put(8 + p, aT[...], dqkv[...])
        tick(21 + 2 * p, (21, 27, 2))

        @tiles(nt)
        def _(i):
            v = dot(dqkv[rows_of(i), :], flat(wg, p), NT)

            @pl.when(p == 0)
            def _():
                nacc[rows_of(i), :] = v

            @pl.when(p > 0)
            def _():
                nacc[rows_of(i), :] += v

    @tiles(nh)
    def _(i):
        eb[rows_of(i), :] = nacc[rows_of((1 - pc.h) * nh + i), :].astype(BF)
        send(10, eb, fr, i).start()

    @tiles(nt)
    def _(i):
        n = norm_rows(x[rows_of(i), :].astype(F32))[0]
        gacc[0:1, :] += jnp.sum(nacc[rows_of(i), :] * n, axis=0, keepdims=True)

    if custom:
        wide = jnp.concatenate([gacc[...], jnp.zeros((120, 768), F32)], 0)
        gbuf[0] = jnp.transpose(wide).astype(BF).reshape(gbuf.shape[1:])

    def late(t):
        tick(t)
        if custom and t - 26 < len(tails):
            tails[t - 26](0)

    late(26)
    late(27)

    @tiles(nh)
    def _(i):
        r = rows_of(i)
        send(10, eb, fr, i).wait()
        gn = nacc[rows_of(pc.h * nh + i), :].astype(BF).astype(F32) + fr[r, :].astype(F32)
        n, inv = norm_rows(x[rows_of(pc.h * nh + i), :].astype(F32))
        a = gn * gr[0:1, :]
        back = (a - jnp.mean(a, axis=1, keepdims=True) - n * jnp.mean(a * n, axis=1, keepdims=True)) * inv
        tg[r, :] += back

    if custom:
        for t in range(28, max(25 + len(ssteps), 26 + len(tails))):
            late(t)
            if t == 25 + len(tails):
                cv = twin_copy(pc, gown, gtwin, vs, vrs)
                cv.start()

        @pl.loop(0, 12)
        def _(i):
            S.drain(jnp.where(i < 3, i + 8, jnp.where(i < 8, i, i + 4)))
        Sg.drain(0)
        cv.wait()
        out_g[0] = gown[0] + gtwin[0]
    else:
        c = pltpu.make_async_copy(wg, out_s, vs)
        c.start()
        out_g[...] = gacc[...]
        c.wait()


def layer(nb, custom, *args):
    V = pl.BlockSpec(memory_space=pltpu.VMEM)
    A = pl.BlockSpec(memory_space=pl.ANY)
    nz = nb // 4
    dma = pltpu.SemaphoreType.DMA
    tt, ws = args[4], args[5:]
    R = ws[1].shape[0]
    shapes = scratch_shapes(custom, nz, R)
    out_shape = [jax.ShapeDtypeStruct((L // 2, 768), BF), jax.ShapeDtypeStruct((L // 2, 768), F32)]
    if custom:
        out_shape += [jax.ShapeDtypeStruct(sh, F32) for sh in ((1, R, 128), (3, R, 384), (R, 384), (R, 1536), (R, 1536))]
        out_specs = [V] * 7
        in_specs = [V] * len(args)
    else:
        out_shape += [jax.ShapeDtypeStruct((8, 768), F32), jax.ShapeDtypeStruct(shapes["wg"][0], BF)]
        out_specs = [V, V, V, A]
        in_specs = [V] * 5 + [A, V]
    scratch = [pltpu.VMEM(*sd) for sd in shapes.values()] + [pltpu.VMEM((tt.shape[1], 128), jnp.int32), dma((12,)), dma((12,)), dma, dma]
    if custom:
        ns, n2 = 2 * (nz - 1) + 4, 4 + 2 * nz
        vb = lambda *sh: pltpu.VMEM(sh, BF)
        scratch += [vb(1, nz, 4, R, 128), pltpu.VMEM((R, 384), F32), vb(1, nz, 4, R, 128), dma((12, ns)), dma((12, ns)), dma((1, ns)), dma((1, ns)),
                    dma((12, n2)), dma((12, n2)), dma((1, n2)), dma((1, n2)), pltpu.VMEM((1, R, 128), F32), pltpu.VMEM((1, R, 128), F32)] + [vb(12, nz, R, 384)] * 5 + [vb(1, nz, R, 128)] * 5
    return pl.pallas_call(
        functools.partial(layer_body, nb, custom, tuple(shapes)),
        out_shape=out_shape, in_specs=in_specs, out_specs=out_specs, scratch_shapes=scratch,
        compiler_params=pltpu.CompilerParams(collective_id=0, has_side_effects=True, vmem_limit_bytes=int(63.9 * (1 << 20))),
    )(*args)


def on_device(tokens, attn_gain, qkv_weight, out_weight, ffn_gain, up_weight, down_weight, cotangent, segment, cluster, top_keys):
    nb = lax.axis_size("batch")
    R = qkv_weight.shape[0]
    custom = R % 16 == 0 and nb % 4 == 0
    x, ct = tokens[0], cotangent[0]
    tt = top_keys[0].transpose(0, 2, 1)
    if custom:
        ws = (qkv_weight.transpose(1, 0, 2), out_weight.T, up_weight, down_weight.T, attn_gain[None], ffn_gain[None])
    else:
        w = pack(qkv_weight, out_weight, up_weight, down_weight)
        gw = jnp.pad(jnp.stack([attn_gain, ffn_gain], 1), ((0, 0), (0, 126)))
        ws = (lax.all_gather(w, "batch", axis=1, tiled=True), lax.all_gather(gw, "batch", axis=0, tiled=True))
    y, tg, gg, *S = layer(nb, custom, x, ct, segment, cluster[0][:, None, :], tt, *ws)
    if custom:
        y, tg, qg, og, ug, dg, g1, g2 = finish(y, tg, *S, gg)
        return y[None], tg[None], g1[0], qg.transpose(1, 0, 2), og.T, g2[0], ug, dg.T
    S = lax.psum_scatter(S[0].astype(F32), "batch", scatter_dimension=1, tiled=True)
    g = lax.psum_scatter(lax.psum(gg, "head"), "batch", scatter_dimension=1, tiled=True)
    cat = lambda a: a.transpose(1, 0, 2).reshape(R, -1)
    qg = S[8:11].reshape(3, R, 3, 128).transpose(1, 2, 0, 3).reshape(R, 3, 384)
    return y[None], tg[None], g[0], qg, S[3].T, g[1], cat(S[4:8]), cat(S[12:16]).T


def pack(q, o, u, d):
    R = q.shape[0]
    qp = q.reshape(R, 3, 3, 128).transpose(2, 0, 1, 3).reshape(3, R, 384)
    up = u.reshape(R, 4, 384).transpose(1, 0, 2)
    dn = d.T.reshape(R, 4, 384).transpose(1, 0, 2)
    return jnp.concatenate([qp, o.T[None], up, dn], 0)


def solution(mesh):
    in_specs = (P("batch", None, None), P("batch"), P("batch", None, "head"), P("head", "batch"), P("batch"), P("batch", "head"), P("head", "batch"), P("batch", None, None), P("batch", None), P("batch", "head", None), P("batch", "head", None, None))
    out_specs = (P("batch", "head", None), P("batch", "head", None), P("batch"), P("batch", None, "head"), P("head", "batch"), P("batch"), P("batch", "head"), P("head", "batch"))
    return jax.shard_map(on_device, mesh=mesh, in_specs=in_specs, out_specs=out_specs, check_vma=False)
```

```python
import functools

import jax
import jax.numpy as jnp
from jax import lax
from jax.experimental import pallas as pl
from jax.experimental.pallas import tpu as pltpu
from jax.sharding import PartitionSpec as P

F32=jnp.float32; BF=jnp.bfloat16
BIG=1e30
NT=(((1,),(1,)),((),()))
TN=(((0,),(0,)),((),()))
NN=(((1,),(0,)),((),()))
def dot(a,b,dims=NN): return lax.dot_general(a,b,dims,preferred_element_type=F32)
def split3(x):
    a=x.astype(BF); r=x-a.astype(F32); b=r.astype(BF); c=(r-b.astype(F32)).astype(BF)
    return a,b,c
def split2(x):
    a=x.astype(BF); return a,(x-a.astype(F32)).astype(BF)
L=1024
def lane(shape): return lax.broadcasted_iota(jnp.int32,shape,len(shape)-1)
def sub(shape): return lax.broadcasted_iota(jnp.int32,shape,len(shape)-2)

def build_masks(own_row, topT):
    mt=jnp.where(own_row==sub((128,L)),1.0,0.0).astype(BF)
    m=jnp.transpose(mt)
    hi=lax.shift_right_arithmetic(topT,5); bit=lax.shift_left(jnp.int32(1),topT&31)
    words=L//32
    a_iota=sub((words,128))
    w=jnp.zeros((words,128),jnp.int32)
    for t in range(topT.shape[0]):
        w=w|jnp.where(hi[t:t+1]==a_iota,bit[t:t+1],0)
    b_iota=sub((32,128)); ln=lane((32,128))
    extra=(ln>=100)&(ln<103)
    ns=[]
    for a in range(words):
        b=(lax.shift_right_logical(jnp.broadcast_to(w[a:a+1],(32,128)),b_iota)&1)
        ns.append(jnp.where(extra,-1.0,jnp.where(b==1,0.0,-BIG)))
    n=jnp.concatenate(ns,0).astype(BF)
    return m,n


TQ = 512
TJ = 512
MESH=pl.DeviceIdType.MESH


def NOP(p): pass
class Place:
    def __init__(self, nb):
        self.nz=nb//4
        self.b=lax.axis_index("batch"); self.h=lax.axis_index("head")
        self.z=self.b//4; self.r=lax.rem(self.b,4)
        even=lax.rem(self.r,2)==0
        self.rx=jnp.where(even,self.r+1,self.r-1)
        self.ry=jnp.where(self.r<2,self.r+2,self.r-2)
        self.rd=3-self.r
        self.X=(self.z*4+self.rx,self.h); self.Y=(self.z*4+self.ry,self.h)
        self.up=(self.b+4,self.h); self.dn=(self.b-4,self.h); self.twin=(self.b,1-self.h)
    def barrier(self):
        bar=pltpu.get_barrier_semaphore()
        for d in (self.X,self.Y,self.twin):
            pl.semaphore_signal(bar,inc=1,device_id=d,device_id_type=MESH)
        @pl.when(self.z<self.nz-1)
        def _(): pl.semaphore_signal(bar,inc=1,device_id=self.up,device_id_type=MESH)
        @pl.when(self.z>0)
        def _(): pl.semaphore_signal(bar,inc=1,device_id=self.dn,device_id_type=MESH)
        lines=jnp.where(self.z<self.nz-1,1,0)+jnp.where(self.z>0,1,0)
        pl.semaphore_wait(bar,3+lines)

def rc(src,dst,ss,rs,dev):
    return pltpu.make_async_remote_copy(src_ref=src,dst_ref=dst,send_sem=ss,recv_sem=rs,device_id=dev,device_id_type=MESH)

class Gather:
    def __init__(self, pc, g, ss, rs):
        self.pc=pc; self.g=g; self.ss=ss; self.rs=rs; self.n=2*(pc.nz-1)
    def cz(self,p,zz,k,dev):
        s=self.g.at[p,zz,self.pc.r]
        return rc(s,s,self.ss.at[p,k],self.rs.at[p,k],dev)
    def z0(self,p):
        c=self.pc
        @pl.when(c.z<c.nz-1)
        def _(): self.cz(p,c.z,0,c.up).start()
        @pl.when(c.z>0)
        def _(): self.cz(p,c.z,1,c.dn).start()
    def zk(self,p,d):
        c=self.pc
        @pl.when(c.z-d>=0)
        def _():
            self.cz(p,c.z-d,2*(d-1),c.up).wait_recv()
        if d<c.nz-1:
            @pl.when((c.z-d>=0)&(c.z<c.nz-1))
            def _(): self.cz(p,c.z-d,2*d,c.up).start()
        @pl.when(c.z+d<c.nz)
        def _():
            self.cz(p,c.z+d,2*(d-1)+1,c.dn).wait_recv()
        if d<c.nz-1:
            @pl.when((c.z+d<c.nz)&(c.z>0))
            def _(): self.cz(p,c.z+d,2*d+1,c.dn).start()
    def cb(self,p,r,k,dev):
        s=self.g.at[p,:,r]
        return rc(s,s,self.ss.at[p,self.n+k],self.rs.at[p,self.n+k],dev)
    def ch(self,p,r,lo,k,dev):
        h=self.pc.nz//2
        s=self.g.at[p,pl.ds(0,h),r] if lo else self.g.at[p,pl.ds(h,self.pc.nz-h),r]
        return rc(s,s,self.ss.at[p,self.n+k],self.rs.at[p,self.n+k],dev)
    def x0(self,p):
        c=self.pc
        self.cb(p,c.r,0,c.X).start(); self.cb(p,c.r,1,c.Y).start()
    def x1(self,p):
        c=self.pc
        self.cb(p,c.rx,0,c.X).wait_recv()
        self.ch(p,c.rx,True,2,c.Y).start()
        self.cb(p,c.ry,1,c.Y).wait_recv()
        self.ch(p,c.ry,False,3,c.X).start()
    def x2(self,p):
        c=self.pc
        self.ch(p,c.rd,True,2,c.Y).wait_recv()
        self.ch(p,c.rd,False,3,c.X).wait_recv()
    def drain(self,p):
        c=self.pc
        for d in range(c.nz-1):
            @pl.when((c.z-d>=0)&(c.z<c.nz-1))
            def _(): self.cz(p,c.z-d,2*d,c.up).wait_send()
            @pl.when((c.z+d<c.nz)&(c.z>0))
            def _(): self.cz(p,c.z+d,2*d+1,c.dn).wait_send()
        self.cb(p,c.r,0,c.X).wait_send(); self.cb(p,c.r,1,c.Y).wait_send()
        self.ch(p,c.rx,True,2,c.Y).wait_send(); self.ch(p,c.ry,False,3,c.X).wait_send()
    def steps(self):
        nz=self.pc.nz
        def last(p):
            self.zk(p,nz-1); self.x0(p)
        return [self.z0]+[functools.partial(lambda d,p:self.zk(p,d),d) for d in range(1,nz-1)]+[last]+[NOP]+[self.x1]+[NOP]+[self.x2]

class PlaneFirst(Gather):
    def cz(self,p,zz,k,dev):
        s=self.g.at[p,zz]
        return rc(s,s,self.ss.at[p,k],self.rs.at[p,k],dev)
    def cb(self,p,r,k,dev):
        s=self.g.at[p,self.pc.z,r]
        return rc(s,s,self.ss.at[p,self.n+k],self.rs.at[p,self.n+k],dev)
    def ch(self,p,r,lo,k,dev):
        n=self.g.shape[3]; h=(n//32)*16
        s=self.g.at[p,self.pc.z,r,pl.ds(0,h)] if lo else self.g.at[p,self.pc.z,r,pl.ds(h,n-h)]
        return rc(s,s,self.ss.at[p,self.n+k],self.rs.at[p,self.n+k],dev)

class Scatter:
    def __init__(self, pc, g, d, rx, ry, ru, rd, ss, rs, slot=lambda p: p):
        self.pc=pc;self.g=g;self.d=d;self.bx=rx;self.by=ry;self.bu=ru;self.bd=rd;self.ss=ss;self.rs=rs
        self.h=pc.nz//2; self.slot=slot
    def half(self,p,r,lo):
        h=self.h; n=self.pc.nz
        return (self.g.at[p,pl.ds(0,h),r],self.d.at[self.slot(p),pl.ds(0,h)]) if lo else (self.g.at[p,pl.ds(h,n-h),r],self.d.at[self.slot(p),pl.ds(h,n-h)])
    def c0(self,p,lo):
        s,t=self.half(p,self.pc.rd,lo); k=0 if lo else 1
        return rc(s,t,self.ss.at[self.slot(p),k],self.rs.at[self.slot(p),k],self.pc.X if lo else self.pc.Y)
    def c1(self,p,x):
        c=self.pc
        return rc(self.g.at[p,:,c.rx if x else c.ry],(self.bx if x else self.by).at[self.slot(p)],self.ss.at[self.slot(p),2 if x else 3],self.rs.at[self.slot(p),2 if x else 3],c.X if x else c.Y)
    def cu(self,p,zz,up):
        c=self.pc; k=4+zz if up else 4+c.nz+zz
        return rc(self.g.at[p,zz,c.r],(self.bu if up else self.bd).at[self.slot(p),zz],self.ss.at[self.slot(p),k],self.rs.at[self.slot(p),k],c.up if up else c.dn)
    def add(self,dst,*srcs):
        v=dst[...].astype(F32)
        for s in srcs: v=v+s[...].astype(F32)
        dst[...]=v.astype(BF)
    def s0(self,p):
        self.c0(p,True).start(); self.c0(p,False).start()
    def s1(self,p):
        c=self.pc;h=self.h;n=c.nz
        self.c0(p,True).wait_recv()
        self.add(self.g.at[p,pl.ds(0,h),c.ry],self.d.at[self.slot(p),pl.ds(0,h)])
        self.c1(p,False).start()
        self.c0(p,False).wait_recv()
        self.add(self.g.at[p,pl.ds(h,n-h),c.rx],self.d.at[self.slot(p),pl.ds(h,n-h)])
        self.c1(p,True).start()
    def s2(self,p):
        c=self.pc
        self.c1(p,True).wait_recv(); self.c1(p,False).wait_recv()
        self.add(self.g.at[p,:,c.r],self.bx.at[self.slot(p)],self.by.at[self.slot(p)])
        self.zk(p,0)
    def zk(self,p,k):
        c=self.pc; nz=c.nz
        @pl.when(c.z==k)
        def _():
            for zz in range(nz-1,k,-1):
                if k>0:
                    self.cu(p,zz,True).wait_recv()
                    self.add(self.g.at[p,zz,c.r],self.bu.at[self.slot(p),zz])
                self.cu(p,zz,True).start()
        @pl.when(c.z==nz-1-k)
        def _():
            for zz in range(0,nz-1-k):
                if k>0:
                    self.cu(p,zz,False).wait_recv()
                    self.add(self.g.at[p,zz,c.r],self.bd.at[self.slot(p),zz])
                self.cu(p,zz,False).start()
    def fin(self,p,tot,place=None):
        c=self.pc
        tot[...]=self.g[p,c.z,c.r].astype(F32)
        @pl.when(c.z>0)
        def _():
            self.cu(p,c.z,True).wait_recv()
            tot[...]+=self.bu[self.slot(p),c.z].astype(F32)
        @pl.when(c.z<c.nz-1)
        def _():
            self.cu(p,c.z,False).wait_recv()
            tot[...]+=self.bd[self.slot(p),c.z].astype(F32)
        if place is not None: place(p)
    def drain(self,p):
        c=self.pc; nz=c.nz
        self.c0(p,True).wait_send(); self.c0(p,False).wait_send()
        self.c1(p,True).wait_send(); self.c1(p,False).wait_send()
        for zz in range(nz):
            @pl.when(zz>c.z)
            def _(): self.cu(p,zz,True).wait_send()
            @pl.when(zz<c.z)
            def _(): self.cu(p,zz,False).wait_send()
    def lines(self):
        return [functools.partial(lambda k,p:self.zk(p,k),k) for k in range(1,self.pc.nz-1)]
    def steps(self,place,tot):
        return [self.s0,NOP,self.s1,NOP,self.s2]+self.lines()+[lambda p:self.fin(p,tot,place)]
    def tight(self,out):
        return [self.s0,self.s1,self.s2]+self.lines()+[lambda p:self.fin(p,out.at[0])]


EPS = 1e-5
RT = 512


def pick(static, cond, body):
    if isinstance(cond, (bool, int)):
        if cond:
            body()
    else:
        pl.when(cond)(body)


def norm_rows(values):
    mean = jnp.mean(values, axis=1, keepdims=True)
    centred = values - mean
    inverse = lax.rsqrt(jnp.mean(centred * centred, axis=1, keepdims=True) + EPS)
    return centred * inverse, inverse


def gelu_both(u):
    c = 0.7978845608028654
    u2 = u * u
    t = jnp.tanh(c * u * (1.0 + 0.044715 * u2))
    half = 0.5 + 0.5 * t
    act = u * half
    grad = half + (0.5 * c) * u * (1.0 - t * t) * (1.0 + (3 * 0.044715) * u2)
    return act, grad


def flat(ref, p):
    v = ref[p]
    return v.reshape(-1, v.shape[-1])


def tiles(n):
    return lambda f: pl.loop(0, n)(f)


def rows_of(i, n=RT):
    return pl.ds(pl.multiple_of(i * n, n), n)


def twin_copy(pc, src, dst, ss, rs):
    return rc(src, dst, ss, rs, pc.twin)


def members(cl, hh):
    return jnp.where(cl[hh] == sub((128, L)), 1.0, 0.0).astype(BF)


def pair_members(cl, p):
    return jnp.concatenate([members(cl, 2 * p), members(cl, 2 * p + 1)], 0)


def pair_own():
    return (lane((256, 128)) >= 64) == (sub((256, 128)) >= 128)


def fwd_clusters(p, qkv, cl, n_s, seg, prob_o):
    q = qkv[p, :, 0:128]
    k = qkv[p, :, 128:256]
    v = qkv[p, :, 256:384]
    own = pair_own()
    mt = pair_members(cl, p)
    cnt = jnp.maximum(jnp.sum(mt.astype(F32), axis=1, keepdims=True), 1.0)
    cen = jnp.where(own, dot(mt, q) / cnt, 0.0).astype(BF)
    s = dot((cen.astype(F32) * 0.125).astype(BF), k, NT)
    top = jnp.concatenate([jnp.transpose(n_s[2 * p + h]).astype(F32) for h in range(2)], 0) == 0.0
    c = sub((256, 1))
    cm = lax.rem(jnp.where(c < 128, c, c - 128), jnp.int32(10))
    s = jnp.where(seg[...] == cm, s, -BIG)
    e = jnp.exp(s - jnp.max(s, axis=1, keepdims=True))
    prob = e / jnp.sum(e, axis=1, keepdims=True)
    mass = jnp.sum(jnp.where(top, prob, 0.0), axis=1, keepdims=True)
    signed = jnp.where(top, -prob, prob).astype(BF)
    prob_o[2 * p] = signed[0:128]
    prob_o[2 * p + 1] = signed[128:256]
    rest = dot(jnp.where(top, 0.0, prob).astype(BF), v)
    rh, rl = split2(jnp.where(own, rest, jnp.broadcast_to(mass, (256, 128))))
    rr = jnp.concatenate([rh, rl], 1)
    return rr[0:128], rr[128:256]


def fwd_head(p, h, rr, qkv, mb, n_s, qaug, kaug, att, ex):
    odd = h == 1
    hh = 2 * p + h
    k = qkv[p, :, 128:256]
    ln = lane((L, 128))
    mine = (ln >= 64) if odd else (ln < 64)
    zero = jnp.zeros((), BF)
    vaug = jnp.where(mine, qkv[p, :, 256:384], jnp.ones((), BF))
    qaug[:, :128] = (jnp.where(mine, qkv[p, :, 0:128], zero).astype(F32) * 0.125).astype(BF)
    qaug[:, 128:] = mb[hh]
    kaug[:, :128] = k
    kaug[:, 128:] = n_s[hh]
    lt = lane((TQ, 128))
    minet = (lt >= 64) if odd else (lt < 64)
    cols = pl.ds(pl.multiple_of(p * 128, 128), 128)
    for t in range(L // TQ):
        sl = pl.ds(t * TQ, TQ)
        sc = dot(qaug[sl, :], kaug[...], NT)
        mm = jnp.max(sc, axis=1, keepdims=True)
        pr = jnp.exp(sc - mm).astype(BF)
        o = dot(pr, vaug)
        mt_ = qaug[sl, 128:]
        ee = dot(mt_, rr)
        ee = ee[:, :128] + ee[:, 128:]
        osw = pltpu.roll(o, 64, 1)
        esw = pltpu.roll(ee, 64, 1)
        exact = o / osw
        a = exact * esw + ee
        tot = jnp.where(minet, osw, o)
        ms = jnp.where(minet, esw, ee)
        lse = mm + jnp.log(tot) - jnp.log(jnp.maximum(ms, 1e-37))
        h3, m3, l3 = split3(lse)
        mb[hh, sl, :] = jnp.where(lt == 100, h3.astype(F32), jnp.where(lt == 101, m3.astype(F32), jnp.where(lt == 102, l3.astype(F32), mt_.astype(F32)))).astype(BF)
        if odd:
            att[sl, cols] = jnp.where(lt < 64, att[sl, cols], a.astype(BF))
            ex[sl, cols] = jnp.where(lt < 64, ex[sl, cols], exact.astype(BF))
        else:
            att[sl, cols] = a.astype(BF)
            ex[sl, cols] = exact.astype(BF)


def as_column(row):
    n = row.shape[1]
    eye = sub((n, n)) == lane((n, n))
    return jnp.sum(jnp.where(eye, row.astype(F32), 0.0), axis=1, keepdims=True)


def fill_own(pc, g, gg, q3, oT, upw, dT, ga, gf):
    for p in range(3):
        for i in range(3):
            g[p, pc.z, pc.r, :, i * 128:(i + 1) * 128] = q3[i, :, p * 128:(p + 1) * 128]
    g[3, pc.z, pc.r] = oT[...]
    for q in range(4):
        g[4 + q, pc.z, pc.r] = upw[:, q * 384:(q + 1) * 384]
        g[8 + q, pc.z, pc.r] = dT[:, q * 384:(q + 1) * 384]
    R = oT.shape[0]
    ln = lane((R, 128))
    gg[0, pc.z, pc.r] = jnp.where(ln == 0, as_column(ga[...]), jnp.where(ln == 1, as_column(gf[...]), 0.0)).astype(BF)


def bwd_clusters(p, cl, s, gaugs, dq_o, dk_o, dv_o):
    qkv = s["qkv"]
    cols = pl.ds(pl.multiple_of(p * 128, 128), 128)
    qv = qkv[p, :, 0:128]
    kv = qkv[p, :, 128:256]
    vv = qkv[p, :, 256:384]
    gv = s["gatt"][:, cols]
    ln = lane((L, 128))
    lc = lane((256, 128))
    row = sub((256, 128))
    own = pair_own()
    prod = gv.astype(F32) * s["ex"][:, cols].astype(F32)
    dots = jnp.zeros((L, 128), F32)
    for h in range(2):
        mine = (ln >= 64) if h else (ln < 64)
        o = 0 if h else 64
        three = [a.astype(F32) for a in split3(jnp.sum(jnp.where(mine, prod, 0.0), axis=1, keepdims=True))]
        ga = jnp.where(mine, gv.astype(F32), 0.0)
        for i, a in enumerate(three):
            ga = jnp.where(ln == o + i, a, ga)
            dots = jnp.where(ln == 3 * h + i, a, dots)
        gaugs[h][...] = ga.astype(BF)
    mt = pair_members(cl, p)
    cnt = jnp.maximum(jnp.sum(mt.astype(F32), axis=1, keepdims=True), 1.0)
    cq = dot(mt, jnp.concatenate([qv, gv], 1))
    cen = jnp.where(own, cq[:, 0:128] / cnt, 0.0).astype(BF)
    cs = (cen.astype(F32) * 0.125).astype(BF)
    grest = jnp.where(own, cq[:, 128:256], 0.0).astype(BF)
    gm = dot(mt, dots.astype(BF))
    lo = jnp.where(row >= 128, 3, 0)
    gmass = jnp.sum(jnp.where((lc >= lo) & (lc < lo + 3), gm, 0.0), axis=1, keepdims=True)
    signed = jnp.concatenate([s["prob"][2 * p], s["prob"][2 * p + 1]], 0).astype(F32)
    top = signed < 0.0
    prob = jnp.abs(signed)
    gp = jnp.where(top, gmass, dot(grest, vv, NT))
    gs = (prob * (gp - jnp.sum(prob * gp, axis=1, keepdims=True))).astype(BF)
    rw = jnp.where(top, 0.0, prob).astype(BF)
    gcen = jnp.where(own, dot(gs, kv) / cnt, 0.0)
    gh, gl = split2(gcen)
    dk_o[...] = dot(jnp.transpose(gs), cs)
    dv_o[...] = dot(jnp.transpose(rw), grest)
    zero = jnp.zeros((), BF)
    two = jnp.concatenate([jnp.where(ln < 100, s["mb"][2 * p + h], zero) for h in range(2)], 1)
    dd = dot(two, jnp.concatenate([gh, gl], 1))
    dq_o[...] = dd[:, :128] + dd[:, 128:]


def bwd_head(p, h, s, qaug, kaug, gaug, vaug, dk_o, dv_o, dqt):
    qkv = s["qkv"]
    hh = 2 * p + h
    cols = pl.ds(pl.multiple_of(p * 128, 128), 128)
    kv = qkv[p, :, 128:256]
    ln = lane((L, 128))
    zero = jnp.zeros((), BF)
    mine = (ln >= 64) if h else (ln < 64)
    o = 0 if h else 64
    gm = jnp.where(mine, s["gatt"][:, cols], zero)
    vaug[...] = jnp.where(mine, qkv[p, :, 256:384], jnp.where((ln >= o) & (ln < o + 3), jnp.full((), -1.0, BF), zero))
    qs = (jnp.where(mine, qkv[p, :, 0:128], zero).astype(F32) * 0.125).astype(BF)
    qaug[:, :128] = qs
    qaug[:, 128:] = s["mb"][hh]
    kaug[:, :128] = kv
    kaug[:, 128:] = s["ns"][hh]
    kTh = jnp.transpose(kv)[64 * h:64 * h + 64]
    for t in range(L // TJ):
        sl = pl.ds(t * TJ, TJ)
        pr = jnp.exp(dot(kaug[sl, :], qaug[...], NT))
        ds = (pr * dot(vaug[sl, :], gaug[...], NT)).astype(BF)
        dv_o[sl, :] += dot(pr.astype(BF), gm)
        dk_o[sl, :] += dot(ds, qs)
        dqp = dot(kTh[:, t * TJ:(t + 1) * TJ], ds)
        if t == 0:
            dqt[64 * h:64 * h + 64, :] = dqp
        else:
            dqt[64 * h:64 * h + 64, :] += dqp


def place_sum(p, tot, outs):
    qg, og, ug, dg = outs

    def pair(p):
        for i in range(3):
            qg[i, :, pl.ds(pl.multiple_of(p * 128, 128), 128)] = tot[:, i * 128:(i + 1) * 128]

    def wide(ref, q):
        ref[:, pl.ds(pl.multiple_of(q * 384, 128), 384)] = tot[...]

    pick(None, (8 <= p < 12) if isinstance(p, int) else (p >= 8) & (p < 12), lambda: pair(p - 8))
    pick(None, p == 3, lambda: og.__setitem__(..., tot[...]))
    pick(None, (3 < p < 8) if isinstance(p, int) else (p > 3) & (p < 8), lambda: wide(ug, p - 4))
    pick(None, p >= 12, lambda: wide(dg, p - 12))


def finish_body(*refs):
    ins, gg, outs, (g1, g2), bufs, (si, so) = refs[:6], refs[6], refs[7:13], refs[13:15], refs[15:21], refs[21:]
    cuts = [(i, j * (a.shape[0] // n), a.shape[0] // n) for i, (a, n) in enumerate(zip(ins, (2, 4, 3, 1, 1, 1))) for j in range(n)]
    ci = [pltpu.make_async_copy(ins[i].at[pl.ds(o, n)], bufs[i].at[pl.ds(o, n)], si.at[k]) for k, (i, o, n) in enumerate(cuts)]
    co = [pltpu.make_async_copy(bufs[i].at[pl.ds(o, n)], outs[i].at[pl.ds(o, n)], so.at[k]) for k, (i, o, n) in enumerate(cuts)]
    for c in ci:
        c.start()
    R = gg.shape[1]
    eye = sub((R, R)) == lane((R, R))
    for i, g in enumerate((g1, g2)):
        g[...] = jnp.sum(jnp.where(eye, gg[0, :, i:i + 1], 0.0), axis=0, keepdims=True)
    for a, b in zip(ci, co):
        a.wait()
        b.start()
    for c in co:
        c.wait()


def finish(*arrays):
    V = pl.BlockSpec(memory_space=pltpu.VMEM)
    A = pl.BlockSpec(memory_space=pl.ANY)
    R = arrays[6].shape[1]
    dma = pltpu.SemaphoreType.DMA
    return pl.pallas_call(
        finish_body,
        out_shape=[jax.ShapeDtypeStruct(a.shape, a.dtype) for a in arrays[:6]] + [jax.ShapeDtypeStruct((1, R), F32)] * 2,
        in_specs=[A] * 6 + [V], out_specs=[A] * 6 + [V] * 2,
        scratch_shapes=[pltpu.VMEM(a.shape, a.dtype) for a in arrays[:6]] + [dma((12,)), dma((12,))],
        compiler_params=pltpu.CompilerParams(vmem_limit_bytes=60 << 20),
    )(*arrays)


def scratch_shapes(custom, nz, R):
    f = lambda *s: (s, F32)
    b = lambda *s: (s, BF)
    wide = (16, nz, 4, R, 384) if custom else (16, 768, 384)
    return {
        "gr": f(8, 768), "n1": b(L, 768), "qkv": b(3, L, 384), "att": b(L, 384), "ex": b(L, 384), "mb": b(6, L, 128),
        "ns": b(6, L, 128), "prob": b(6, 128, L), "hid": f(L, 768), "n2": b(L, 768), "act": b(4, L, 384), "dg": b(4, L, 384),
        "aT": b(768, L), "eb": b(L, 768), "er": b(L, 768), "fr": b(L // 2, 768), "gatt": b(L, 384),
        "qaug": b(L, 256), "kaug": b(L, 256), "gaug": b(L, 128), "gaug1": b(L, 128), "vaug": b(L, 128),
        "dqs": f(L, 128), "dks": f(L, 128), "dvs": f(L, 128), "dqt": f(128, L), "gacc": f(8, 768),
        "wg": b(*wide),
    }


def layer_body(nb, custom, names, *refs):
    refs = list(refs)
    take = lambda n: [refs.pop(0) for _ in range(n)]
    x, ct, seg, cl, tt = take(5)
    own = take(6 if custom else 2)
    y, tg, out_g = take(3)
    out_s = take(4) if custom else take(1)[0]
    s = dict(zip(names, take(len(names))))
    tpad, es, ers, vs, vrs = take(5)
    pc = Place(nb)
    wg, hid, n1, n2, qkv, att, ex, act, dg = (s[n] for n in ("wg", "hid", "n1", "n2", "qkv", "att", "ex", "act", "dg"))
    aT, eb, er, fr, gr, gacc = (s[n] for n in ("aT", "eb", "er", "fr", "gr", "gacc"))
    half, nh, nt = L // 2, L // 2 // RT, L // RT

    if custom:
        gg, tot, gbuf, ss, rs, gss, grs, ss2, rs2, gss2, grs2, gown, gtwin = take(13)
        land, gland = take(5), take(5)
        G, Gg = Gather(pc, wg, ss, rs), Gather(pc, gg, gss, grs)
        S = Scatter(pc, wg, *land, ss2, rs2, slot=lambda p: (p - 4 if p >= 12 else p - 8 if p >= 8 else p) if isinstance(p, int) else jnp.where(p >= 12, p - 4, jnp.where(p >= 8, p - 8, p)))
        Sg = Scatter(pc, gbuf, *gland, gss2, grs2)
        Gp = PlaneFirst(pc, wg, ss, rs)
        m = pc.nz - 1

        def last(p):
            G.zk(p, m)
            G.x0(p)

        def turn(p):
            Gp.x2(p)
            Gp.z0(p)
        line = lambda g, off: [(off + d, functools.partial(lambda d, p: g.zk(p, d), d)) for d in range(1, m)][::-1]
        nine = lambda k: k + k // 3
        three = lambda k: k + 3
        rest = list(range(1, 9))
        gather = [(m + 2, G.x2, [0], nine), (m + 1, G.x1, [0], nine), (m + 3, G.x2, rest, nine), (m + 2, G.x1, rest, nine)]
        gather += [(e, fn, list(range(9)), nine) for e, fn in [(m, last)] + line(G, 0) + [(0, G.z0)]]
        gather += [(9, G.drain, list(range(9)), nine), (8, Gp.drain, [0, 4, 8], three)]
        gather += [(e, fn, [0, 4, 8], three) for e, fn in [(m + 3, lambda p: Gp.zk(p, m))] + line(Gp, 3) + [(2, turn), (1, Gp.x1), (0, Gp.x0)]]
        gsteps = [Gg.z0] + [functools.partial(lambda d: Gg.zk(0, d), d) for d in range(1, m)] + [None, Gg.x1, Gg.x2]
        ssteps = S.steps(lambda p: place_sum(p, tot, out_s), tot)
        tails = Sg.tight(gown)
        starts = {13: 12, 14: 13, 15: 14, 16: 15, 17: 4, 18: 5, 19: 6, 20: 7, 21: 3, 22: 8, 23: 9, 25: 10}

        def tick(t, span=None):
            fixed = isinstance(t, int)
            ts = [t] if fixed else list(range(*span))
            for i in range(len(ssteps) - 1, -1, -1):
                hits = [u - i for u in ts if u - i in starts]
                if not hits or ssteps[i] is NOP:
                    continue
                if fixed:
                    ssteps[i](starts[hits[0]])
                    continue
                u = t - i
                ok = functools.reduce(jnp.logical_or, [u == k for k in hits])
                part = functools.reduce(lambda a, k: jnp.where(u == k, starts[k], a), hits, 0)
                pl.when(ok)(lambda i=i, part=part: ssteps[i](part))
            for off, fn, at, to in gather:
                hits = [u - off for u in ts if u - off in at]
                if not hits:
                    continue
                u = t - off
                ok = True if fixed else functools.reduce(jnp.logical_or, [u == k for k in hits])
                pick(None, ok, lambda fn=fn, p=to(u): fn(p))
            if fixed and t < len(gsteps):
                if t == m:
                    Gg.zk(0, m)
                    Gg.x0(0)
                elif t == 0:
                    gsteps[0](0)
                elif t < m:
                    gsteps[t]()
                else:
                    gsteps[t](0)
    else:
        tick = lambda t, span=None: None

    tpad[...] = jnp.full_like(tpad, -1)
    pc.barrier()
    if custom:
        fill_own(pc, wg, gg, *own)
    tick(0)

    @tiles(nt)
    def _(i):
        hid[rows_of(i), :] = norm_rows(x[rows_of(i), :].astype(F32))[0]

    tick(1)

    def mask(h):
        tpad[:, 0:tt.shape[2]] = tt[h]
        a, n = build_masks(cl[h], tpad[...])
        s["mb"][h], s["ns"][h] = a, n

    def transpose_into(src):
        for i in range(nt):
            aT[:, i * RT:(i + 1) * RT] = jnp.transpose(src[i * RT:(i + 1) * RT, :])

    def put(p, left, right):
        wg[p] = dot(left, right).astype(BF).reshape(wg.shape[1:])

    pl.loop(0, 2)(mask)
    tick(2)
    pl.loop(2, 4)(mask)
    tick(3)
    pl.loop(4, 6)(mask)
    transpose_into(ct)
    tick(4)
    tick(5)
    if custom:
        gains = gg[0].reshape(768, 128)
    else:
        c = pltpu.make_async_copy(own[0], wg.at[0:12], vs)
        c.start()
        c.wait()
        gains = own[1][...]
    gr[...] = jnp.transpose(gains.astype(F32))[0:8]

    @tiles(nt)
    def _(i):
        n1[rows_of(i), :] = (hid[rows_of(i), :] * gr[0:1, :]).astype(BF)

    @pl.loop(0, 3)
    def _(p):
        @tiles(nt)
        def _(i):
            qkv[p, rows_of(i), :] = dot(n1[rows_of(i), :], flat(wg, p)).astype(BF)
        rr = fwd_clusters(p, qkv, cl, s["ns"], seg, s["prob"])
        fwd_head(p, 0, rr[0], qkv, s["mb"], s["ns"], s["qaug"], s["kaug"], att, ex)
        pl.when(p == 0)(lambda: tick(6))
        fwd_head(p, 1, rr[1], qkv, s["mb"], s["ns"], s["qaug"], s["kaug"], att, ex)
        tick(7 + p, (7, 10))

    def send(k, src, dst, i):
        return twin_copy(pc, src.at[rows_of(i)], dst.at[rows_of(i)], es.at[k + i], ers.at[k + i])

    @tiles(nt)
    def _(i):
        eb[rows_of(i), :] = dot(att[rows_of(i), :], flat(wg, 3), NT).astype(BF)
        send(0, eb, er, i).start()

    tick(10)

    @tiles(nt)
    def _(i):
        r = rows_of(i)
        send(0, eb, er, i).wait()
        hv = x[r, :].astype(F32) + (eb[r, :].astype(F32) + er[r, :].astype(F32))
        hid[r, :] = hv
        n2[r, :] = (norm_rows(hv)[0] * gr[1:2, :]).astype(BF)

    def up(q):
        @tiles(nt)
        def _(i):
            a, d = gelu_both(dot(n2[rows_of(i), :], flat(wg, 4 + q)))
            act[q, rows_of(i), :] = a.astype(BF)
            dg[q, rows_of(i), :] = d.astype(BF)

    def down_grad(q):
        up(q)
        put(12 + q, aT[...], act[q])

    tick(11)
    pl.loop(0, 2)(down_grad)
    tick(12)
    def gate(q):
        @tiles(nt)
        def _(i):
            ga = dot(ct[rows_of(i), :], flat(wg, 8 + q))
            dg[q, rows_of(i), :] = (ga * dg[q, rows_of(i), :].astype(F32)).astype(BF)

    pl.loop(2, 4)(down_grad)
    tick(13)
    pl.loop(0, 2)(gate)
    tick(14)
    transpose_into(n2)

    def part(i):
        acc = dot(act[0, rows_of(i), :], flat(wg, 8), NT)
        for q in range(1, 4):
            acc += dot(act[q, rows_of(i), :], flat(wg, 8 + q), NT)
        return acc

    @tiles(nh)
    def _(i):
        eb[rows_of(i), :] = part((1 - pc.h) * nh + i).astype(BF)
        send(4, eb, fr, i).start()

    tick(15)

    pl.loop(2, 4)(gate)

    @tiles(nh)
    def _(i):
        acc = part(pc.h * nh + i).astype(BF).astype(F32)
        send(4, eb, fr, i).wait()
        y[rows_of(i), :] = (hid[rows_of(pc.h * nh + i), :] + (acc + fr[rows_of(i), :].astype(F32))).astype(BF)

    tick(16)
    @tiles(nt)
    def _(i):
        acc = dot(dg[0, rows_of(i), :], flat(wg, 4), NT)
        for q in range(1, 4):
            acc += dot(dg[q, rows_of(i), :], flat(wg, 4 + q), NT)
        eb[rows_of(i), :] = acc.astype(BF)
        send(6, eb, er, i).start()

    def up_grad(q):
        put(4 + q, aT[...], dg[q])

    pl.loop(0, 4)(up_grad)
    tick(17)
    gacc[...] = jnp.zeros_like(gacc)
    gat = n2

    @tiles(nt)
    def _(i):
        r = rows_of(i)
        send(6, eb, er, i).wait()
        gn = eb[r, :].astype(F32) + er[r, :].astype(F32)
        n, inv = norm_rows(hid[r, :])
        a = gn * gr[1:2, :]
        back = (a - jnp.mean(a, axis=1, keepdims=True) - n * jnp.mean(a * n, axis=1, keepdims=True)) * inv
        gh = ct[r, :].astype(F32) + back
        gat[r, :] = gh.astype(BF)

        @pl.when((i >= pc.h * nh) & (i < pc.h * nh + nh))
        def _():
            tg[rows_of(i - pc.h * nh), :] = gh
            gacc[1:2, :] += jnp.sum(gn * n, axis=0, keepdims=True)

    tick(18)

    @tiles(nt)
    def _(i):
        s["gatt"][rows_of(i), :] = dot(gat[rows_of(i), :], flat(wg, 3)).astype(BF)

    transpose_into(gat)
    put(3, aT[...], att[...])
    tick(19)
    transpose_into(n1)
    nacc = hid
    dqkv = att

    @pl.loop(0, 3)
    def _(p):
        bwd_clusters(p, cl, s, (s["gaug"], s["gaug1"]), s["dqs"], s["dks"], s["dvs"])
        bwd_head(p, 0, s, s["qaug"], s["kaug"], s["gaug"], s["vaug"], s["dks"], s["dvs"], s["dqt"])
        tick(20 + 2 * p, (20, 26, 2))
        bwd_head(p, 1, s, s["qaug"], s["kaug"], s["gaug1"], s["vaug"], s["dks"], s["dvs"], s["dqt"])
        dqkv[:, 0:128] = ((s["dqs"][...] + jnp.transpose(s["dqt"][...])) * 0.125).astype(BF)
        dqkv[:, 128:256] = s["dks"][...].astype(BF)
        dqkv[:, 256:384] = s["dvs"][...].astype(BF)

        put(8 + p, aT[...], dqkv[...])
        tick(21 + 2 * p, (21, 27, 2))

        @tiles(nt)
        def _(i):
            v = dot(dqkv[rows_of(i), :], flat(wg, p), NT)

            @pl.when(p == 0)
            def _():
                nacc[rows_of(i), :] = v

            @pl.when(p > 0)
            def _():
                nacc[rows_of(i), :] += v

    @tiles(nh)
    def _(i):
        eb[rows_of(i), :] = nacc[rows_of((1 - pc.h) * nh + i), :].astype(BF)
        send(10, eb, fr, i).start()

    @tiles(nt)
    def _(i):
        n = norm_rows(x[rows_of(i), :].astype(F32))[0]
        gacc[0:1, :] += jnp.sum(nacc[rows_of(i), :] * n, axis=0, keepdims=True)

    if custom:
        wide = jnp.concatenate([gacc[...], jnp.zeros((120, 768), F32)], 0)
        gbuf[0] = jnp.transpose(wide).astype(BF).reshape(gbuf.shape[1:])

    def late(t):
        tick(t)
        if custom and t - 26 < len(tails):
            tails[t - 26](0)

    late(26)
    late(27)

    @tiles(nh)
    def _(i):
        r = rows_of(i)
        send(10, eb, fr, i).wait()
        gn = nacc[rows_of(pc.h * nh + i), :].astype(BF).astype(F32) + fr[r, :].astype(F32)
        n, inv = norm_rows(x[rows_of(pc.h * nh + i), :].astype(F32))
        a = gn * gr[0:1, :]
        back = (a - jnp.mean(a, axis=1, keepdims=True) - n * jnp.mean(a * n, axis=1, keepdims=True)) * inv
        tg[r, :] += back

    if custom:
        @pl.loop(0, 9)
        def _(i):
            S.drain(jnp.where(i < 5, i + 3, i + 7))

        for t in range(28, max(25 + len(ssteps), 26 + len(tails))):
            late(t)
            if t == 25 + len(tails):
                cv = twin_copy(pc, gown, gtwin, vs, vrs)
                cv.start()

        @pl.loop(8, 11)
        def _(p):
            S.drain(p)
        Sg.drain(0)
        Gg.drain(0)
        cv.wait()
        out_g[0] = gown[0] + gtwin[0]
    else:
        c = pltpu.make_async_copy(wg, out_s, vs)
        c.start()
        out_g[...] = gacc[...]
        c.wait()


def layer(nb, custom, *args):
    V = pl.BlockSpec(memory_space=pltpu.VMEM)
    A = pl.BlockSpec(memory_space=pl.ANY)
    nz = nb // 4
    dma = pltpu.SemaphoreType.DMA
    tt, ws = args[4], args[5:]
    R = ws[1].shape[0]
    shapes = scratch_shapes(custom, nz, R)
    out_shape = [jax.ShapeDtypeStruct((L // 2, 768), BF), jax.ShapeDtypeStruct((L // 2, 768), F32)]
    if custom:
        out_shape += [jax.ShapeDtypeStruct(sh, F32) for sh in ((1, R, 128), (3, R, 384), (R, 384), (R, 1536), (R, 1536))]
        out_specs = [V] * 7
        in_specs = [V] * len(args)
    else:
        out_shape += [jax.ShapeDtypeStruct((8, 768), F32), jax.ShapeDtypeStruct(shapes["wg"][0], BF)]
        out_specs = [V, V, V, A]
        in_specs = [V] * 5 + [A, V]
    scratch = [pltpu.VMEM(*sd) for sd in shapes.values()] + [pltpu.VMEM((tt.shape[1], 128), jnp.int32), dma((12,)), dma((12,)), dma, dma]
    if custom:
        ns, n2 = 2 * (nz - 1) + 4, 4 + 2 * nz
        vb = lambda *sh: pltpu.VMEM(sh, BF)
        scratch += [vb(1, nz, 4, R, 128), pltpu.VMEM((R, 384), F32), vb(1, nz, 4, R, 128), dma((12, ns)), dma((12, ns)), dma((1, ns)), dma((1, ns)),
                    dma((12, n2)), dma((12, n2)), dma((1, n2)), dma((1, n2)), pltpu.VMEM((1, R, 128), F32), pltpu.VMEM((1, R, 128), F32)] + [vb(12, nz, R, 384)] * 5 + [vb(1, nz, R, 128)] * 5
    return pl.pallas_call(
        functools.partial(layer_body, nb, custom, tuple(shapes)),
        out_shape=out_shape, in_specs=in_specs, out_specs=out_specs, scratch_shapes=scratch,
        compiler_params=pltpu.CompilerParams(collective_id=0, has_side_effects=True, vmem_limit_bytes=int(63.9 * (1 << 20))),
    )(*args)


def on_device(tokens, attn_gain, qkv_weight, out_weight, ffn_gain, up_weight, down_weight, cotangent, segment, cluster, top_keys):
    nb = lax.axis_size("batch")
    R = qkv_weight.shape[0]
    custom = R % 16 == 0 and nb % 4 == 0
    x, ct = tokens[0], cotangent[0]
    tt = top_keys[0].transpose(0, 2, 1)
    if custom:
        ws = (qkv_weight.transpose(1, 0, 2), out_weight.T, up_weight, down_weight.T, attn_gain[None], ffn_gain[None])
    else:
        w = pack(qkv_weight, out_weight, up_weight, down_weight)
        gw = jnp.pad(jnp.stack([attn_gain, ffn_gain], 1), ((0, 0), (0, 126)))
        ws = (lax.all_gather(w, "batch", axis=1, tiled=True), lax.all_gather(gw, "batch", axis=0, tiled=True))
    y, tg, gg, *S = layer(nb, custom, x, ct, segment, cluster[0][:, None, :], tt, *ws)
    if custom:
        y, tg, qg, og, ug, dg, g1, g2 = finish(y, tg, *S, gg)
        return y[None], tg[None], g1[0], qg.transpose(1, 0, 2), og.T, g2[0], ug, dg.T
    S = lax.psum_scatter(S[0].astype(F32), "batch", scatter_dimension=1, tiled=True)
    g = lax.psum_scatter(lax.psum(gg, "head"), "batch", scatter_dimension=1, tiled=True)
    cat = lambda a: a.transpose(1, 0, 2).reshape(R, -1)
    qg = S[8:11].reshape(3, R, 3, 128).transpose(1, 2, 0, 3).reshape(R, 3, 384)
    return y[None], tg[None], g[0], qg, S[3].T, g[1], cat(S[4:8]), cat(S[12:16]).T


def pack(q, o, u, d):
    R = q.shape[0]
    qp = q.reshape(R, 3, 3, 128).transpose(2, 0, 1, 3).reshape(3, R, 384)
    up = u.reshape(R, 4, 384).transpose(1, 0, 2)
    dn = d.T.reshape(R, 4, 384).transpose(1, 0, 2)
    return jnp.concatenate([qp, o.T[None], up, dn], 0)


def solution(mesh):
    in_specs = (P("batch", None, None), P("batch"), P("batch", None, "head"), P("head", "batch"), P("batch"), P("batch", "head"), P("head", "batch"), P("batch", None, None), P("batch", None), P("batch", "head", None), P("batch", "head", None, None))
    out_specs = (P("batch", "head", None), P("batch", "head", None), P("batch"), P("batch", None, "head"), P("head", "batch"), P("batch"), P("batch", "head"), P("head", "batch"))
    return jax.shard_map(on_device, mesh=mesh, in_specs=in_specs, out_specs=out_specs, check_vma=False)
```

```python
import functools

import jax
import jax.numpy as jnp
from jax import lax
from jax.experimental import pallas as pl
from jax.experimental.pallas import tpu as pltpu
from jax.sharding import PartitionSpec as P

F32=jnp.float32; BF=jnp.bfloat16
BIG=1e30
NT=(((1,),(1,)),((),()))
TN=(((0,),(0,)),((),()))
NN=(((1,),(0,)),((),()))
def dot(a,b,dims=NN): return lax.dot_general(a,b,dims,preferred_element_type=F32)
def split3(x):
    a=x.astype(BF); r=x-a.astype(F32); b=r.astype(BF); c=(r-b.astype(F32)).astype(BF)
    return a,b,c
def split2(x):
    a=x.astype(BF); return a,(x-a.astype(F32)).astype(BF)
L=1024
def lane(shape): return lax.broadcasted_iota(jnp.int32,shape,len(shape)-1)
def sub(shape): return lax.broadcasted_iota(jnp.int32,shape,len(shape)-2)

def build_masks(own_row, topT):
    mt=jnp.where(own_row==sub((128,L)),1.0,0.0).astype(BF)
    m=jnp.transpose(mt)
    hi=lax.shift_right_arithmetic(topT,5); bit=lax.shift_left(jnp.int32(1),topT&31)
    words=L//32
    a_iota=sub((words,128))
    w=jnp.zeros((words,128),jnp.int32)
    for t in range(topT.shape[0]):
        w=w|jnp.where(hi[t:t+1]==a_iota,bit[t:t+1],0)
    b_iota=sub((32,128)); ln=lane((32,128))
    extra=(ln>=100)&(ln<103)
    ns=[]
    for a in range(words):
        b=(lax.shift_right_logical(jnp.broadcast_to(w[a:a+1],(32,128)),b_iota)&1)
        ns.append(jnp.where(extra,-1.0,jnp.where(b==1,0.0,-BIG)))
    n=jnp.concatenate(ns,0).astype(BF)
    return m,n


TQ = 512
TJ = 512
MESH=pl.DeviceIdType.MESH


def NOP(p): pass
class Place:
    def __init__(self, nb):
        self.nz=nb//4
        self.b=lax.axis_index("batch"); self.h=lax.axis_index("head")
        self.z=self.b//4; self.r=lax.rem(self.b,4)
        even=lax.rem(self.r,2)==0
        self.rx=jnp.where(even,self.r+1,self.r-1)
        self.ry=jnp.where(self.r<2,self.r+2,self.r-2)
        self.rd=3-self.r
        self.X=(self.z*4+self.rx,self.h); self.Y=(self.z*4+self.ry,self.h)
        self.up=(self.b+4,self.h); self.dn=(self.b-4,self.h); self.twin=(self.b,1-self.h)
    def greet(self):
        bar=pltpu.get_barrier_semaphore()
        for d in (self.X,self.Y,self.twin):
            pl.semaphore_signal(bar,inc=1,device_id=d,device_id_type=MESH)
        @pl.when(self.z<self.nz-1)
        def _(): pl.semaphore_signal(bar,inc=1,device_id=self.up,device_id_type=MESH)
        @pl.when(self.z>0)
        def _(): pl.semaphore_signal(bar,inc=1,device_id=self.dn,device_id_type=MESH)
    def meet(self):
        bar=pltpu.get_barrier_semaphore()
        lines=jnp.where(self.z<self.nz-1,1,0)+jnp.where(self.z>0,1,0)
        pl.semaphore_wait(bar,3+lines)

def rc(src,dst,ss,rs,dev):
    return pltpu.make_async_remote_copy(src_ref=src,dst_ref=dst,send_sem=ss,recv_sem=rs,device_id=dev,device_id_type=MESH)

class Gather:
    def __init__(self, pc, g, ss, rs):
        self.pc=pc; self.g=g; self.ss=ss; self.rs=rs; self.n=2*(pc.nz-1)
    def cz(self,p,zz,k,dev):
        s=self.g.at[p,zz,self.pc.r]
        return rc(s,s,self.ss.at[p,k],self.rs.at[p,k],dev)
    def z0(self,p):
        c=self.pc
        @pl.when(c.z<c.nz-1)
        def _(): self.cz(p,c.z,0,c.up).start()
        @pl.when(c.z>0)
        def _(): self.cz(p,c.z,1,c.dn).start()
    def zk(self,p,d):
        c=self.pc
        @pl.when(c.z-d>=0)
        def _():
            self.cz(p,c.z-d,2*(d-1),c.up).wait_recv()
        if d<c.nz-1:
            @pl.when((c.z-d>=0)&(c.z<c.nz-1))
            def _(): self.cz(p,c.z-d,2*d,c.up).start()
        @pl.when(c.z+d<c.nz)
        def _():
            self.cz(p,c.z+d,2*(d-1)+1,c.dn).wait_recv()
        if d<c.nz-1:
            @pl.when((c.z+d<c.nz)&(c.z>0))
            def _(): self.cz(p,c.z+d,2*d+1,c.dn).start()
    def cb(self,p,r,k,dev):
        s=self.g.at[p,:,r]
        return rc(s,s,self.ss.at[p,self.n+k],self.rs.at[p,self.n+k],dev)
    def ch(self,p,r,lo,k,dev):
        h=self.pc.nz//2
        s=self.g.at[p,pl.ds(0,h),r] if lo else self.g.at[p,pl.ds(h,self.pc.nz-h),r]
        return rc(s,s,self.ss.at[p,self.n+k],self.rs.at[p,self.n+k],dev)
    def x0(self,p):
        c=self.pc
        self.cb(p,c.r,0,c.X).start(); self.cb(p,c.r,1,c.Y).start()
    def x1(self,p):
        c=self.pc
        self.cb(p,c.rx,0,c.X).wait_recv()
        self.ch(p,c.rx,True,2,c.Y).start()
        self.cb(p,c.ry,1,c.Y).wait_recv()
        self.ch(p,c.ry,False,3,c.X).start()
    def x2(self,p):
        c=self.pc
        self.ch(p,c.rd,True,2,c.Y).wait_recv()
        self.ch(p,c.rd,False,3,c.X).wait_recv()
    def drain(self,p):
        c=self.pc
        for d in range(c.nz-1):
            @pl.when((c.z-d>=0)&(c.z<c.nz-1))
            def _(): self.cz(p,c.z-d,2*d,c.up).wait_send()
            @pl.when((c.z+d<c.nz)&(c.z>0))
            def _(): self.cz(p,c.z+d,2*d+1,c.dn).wait_send()
        self.cb(p,c.r,0,c.X).wait_send(); self.cb(p,c.r,1,c.Y).wait_send()
        self.ch(p,c.rx,True,2,c.Y).wait_send(); self.ch(p,c.ry,False,3,c.X).wait_send()
    def steps(self):
        nz=self.pc.nz
        def last(p):
            self.zk(p,nz-1); self.x0(p)
        return [self.z0]+[functools.partial(lambda d,p:self.zk(p,d),d) for d in range(1,nz-1)]+[last]+[NOP]+[self.x1]+[NOP]+[self.x2]

class PlaneFirst(Gather):
    def cz(self,p,zz,k,dev):
        s=self.g.at[p,zz]
        return rc(s,s,self.ss.at[p,k],self.rs.at[p,k],dev)
    def cb(self,p,r,k,dev):
        s=self.g.at[p,self.pc.z,r]
        return rc(s,s,self.ss.at[p,self.n+k],self.rs.at[p,self.n+k],dev)
    def ch(self,p,r,lo,k,dev):
        n=self.g.shape[3]; h=(n//32)*16
        s=self.g.at[p,self.pc.z,r,pl.ds(0,h)] if lo else self.g.at[p,self.pc.z,r,pl.ds(h,n-h)]
        return rc(s,s,self.ss.at[p,self.n+k],self.rs.at[p,self.n+k],dev)

class Scatter:
    def __init__(self, pc, g, d, rx, ry, ru, rd, ss, rs, slot=lambda p: p):
        self.pc=pc;self.g=g;self.d=d;self.bx=rx;self.by=ry;self.bu=ru;self.bd=rd;self.ss=ss;self.rs=rs
        self.h=pc.nz//2; self.slot=slot
    def half(self,p,r,lo):
        h=self.h; n=self.pc.nz
        return (self.g.at[p,pl.ds(0,h),r],self.d.at[self.slot(p),pl.ds(0,h)]) if lo else (self.g.at[p,pl.ds(h,n-h),r],self.d.at[self.slot(p),pl.ds(h,n-h)])
    def c0(self,p,lo):
        s,t=self.half(p,self.pc.rd,lo); k=0 if lo else 1
        return rc(s,t,self.ss.at[self.slot(p),k],self.rs.at[self.slot(p),k],self.pc.X if lo else self.pc.Y)
    def c1(self,p,x):
        c=self.pc
        return rc(self.g.at[p,:,c.rx if x else c.ry],(self.bx if x else self.by).at[self.slot(p)],self.ss.at[self.slot(p),2 if x else 3],self.rs.at[self.slot(p),2 if x else 3],c.X if x else c.Y)
    def cu(self,p,zz,up):
        c=self.pc; k=4+zz if up else 4+c.nz+zz
        return rc(self.g.at[p,zz,c.r],(self.bu if up else self.bd).at[self.slot(p),zz],self.ss.at[self.slot(p),k],self.rs.at[self.slot(p),k],c.up if up else c.dn)
    def add(self,dst,*srcs):
        v=dst[...].astype(F32)
        for s in srcs: v=v+s[...].astype(F32)
        dst[...]=v.astype(BF)
    def s0(self,p):
        self.c0(p,True).start(); self.c0(p,False).start()
    def s1(self,p):
        c=self.pc;h=self.h;n=c.nz
        self.c0(p,True).wait_recv()
        self.add(self.g.at[p,pl.ds(0,h),c.ry],self.d.at[self.slot(p),pl.ds(0,h)])
        self.c1(p,False).start()
        self.c0(p,False).wait_recv()
        self.add(self.g.at[p,pl.ds(h,n-h),c.rx],self.d.at[self.slot(p),pl.ds(h,n-h)])
        self.c1(p,True).start()
    def s2(self,p):
        c=self.pc
        self.c1(p,True).wait_recv(); self.c1(p,False).wait_recv()
        self.add(self.g.at[p,:,c.r],self.bx.at[self.slot(p)],self.by.at[self.slot(p)])
        self.zk(p,0)
    def zk(self,p,k):
        c=self.pc; nz=c.nz
        @pl.when(c.z==k)
        def _():
            for zz in range(nz-1,k,-1):
                if k>0:
                    self.cu(p,zz,True).wait_recv()
                    self.add(self.g.at[p,zz,c.r],self.bu.at[self.slot(p),zz])
                self.cu(p,zz,True).start()
        @pl.when(c.z==nz-1-k)
        def _():
            for zz in range(0,nz-1-k):
                if k>0:
                    self.cu(p,zz,False).wait_recv()
                    self.add(self.g.at[p,zz,c.r],self.bd.at[self.slot(p),zz])
                self.cu(p,zz,False).start()
    def fin(self,p,tot,place=None):
        c=self.pc
        tot[...]=self.g[p,c.z,c.r].astype(F32)
        @pl.when(c.z>0)
        def _():
            self.cu(p,c.z,True).wait_recv()
            tot[...]+=self.bu[self.slot(p),c.z].astype(F32)
        @pl.when(c.z<c.nz-1)
        def _():
            self.cu(p,c.z,False).wait_recv()
            tot[...]+=self.bd[self.slot(p),c.z].astype(F32)
        if place is not None: place(p)
    def drain(self,p):
        c=self.pc; nz=c.nz
        self.c0(p,True).wait_send(); self.c0(p,False).wait_send()
        self.c1(p,True).wait_send(); self.c1(p,False).wait_send()
        for zz in range(nz):
            @pl.when(zz>c.z)
            def _(): self.cu(p,zz,True).wait_send()
            @pl.when(zz<c.z)
            def _(): self.cu(p,zz,False).wait_send()
    def lines(self):
        return [functools.partial(lambda k,p:self.zk(p,k),k) for k in range(1,self.pc.nz-1)]
    def steps(self,place,tot):
        return [self.s0,NOP,self.s1,NOP,self.s2]+self.lines()+[lambda p:self.fin(p,tot,place)]
    def tight(self,out):
        return [self.s0,self.s1,self.s2]+self.lines()+[lambda p:self.fin(p,out.at[0])]


EPS = 1e-5
RT = 512


def pick(static, cond, body):
    if isinstance(cond, (bool, int)):
        if cond:
            body()
    else:
        pl.when(cond)(body)


def norm_rows(values):
    mean = jnp.mean(values, axis=1, keepdims=True)
    centred = values - mean
    inverse = lax.rsqrt(jnp.mean(centred * centred, axis=1, keepdims=True) + EPS)
    return centred * inverse, inverse


def gelu_both(u):
    c = 0.7978845608028654
    u2 = u * u
    t = jnp.tanh(c * u * (1.0 + 0.044715 * u2))
    half = 0.5 + 0.5 * t
    act = u * half
    grad = half + (0.5 * c) * u * (1.0 - t * t) * (1.0 + (3 * 0.044715) * u2)
    return act, grad


def flat(ref, p):
    v = ref[p]
    return v.reshape(-1, v.shape[-1])


def tiles(n):
    return lambda f: pl.loop(0, n)(f)


def rows_of(i, n=RT):
    return pl.ds(pl.multiple_of(i * n, n), n)


def twin_copy(pc, src, dst, ss, rs):
    return rc(src, dst, ss, rs, pc.twin)


def members(cl, hh):
    return jnp.where(cl[hh] == sub((128, L)), 1.0, 0.0).astype(BF)


def pair_members(cl, p):
    return jnp.concatenate([members(cl, 2 * p), members(cl, 2 * p + 1)], 0)


def pair_own():
    return (lane((256, 128)) >= 64) == (sub((256, 128)) >= 128)


def fwd_clusters(p, qkv, cl, n_s, seg, prob_o):
    q = qkv[p, :, 0:128]
    k = qkv[p, :, 128:256]
    v = qkv[p, :, 256:384]
    own = pair_own()
    mt = pair_members(cl, p)
    cnt = jnp.maximum(jnp.sum(mt.astype(F32), axis=1, keepdims=True), 1.0)
    cen = jnp.where(own, dot(mt, q) / cnt, 0.0).astype(BF)
    s = dot((cen.astype(F32) * 0.125).astype(BF), k, NT)
    top = jnp.concatenate([jnp.transpose(n_s[2 * p + h]).astype(F32) for h in range(2)], 0) == 0.0
    c = sub((256, 1))
    cm = lax.rem(jnp.where(c < 128, c, c - 128), jnp.int32(10))
    s = jnp.where(seg[...] == cm, s, -BIG)
    e = jnp.exp(s - jnp.max(s, axis=1, keepdims=True))
    prob = e / jnp.sum(e, axis=1, keepdims=True)
    mass = jnp.sum(jnp.where(top, prob, 0.0), axis=1, keepdims=True)
    signed = jnp.where(top, -prob, prob).astype(BF)
    prob_o[2 * p] = signed[0:128]
    prob_o[2 * p + 1] = signed[128:256]
    rest = dot(jnp.where(top, 0.0, prob).astype(BF), v)
    rh, rl = split2(jnp.where(own, rest, jnp.broadcast_to(mass, (256, 128))))
    rr = jnp.concatenate([rh, rl], 1)
    return rr[0:128], rr[128:256]


def fwd_head(p, h, rr, qkv, mb, n_s, qaug, kaug, att, ex):
    odd = h == 1
    hh = 2 * p + h
    k = qkv[p, :, 128:256]
    ln = lane((L, 128))
    mine = (ln >= 64) if odd else (ln < 64)
    zero = jnp.zeros((), BF)
    vaug = jnp.where(mine, qkv[p, :, 256:384], jnp.ones((), BF))
    qaug[:, :128] = (jnp.where(mine, qkv[p, :, 0:128], zero).astype(F32) * 0.125).astype(BF)
    qaug[:, 128:] = mb[hh]
    kaug[:, :128] = k
    kaug[:, 128:] = n_s[hh]
    lt = lane((TQ, 128))
    minet = (lt >= 64) if odd else (lt < 64)
    cols = pl.ds(pl.multiple_of(p * 128, 128), 128)
    for t in range(L // TQ):
        sl = pl.ds(t * TQ, TQ)
        sc = dot(qaug[sl, :], kaug[...], NT)
        mm = jnp.max(sc, axis=1, keepdims=True)
        pr = jnp.exp(sc - mm).astype(BF)
        o = dot(pr, vaug)
        mt_ = qaug[sl, 128:]
        ee = dot(mt_, rr)
        ee = ee[:, :128] + ee[:, 128:]
        osw = pltpu.roll(o, 64, 1)
        esw = pltpu.roll(ee, 64, 1)
        exact = o / osw
        a = exact * esw + ee
        tot = jnp.where(minet, osw, o)
        ms = jnp.where(minet, esw, ee)
        lse = mm + jnp.log(tot) - jnp.log(jnp.maximum(ms, 1e-37))
        h3, m3, l3 = split3(lse)
        mb[hh, sl, :] = jnp.where(lt == 100, h3.astype(F32), jnp.where(lt == 101, m3.astype(F32), jnp.where(lt == 102, l3.astype(F32), mt_.astype(F32)))).astype(BF)
        if odd:
            att[sl, cols] = jnp.where(lt < 64, att[sl, cols], a.astype(BF))
            ex[sl, cols] = jnp.where(lt < 64, ex[sl, cols], exact.astype(BF))
        else:
            att[sl, cols] = a.astype(BF)
            ex[sl, cols] = exact.astype(BF)


def as_column(row):
    n = row.shape[1]
    eye = sub((n, n)) == lane((n, n))
    return jnp.sum(jnp.where(eye, row.astype(F32), 0.0), axis=1, keepdims=True)


def fill_own(pc, g, gg, q3, oT, upw, dT, ga, gf):
    for p in range(3):
        for i in range(3):
            g[p, pc.z, pc.r, :, i * 128:(i + 1) * 128] = q3[i, :, p * 128:(p + 1) * 128]
    g[3, pc.z, pc.r] = oT[...]
    for q in range(4):
        g[4 + q, pc.z, pc.r] = upw[:, q * 384:(q + 1) * 384]
        g[8 + q, pc.z, pc.r] = dT[:, q * 384:(q + 1) * 384]
    R = oT.shape[0]
    ln = lane((R, 128))
    gg[0, pc.z, pc.r] = jnp.where(ln == 0, as_column(ga[...]), jnp.where(ln == 1, as_column(gf[...]), 0.0)).astype(BF)


def bwd_clusters(p, cl, s, gaugs, dq_o, dk_o, dv_o):
    qkv = s["qkv"]
    cols = pl.ds(pl.multiple_of(p * 128, 128), 128)
    qv = qkv[p, :, 0:128]
    kv = qkv[p, :, 128:256]
    vv = qkv[p, :, 256:384]
    gv = s["gatt"][:, cols]
    ln = lane((L, 128))
    lc = lane((256, 128))
    row = sub((256, 128))
    own = pair_own()
    prod = gv.astype(F32) * s["ex"][:, cols].astype(F32)
    dots = jnp.zeros((L, 128), F32)
    for h in range(2):
        mine = (ln >= 64) if h else (ln < 64)
        o = 0 if h else 64
        three = [a.astype(F32) for a in split3(jnp.sum(jnp.where(mine, prod, 0.0), axis=1, keepdims=True))]
        ga = jnp.where(mine, gv.astype(F32), 0.0)
        for i, a in enumerate(three):
            ga = jnp.where(ln == o + i, a, ga)
            dots = jnp.where(ln == 3 * h + i, a, dots)
        gaugs[h][...] = ga.astype(BF)
    mt = pair_members(cl, p)
    cnt = jnp.maximum(jnp.sum(mt.astype(F32), axis=1, keepdims=True), 1.0)
    cq = dot(mt, jnp.concatenate([qv, gv], 1))
    cen = jnp.where(own, cq[:, 0:128] / cnt, 0.0).astype(BF)
    cs = (cen.astype(F32) * 0.125).astype(BF)
    grest = jnp.where(own, cq[:, 128:256], 0.0).astype(BF)
    gm = dot(mt, dots.astype(BF))
    lo = jnp.where(row >= 128, 3, 0)
    gmass = jnp.sum(jnp.where((lc >= lo) & (lc < lo + 3), gm, 0.0), axis=1, keepdims=True)
    signed = jnp.concatenate([s["prob"][2 * p], s["prob"][2 * p + 1]], 0).astype(F32)
    top = signed < 0.0
    prob = jnp.abs(signed)
    gp = jnp.where(top, gmass, dot(grest, vv, NT))
    gs = (prob * (gp - jnp.sum(prob * gp, axis=1, keepdims=True))).astype(BF)
    rw = jnp.where(top, 0.0, prob).astype(BF)
    gcen = jnp.where(own, dot(gs, kv) / cnt, 0.0)
    gh, gl = split2(gcen)
    dk_o[...] = dot(jnp.transpose(gs), cs)
    dv_o[...] = dot(jnp.transpose(rw), grest)
    zero = jnp.zeros((), BF)
    two = jnp.concatenate([jnp.where(ln < 100, s["mb"][2 * p + h], zero) for h in range(2)], 1)
    dd = dot(two, jnp.concatenate([gh, gl], 1))
    dq_o[...] = dd[:, :128] + dd[:, 128:]


def bwd_head(p, h, s, qaug, kaug, gaug, vaug, dk_o, dv_o, dqt):
    qkv = s["qkv"]
    hh = 2 * p + h
    cols = pl.ds(pl.multiple_of(p * 128, 128), 128)
    kv = qkv[p, :, 128:256]
    ln = lane((L, 128))
    zero = jnp.zeros((), BF)
    mine = (ln >= 64) if h else (ln < 64)
    o = 0 if h else 64
    gm = jnp.where(mine, s["gatt"][:, cols], zero)
    vaug[...] = jnp.where(mine, qkv[p, :, 256:384], jnp.where((ln >= o) & (ln < o + 3), jnp.full((), -1.0, BF), zero))
    qs = (jnp.where(mine, qkv[p, :, 0:128], zero).astype(F32) * 0.125).astype(BF)
    qaug[:, :128] = qs
    qaug[:, 128:] = s["mb"][hh]
    kaug[:, :128] = kv
    kaug[:, 128:] = s["ns"][hh]
    kTh = jnp.transpose(kv)[64 * h:64 * h + 64]
    for t in range(L // TJ):
        sl = pl.ds(t * TJ, TJ)
        pr = jnp.exp(dot(kaug[sl, :], qaug[...], NT))
        ds = (pr * dot(vaug[sl, :], gaug[...], NT)).astype(BF)
        dv_o[sl, :] += dot(pr.astype(BF), gm)
        dk_o[sl, :] += dot(ds, qs)
        dqp = dot(kTh[:, t * TJ:(t + 1) * TJ], ds)
        if t == 0:
            dqt[64 * h:64 * h + 64, :] = dqp
        else:
            dqt[64 * h:64 * h + 64, :] += dqp


def place_sum(p, tot, outs):
    qg, og, ug, dg = outs

    def pair(p):
        for i in range(3):
            qg[i, :, pl.ds(pl.multiple_of(p * 128, 128), 128)] = tot[:, i * 128:(i + 1) * 128]

    def wide(ref, q):
        ref[:, pl.ds(pl.multiple_of(q * 384, 128), 384)] = tot[...]

    pick(None, (8 <= p < 12) if isinstance(p, int) else (p >= 8) & (p < 12), lambda: pair(p - 8))
    pick(None, p == 3, lambda: og.__setitem__(..., tot[...]))
    pick(None, (3 < p < 8) if isinstance(p, int) else (p > 3) & (p < 8), lambda: wide(ug, p - 4))
    pick(None, p >= 12, lambda: wide(dg, p - 12))


def finish_body(*refs):
    ins, gg, outs, (g1, g2), bufs, (si, so) = refs[:6], refs[6], refs[7:13], refs[13:15], refs[15:21], refs[21:]
    cuts = [(i, j * (a.shape[0] // n), a.shape[0] // n) for i, (a, n) in enumerate(zip(ins, (2, 4, 3, 1, 1, 1))) for j in range(n)]
    ci = [pltpu.make_async_copy(ins[i].at[pl.ds(o, n)], bufs[i].at[pl.ds(o, n)], si.at[k]) for k, (i, o, n) in enumerate(cuts)]
    co = [pltpu.make_async_copy(bufs[i].at[pl.ds(o, n)], outs[i].at[pl.ds(o, n)], so.at[k]) for k, (i, o, n) in enumerate(cuts)]
    for c in ci:
        c.start()
    R = gg.shape[1]
    eye = sub((R, R)) == lane((R, R))
    for i, g in enumerate((g1, g2)):
        g[...] = jnp.sum(jnp.where(eye, gg[0, :, i:i + 1], 0.0), axis=0, keepdims=True)
    for a, b in zip(ci, co):
        a.wait()
        b.start()
    for c in co:
        c.wait()


def finish(*arrays):
    V = pl.BlockSpec(memory_space=pltpu.VMEM)
    A = pl.BlockSpec(memory_space=pl.ANY)
    R = arrays[6].shape[1]
    dma = pltpu.SemaphoreType.DMA
    return pl.pallas_call(
        finish_body,
        out_shape=[jax.ShapeDtypeStruct(a.shape, a.dtype) for a in arrays[:6]] + [jax.ShapeDtypeStruct((1, R), F32)] * 2,
        in_specs=[A] * 6 + [V], out_specs=[A] * 6 + [V] * 2,
        scratch_shapes=[pltpu.VMEM(a.shape, a.dtype) for a in arrays[:6]] + [dma((12,)), dma((12,))],
        compiler_params=pltpu.CompilerParams(vmem_limit_bytes=60 << 20),
    )(*arrays)


def scratch_shapes(custom, nz, R):
    f = lambda *s: (s, F32)
    b = lambda *s: (s, BF)
    wide = (16, nz, 4, R, 384) if custom else (16, 768, 384)
    return {
        "gr": f(8, 768), "n1": b(L, 768), "qkv": b(3, L, 384), "att": b(L, 384), "ex": b(L, 384), "mb": b(6, L, 128),
        "ns": b(6, L, 128), "prob": b(6, 128, L), "hid": f(L, 768), "n2": b(L, 768), "act": b(4, L, 384), "dg": b(4, L, 384),
        "aT": b(768, L), "eb": b(L, 768), "er": b(L, 768), "fr": b(L // 2, 768), "gatt": b(L, 384),
        "qaug": b(L, 256), "kaug": b(L, 256), "gaug": b(L, 128), "gaug1": b(L, 128), "vaug": b(L, 128),
        "dqs": f(L, 128), "dks": f(L, 128), "dvs": f(L, 128), "dqt": f(128, L), "gacc": f(8, 768),
        "wg": b(*wide),
    }


def layer_body(nb, custom, names, *refs):
    refs = list(refs)
    take = lambda n: [refs.pop(0) for _ in range(n)]
    x, ct, seg, cl, tt = take(5)
    own = take(6 if custom else 2)
    y, tg, out_g = take(3)
    out_s = take(4) if custom else take(1)[0]
    s = dict(zip(names, take(len(names))))
    tpad, es, ers, vs, vrs = take(5)
    pc = Place(nb)
    wg, hid, n1, n2, qkv, att, ex, act, dg = (s[n] for n in ("wg", "hid", "n1", "n2", "qkv", "att", "ex", "act", "dg"))
    aT, eb, er, fr, gr, gacc = (s[n] for n in ("aT", "eb", "er", "fr", "gr", "gacc"))
    half, nh, nt = L // 2, L // 2 // RT, L // RT

    if custom:
        gg, tot, gbuf, ss, rs, gss, grs, ss2, rs2, gss2, grs2, gown, gtwin = take(13)
        land, gland = take(5), take(5)
        G, Gg = Gather(pc, wg, ss, rs), Gather(pc, gg, gss, grs)
        S = Scatter(pc, wg, *land, ss2, rs2, slot=lambda p: (p - 4 if p >= 12 else p - 8 if p >= 8 else p) if isinstance(p, int) else jnp.where(p >= 12, p - 4, jnp.where(p >= 8, p - 8, p)))
        Sg = Scatter(pc, gbuf, *gland, gss2, grs2)
        Gp = PlaneFirst(pc, wg, ss, rs)
        m = pc.nz - 1

        def last(p):
            G.zk(p, m)
            G.x0(p)

        def turn(p):
            Gp.x2(p)
            Gp.z0(p)
        line = lambda g, off: [(off + d, functools.partial(lambda d, p: g.zk(p, d), d)) for d in range(1, m)][::-1]
        nine = lambda k: k + k // 3
        three = lambda k: k + 3
        rest = list(range(1, 9))
        gather = [(m + 2, G.x2, [0], nine), (m + 1, G.x1, [0], nine), (m + 3, G.x2, rest, nine), (m + 2, G.x1, rest, nine)]
        gather += [(e, fn, list(range(9)), nine) for e, fn in [(m, last)] + line(G, 0) + [(0, G.z0)]]
        gather += [(9, G.drain, list(range(9)), nine), (8, Gp.drain, [0, 4, 8], three)]
        gather += [(e, fn, [0, 4, 8], three) for e, fn in [(m + 3, lambda p: Gp.zk(p, m))] + line(Gp, 3) + [(2, turn), (1, Gp.x1), (0, Gp.x0)]]
        gsteps = [Gg.z0] + [functools.partial(lambda d: Gg.zk(0, d), d) for d in range(1, m)] + [None, Gg.x1, Gg.x2]
        ssteps = S.steps(lambda p: place_sum(p, tot, out_s), tot)
        tails = Sg.tight(gown)
        starts = {13: 12, 14: 13, 15: 14, 16: 15, 17: 4, 18: 5, 19: 6, 20: 7, 21: 3, 22: 8, 23: 9, 25: 10}

        def tick(t, span=None):
            fixed = isinstance(t, int)
            ts = [t] if fixed else list(range(*span))
            for i in range(len(ssteps) - 1, -1, -1):
                hits = [u - i for u in ts if u - i in starts]
                if not hits or ssteps[i] is NOP:
                    continue
                if fixed:
                    ssteps[i](starts[hits[0]])
                    continue
                u = t - i
                ok = functools.reduce(jnp.logical_or, [u == k for k in hits])
                part = functools.reduce(lambda a, k: jnp.where(u == k, starts[k], a), hits, 0)
                pl.when(ok)(lambda i=i, part=part: ssteps[i](part))
            for off, fn, at, to in gather:
                hits = [u - off for u in ts if u - off in at]
                if not hits:
                    continue
                u = t - off
                ok = True if fixed else functools.reduce(jnp.logical_or, [u == k for k in hits])
                pick(None, ok, lambda fn=fn, p=to(u): fn(p))
            if fixed and t < len(gsteps):
                if t == m:
                    Gg.zk(0, m)
                    Gg.x0(0)
                elif t == 0:
                    gsteps[0](0)
                elif t < m:
                    gsteps[t]()
                else:
                    gsteps[t](0)
    else:
        tick = lambda t, span=None: None

    pc.greet()
    tpad[...] = jnp.full_like(tpad, -1)
    if custom:
        fill_own(pc, wg, gg, *own)
    pc.meet()
    tick(0)

    @tiles(nt)
    def _(i):
        hid[rows_of(i), :] = norm_rows(x[rows_of(i), :].astype(F32))[0]

    tick(1)

    def mask(h):
        tpad[:, 0:tt.shape[2]] = tt[h]
        a, n = build_masks(cl[h], tpad[...])
        s["mb"][h], s["ns"][h] = a, n

    def transpose_into(src):
        for i in range(nt):
            aT[:, i * RT:(i + 1) * RT] = jnp.transpose(src[i * RT:(i + 1) * RT, :])

    def put(p, left, right):
        wg[p] = dot(left, right).astype(BF).reshape(wg.shape[1:])

    pl.loop(0, 2)(mask)
    tick(2)
    pl.loop(2, 4)(mask)
    tick(3)
    pl.loop(4, 6)(mask)
    transpose_into(ct)
    tick(4)
    tick(5)
    if custom:
        gains = gg[0].reshape(768, 128)
    else:
        c = pltpu.make_async_copy(own[0], wg.at[0:12], vs)
        c.start()
        c.wait()
        gains = own[1][...]
    gr[...] = jnp.transpose(gains.astype(F32))[0:8]

    @tiles(nt)
    def _(i):
        n1[rows_of(i), :] = (hid[rows_of(i), :] * gr[0:1, :]).astype(BF)

    @pl.loop(0, 3)
    def _(p):
        @tiles(nt)
        def _(i):
            qkv[p, rows_of(i), :] = dot(n1[rows_of(i), :], flat(wg, p)).astype(BF)
        rr = fwd_clusters(p, qkv, cl, s["ns"], seg, s["prob"])
        fwd_head(p, 0, rr[0], qkv, s["mb"], s["ns"], s["qaug"], s["kaug"], att, ex)
        pl.when(p == 0)(lambda: tick(6))
        fwd_head(p, 1, rr[1], qkv, s["mb"], s["ns"], s["qaug"], s["kaug"], att, ex)
        tick(7 + p, (7, 10))

    def send(k, src, dst, i):
        return twin_copy(pc, src.at[rows_of(i)], dst.at[rows_of(i)], es.at[k + i], ers.at[k + i])

    @tiles(nt)
    def _(i):
        eb[rows_of(i), :] = dot(att[rows_of(i), :], flat(wg, 3), NT).astype(BF)
        send(0, eb, er, i).start()

    tick(10)

    @tiles(nt)
    def _(i):
        r = rows_of(i)
        send(0, eb, er, i).wait()
        hv = x[r, :].astype(F32) + (eb[r, :].astype(F32) + er[r, :].astype(F32))
        hid[r, :] = hv
        n2[r, :] = (norm_rows(hv)[0] * gr[1:2, :]).astype(BF)

    def up(q):
        @tiles(nt)
        def _(i):
            a, d = gelu_both(dot(n2[rows_of(i), :], flat(wg, 4 + q)))
            act[q, rows_of(i), :] = a.astype(BF)
            dg[q, rows_of(i), :] = d.astype(BF)

    def down_grad(q):
        up(q)
        put(12 + q, aT[...], act[q])

    tick(11)
    pl.loop(0, 2)(down_grad)
    tick(12)
    def gate(q):
        @tiles(nt)
        def _(i):
            ga = dot(ct[rows_of(i), :], flat(wg, 8 + q))
            dg[q, rows_of(i), :] = (ga * dg[q, rows_of(i), :].astype(F32)).astype(BF)

    pl.loop(2, 4)(down_grad)
    tick(13)
    pl.loop(0, 2)(gate)
    tick(14)
    transpose_into(n2)

    def part(i):
        acc = dot(act[0, rows_of(i), :], flat(wg, 8), NT)
        for q in range(1, 4):
            acc += dot(act[q, rows_of(i), :], flat(wg, 8 + q), NT)
        return acc

    @tiles(nh)
    def _(i):
        eb[rows_of(i), :] = part((1 - pc.h) * nh + i).astype(BF)
        send(4, eb, fr, i).start()

    tick(15)

    pl.loop(2, 4)(gate)

    @tiles(nh)
    def _(i):
        acc = part(pc.h * nh + i).astype(BF).astype(F32)
        send(4, eb, fr, i).wait()
        y[rows_of(i), :] = (hid[rows_of(pc.h * nh + i), :] + (acc + fr[rows_of(i), :].astype(F32))).astype(BF)

    tick(16)
    @tiles(nt)
    def _(i):
        acc = dot(dg[0, rows_of(i), :], flat(wg, 4), NT)
        for q in range(1, 4):
            acc += dot(dg[q, rows_of(i), :], flat(wg, 4 + q), NT)
        eb[rows_of(i), :] = acc.astype(BF)
        send(6, eb, er, i).start()

    def up_grad(q):
        put(4 + q, aT[...], dg[q])

    pl.loop(0, 4)(up_grad)
    tick(17)
    gacc[...] = jnp.zeros_like(gacc)
    gat = n2

    @tiles(nt)
    def _(i):
        r = rows_of(i)
        send(6, eb, er, i).wait()
        gn = eb[r, :].astype(F32) + er[r, :].astype(F32)
        n, inv = norm_rows(hid[r, :])
        a = gn * gr[1:2, :]
        back = (a - jnp.mean(a, axis=1, keepdims=True) - n * jnp.mean(a * n, axis=1, keepdims=True)) * inv
        gh = ct[r, :].astype(F32) + back
        gat[r, :] = gh.astype(BF)

        @pl.when((i >= pc.h * nh) & (i < pc.h * nh + nh))
        def _():
            tg[rows_of(i - pc.h * nh), :] = gh
            gacc[1:2, :] += jnp.sum(gn * n, axis=0, keepdims=True)

    tick(18)

    @tiles(nt)
    def _(i):
        s["gatt"][rows_of(i), :] = dot(gat[rows_of(i), :], flat(wg, 3)).astype(BF)

    transpose_into(gat)
    put(3, aT[...], att[...])
    tick(19)
    transpose_into(n1)
    nacc = hid
    dqkv = att

    @pl.loop(0, 3)
    def _(p):
        bwd_clusters(p, cl, s, (s["gaug"], s["gaug1"]), s["dqs"], s["dks"], s["dvs"])
        bwd_head(p, 0, s, s["qaug"], s["kaug"], s["gaug"], s["vaug"], s["dks"], s["dvs"], s["dqt"])
        tick(20 + 2 * p, (20, 26, 2))
        bwd_head(p, 1, s, s["qaug"], s["kaug"], s["gaug1"], s["vaug"], s["dks"], s["dvs"], s["dqt"])
        dqkv[:, 0:128] = ((s["dqs"][...] + jnp.transpose(s["dqt"][...])) * 0.125).astype(BF)
        dqkv[:, 128:256] = s["dks"][...].astype(BF)
        dqkv[:, 256:384] = s["dvs"][...].astype(BF)

        put(8 + p, aT[...], dqkv[...])
        tick(21 + 2 * p, (21, 27, 2))

        @tiles(nt)
        def _(i):
            v = dot(dqkv[rows_of(i), :], flat(wg, p), NT)

            @pl.when(p == 0)
            def _():
                nacc[rows_of(i), :] = v

            @pl.when(p > 0)
            def _():
                nacc[rows_of(i), :] += v

    @tiles(nh)
    def _(i):
        eb[rows_of(i), :] = nacc[rows_of((1 - pc.h) * nh + i), :].astype(BF)
        send(10, eb, fr, i).start()

    @tiles(nt)
    def _(i):
        n = norm_rows(x[rows_of(i), :].astype(F32))[0]
        gacc[0:1, :] += jnp.sum(nacc[rows_of(i), :] * n, axis=0, keepdims=True)

    if custom:
        wide = jnp.concatenate([gacc[...], jnp.zeros((120, 768), F32)], 0)
        gbuf[0] = jnp.transpose(wide).astype(BF).reshape(gbuf.shape[1:])

    def late(t):
        tick(t)
        if custom and t - 26 < len(tails):
            tails[t - 26](0)

    late(26)
    late(27)

    @tiles(nh)
    def _(i):
        r = rows_of(i)
        send(10, eb, fr, i).wait()
        gn = nacc[rows_of(pc.h * nh + i), :].astype(BF).astype(F32) + fr[r, :].astype(F32)
        n, inv = norm_rows(x[rows_of(pc.h * nh + i), :].astype(F32))
        a = gn * gr[0:1, :]
        back = (a - jnp.mean(a, axis=1, keepdims=True) - n * jnp.mean(a * n, axis=1, keepdims=True)) * inv
        tg[r, :] += back

    if custom:
        @pl.loop(0, 9)
        def _(i):
            S.drain(jnp.where(i < 5, i + 3, i + 7))

        for t in range(28, max(25 + len(ssteps), 26 + len(tails))):
            late(t)
            if t == 25 + len(tails):
                cv = twin_copy(pc, gown, gtwin, vs, vrs)
                cv.start()

        @pl.loop(8, 11)
        def _(p):
            S.drain(p)
        Sg.drain(0)
        Gg.drain(0)
        cv.wait()
        out_g[0] = gown[0] + gtwin[0]
    else:
        c = pltpu.make_async_copy(wg, out_s, vs)
        c.start()
        out_g[...] = gacc[...]
        c.wait()


def layer(nb, custom, *args):
    V = pl.BlockSpec(memory_space=pltpu.VMEM)
    A = pl.BlockSpec(memory_space=pl.ANY)
    nz = nb // 4
    dma = pltpu.SemaphoreType.DMA
    tt, ws = args[4], args[5:]
    R = ws[1].shape[0]
    shapes = scratch_shapes(custom, nz, R)
    out_shape = [jax.ShapeDtypeStruct((L // 2, 768), BF), jax.ShapeDtypeStruct((L // 2, 768), F32)]
    if custom:
        out_shape += [jax.ShapeDtypeStruct(sh, F32) for sh in ((1, R, 128), (3, R, 384), (R, 384), (R, 1536), (R, 1536))]
        out_specs = [V] * 7
        in_specs = [V] * len(args)
    else:
        out_shape += [jax.ShapeDtypeStruct((8, 768), F32), jax.ShapeDtypeStruct(shapes["wg"][0], BF)]
        out_specs = [V, V, V, A]
        in_specs = [V] * 5 + [A, V]
    scratch = [pltpu.VMEM(*sd) for sd in shapes.values()] + [pltpu.VMEM((tt.shape[1], 128), jnp.int32), dma((12,)), dma((12,)), dma, dma]
    if custom:
        ns, n2 = 2 * (nz - 1) + 4, 4 + 2 * nz
        vb = lambda *sh: pltpu.VMEM(sh, BF)
        scratch += [vb(1, nz, 4, R, 128), pltpu.VMEM((R, 384), F32), vb(1, nz, 4, R, 128), dma((12, ns)), dma((12, ns)), dma((1, ns)), dma((1, ns)),
                    dma((12, n2)), dma((12, n2)), dma((1, n2)), dma((1, n2)), pltpu.VMEM((1, R, 128), F32), pltpu.VMEM((1, R, 128), F32)] + [vb(12, nz, R, 384)] * 5 + [vb(1, nz, R, 128)] * 5
    return pl.pallas_call(
        functools.partial(layer_body, nb, custom, tuple(shapes)),
        out_shape=out_shape, in_specs=in_specs, out_specs=out_specs, scratch_shapes=scratch,
        compiler_params=pltpu.CompilerParams(collective_id=0, has_side_effects=True, vmem_limit_bytes=int(63.9 * (1 << 20))),
    )(*args)


def on_device(tokens, attn_gain, qkv_weight, out_weight, ffn_gain, up_weight, down_weight, cotangent, segment, cluster, top_keys):
    nb = lax.axis_size("batch")
    R = qkv_weight.shape[0]
    custom = R % 16 == 0 and nb % 4 == 0
    x, ct = tokens[0], cotangent[0]
    tt = top_keys[0].transpose(0, 2, 1)
    if custom:
        ws = (qkv_weight.transpose(1, 0, 2), out_weight.T, up_weight, down_weight.T, attn_gain[None], ffn_gain[None])
    else:
        w = pack(qkv_weight, out_weight, up_weight, down_weight)
        gw = jnp.pad(jnp.stack([attn_gain, ffn_gain], 1), ((0, 0), (0, 126)))
        ws = (lax.all_gather(w, "batch", axis=1, tiled=True), lax.all_gather(gw, "batch", axis=0, tiled=True))
    y, tg, gg, *S = layer(nb, custom, x, ct, segment, cluster[0][:, None, :], tt, *ws)
    if custom:
        y, tg, qg, og, ug, dg, g1, g2 = finish(y, tg, *S, gg)
        return y[None], tg[None], g1[0], qg.transpose(1, 0, 2), og.T, g2[0], ug, dg.T
    S = lax.psum_scatter(S[0].astype(F32), "batch", scatter_dimension=1, tiled=True)
    g = lax.psum_scatter(lax.psum(gg, "head"), "batch", scatter_dimension=1, tiled=True)
    cat = lambda a: a.transpose(1, 0, 2).reshape(R, -1)
    qg = S[8:11].reshape(3, R, 3, 128).transpose(1, 2, 0, 3).reshape(R, 3, 384)
    return y[None], tg[None], g[0], qg, S[3].T, g[1], cat(S[4:8]), cat(S[12:16]).T


def pack(q, o, u, d):
    R = q.shape[0]
    qp = q.reshape(R, 3, 3, 128).transpose(2, 0, 1, 3).reshape(3, R, 384)
    up = u.reshape(R, 4, 384).transpose(1, 0, 2)
    dn = d.T.reshape(R, 4, 384).transpose(1, 0, 2)
    return jnp.concatenate([qp, o.T[None], up, dn], 0)


def solution(mesh):
    in_specs = (P("batch", None, None), P("batch"), P("batch", None, "head"), P("head", "batch"), P("batch"), P("batch", "head"), P("head", "batch"), P("batch", None, None), P("batch", None), P("batch", "head", None), P("batch", "head", None, None))
    out_specs = (P("batch", "head", None), P("batch", "head", None), P("batch"), P("batch", None, "head"), P("head", "batch"), P("batch"), P("batch", "head"), P("head", "batch"))
    return jax.shard_map(on_device, mesh=mesh, in_specs=in_specs, out_specs=out_specs, check_vma=False)
```
